256 devices in a mesh: dp: 4 (over y), frame: 4 (over x_hi, core), head: 16 (over x_lo, z).
Axes of the slice: x: 4 (x_hi: 2, x_lo: 2; x = x_hi * 2 + x_lo), y: 4, z: 8, core: 2. Of those that a mesh axis runs over, the one named last changes fastest.
Arguments:
- spatial_qkv: bfloat16 [4, 4, 2048, 3456], P('dp', 'frame', 'head'), may hold values from -24 to 24
- spatial_out: bfloat16 [4, 4, 2048, 1152], P('dp', 'frame', 'head'), may hold values from -6 to 6
- resid: bfloat16 [4, 4, 2048, 1152], P('dp', 'frame', 'head'), may hold values from -6 to 6
- norm_gain: float32 [1152], replicated, may hold values from 0.5 to 2
- qkv_weight: bfloat16 [1152, 3456], P(None, 'dp'), may hold values from -0.29462783 to 0.29462783
- out_weight: bfloat16 [1152, 1152], replicated, may hold values from -0.1875 to 0.1875
- grad_out: bfloat16 [4, 4, 2048, 1152], P('dp', 'frame', 'head'), may hold values from -6 to 6
Outputs:
- d_qkv: bfloat16 [4, 4, 2048, 3456], P('dp', 'frame', 'head')
- d_resid: bfloat16 [4, 4, 2048, 1152], P('dp', 'frame', 'head')
- grad_qkv: float32 [1152, 3456], P(('frame', 'head'), 'dp')
- grad_proj: float32 [1152, 1152], P(('frame', 'head'), 'dp')
The draws below stay inside these ranges and needn't reach their ends.
All inputs are finite; a program needn't handle non-finite values.
Results may differ from the reference program's by a relative error of at most 0.013.
Values may be sent and summed in bfloat16 or wider, within the bound.
No kernel may reach another device: no remote copies, remote signals or barrier semaphores. Data moves between devices by JAX's collectives and lax.ppermute only.
A program may use at most 128 MiB of HBM per device.

```python
import math
import jax
import jax.numpy as jnp
from jax import lax

D = 1152
HEADS = 16
HD = 72
FRAME_TOKENS = 2048
FRAMES = 4
CLIPS = 4


def draw_spatial_qkv(key, part):
    key = jax.random.fold_in(key, 11)
    full_shape = (CLIPS, FRAMES, FRAME_TOKENS, 3, D)
    drawn = jax.random.truncated_normal(key, -6.0, 6.0, full_shape, jnp.float32)
    return drawn.reshape(CLIPS, FRAMES, FRAME_TOKENS, 3 * D).astype(jnp.bfloat16)


def draw_qkv_weight(key, part):
    key = jax.random.fold_in(key, 23)
    subkeys = jax.random.split(key, 1)
    drawn = jax.random.truncated_normal(subkeys[0], -6.0, 6.0, (D, 3 * D), jnp.float32)
    return (drawn * D ** (-0.5)).astype(jnp.bfloat16)


def block_levels(stream_key, extent, cuts, least, high):
    def one(dim, parts):
        draws = jax.random.uniform(jax.random.fold_in(jax.random.fold_in(stream_key, 6), dim), (parts,), jnp.float32, least / len(cuts), high / len(cuts))
        return jnp.repeat(jnp.exp(draws), extent[dim] // parts).reshape((-1,) + (1,) * (len(extent) - dim - 1))

    gain = one(*cuts[0])
    for cut in cuts[1:]:
        gain = gain * one(*cut)
    return gain


def normal_values(own_key, extent, deviation, bound, cuts=(), kind=jnp.bfloat16):
    values = deviation * jax.random.normal(own_key, extent, jnp.float32)
    if cuts:
        values = values * block_levels(own_key, extent, cuts, -0.22, 0.18)
    return jnp.clip(values, -bound, bound).astype(kind)


def setup_inputs(seed: int = 0) -> dict:
    streams_of = jax.random.split(jax.random.key(seed), 8)
    spatial_qkv = draw_spatial_qkv(jax.random.fold_in(streams_of[7], 71), 0)
    spatial_out = normal_values(streams_of[1], (CLIPS, FRAMES, FRAME_TOKENS, D), 1.0, 6.0, ((0, 4), (1, 4), (2, 16)))
    resid = normal_values(streams_of[2], (CLIPS, FRAMES, FRAME_TOKENS, D), 1.0, 6.0, ((0, 4), (1, 4), (2, 16)))
    norm_gain = jnp.clip(jnp.exp(jax.random.uniform(streams_of[3], (D,), jnp.float32, math.log(0.5), math.log(2.0))), 0.5, 2.0)
    qkv_weight = draw_qkv_weight(jax.random.fold_in(streams_of[7], 71), 0)
    out_weight = normal_values(streams_of[5], (D, D), D ** -0.5, 0.1875)
    grad_out = normal_values(streams_of[6], (CLIPS, FRAMES, FRAME_TOKENS, D), 1.0, 6.0, ((0, 4), (1, 4), (2, 16)))
    return dict(spatial_qkv=spatial_qkv, spatial_out=spatial_out, resid=resid, norm_gain=norm_gain, qkv_weight=qkv_weight, out_weight=out_weight, grad_out=grad_out)


EPS = 1e-06

def norm_rows(row_block):
    row_mean = lax.optimization_barrier(jnp.mean(row_block, axis=-1, keepdims=True))
    centred = row_block - row_mean
    spread = lax.optimization_barrier(jnp.mean(centred * centred, axis=-1, keepdims=True))
    inverse = lax.rsqrt(spread + EPS)
    return (centred * inverse, inverse)

def norm_backward(upstream, normed, inverse, norm_gain):
    scaled = upstream * norm_gain
    mean_up = lax.optimization_barrier(jnp.mean(scaled, axis=-1, keepdims=True))
    mean_cross = lax.optimization_barrier(jnp.mean(scaled * normed, axis=-1, keepdims=True))
    return inverse * (scaled - mean_up - normed * mean_cross)

def contract_first(left, right):
    return lax.dot_general(left, right, (((0,), (0,)), ((), ())), preferred_element_type=jnp.float32)

def contract_last(left, right):
    return lax.dot_general(left, right, (((1,), (1,)), ((), ())), preferred_element_type=jnp.float32)

def rounded(values):
    return lax.optimization_barrier(values.astype(jnp.bfloat16))

def temporal_grads(query_t, key_t, value_t, grad_t):
    score_scale = HD ** (-0.5)
    f32 = jnp.float32
    scores = jnp.einsum('fnhd,gnhd->nhfg', query_t.astype(f32), key_t.astype(f32)) * score_scale
    probs = jax.nn.softmax(scores, axis=-1)
    probs_low = rounded(probs)
    d_probs = jnp.einsum('fnhd,gnhd->nhfg', grad_t.astype(f32), value_t.astype(f32))
    d_scores = rounded(probs * (d_probs - lax.optimization_barrier(jnp.sum(probs * d_probs, axis=-1, keepdims=True))))
    d_query = (jnp.einsum('nhfg,gnhd->fnhd', d_scores.astype(f32), key_t.astype(f32)) * score_scale).astype(jnp.bfloat16)
    d_key = (jnp.einsum('nhfg,fnhd->gnhd', d_scores.astype(f32), query_t.astype(f32)) * score_scale).astype(jnp.bfloat16)
    d_value = jnp.einsum('nhfg,fnhd->gnhd', probs_low.astype(f32), grad_t.astype(f32)).astype(jnp.bfloat16)
    return (d_query, d_key, d_value)

def spatial_grads(queries, keys_in, values_in, grad_in):
    score_scale = HD ** (-0.5)
    length = queries.shape[0]
    block_rows = min(512, length)
    block_count = length // block_rows
    query_blocks = queries.reshape(block_count, block_rows, queries.shape[1])
    grad_blocks = grad_in.reshape(block_count, block_rows, grad_in.shape[1])

    def block_step(totals, inputs_pair):
        query_block, grad_block = inputs_pair
        scores = jnp.dot(query_block, keys_in.T, preferred_element_type=jnp.float32) * score_scale
        probs = jax.nn.softmax(scores, axis=-1)
        probs_low = probs.astype(jnp.bfloat16)
        d_probs = jnp.dot(grad_block, values_in.T, preferred_element_type=jnp.float32)
        d_scores = (probs * (d_probs - lax.optimization_barrier(jnp.sum(probs * d_probs, axis=-1, keepdims=True)))).astype(jnp.bfloat16)
        d_query = (jnp.dot(d_scores, keys_in, preferred_element_type=jnp.float32) * score_scale).astype(jnp.bfloat16)
        key_total = totals[0] + contract_first(d_scores, query_block)
        value_total = totals[1] + contract_first(probs_low, grad_block)
        return ((key_total, value_total), d_query)
    empty_grad = jnp.zeros(keys_in.shape, jnp.float32)
    (key_total, value_total), d_query = lax.scan(block_step, (empty_grad, empty_grad), (query_blocks, grad_blocks))
    return (d_query.reshape(length, queries.shape[1]), (key_total * score_scale).astype(jnp.bfloat16), value_total.astype(jnp.bfloat16))

def reference(spatial_qkv, spatial_out, resid, norm_gain, qkv_weight, out_weight, grad_out):
    row_block = resid.reshape(-1, D).astype(jnp.float32)
    normed, inverse = norm_rows(row_block)
    unit_rows = (normed * norm_gain).astype(jnp.bfloat16)
    projected = jnp.dot(unit_rows, qkv_weight, preferred_element_type=jnp.float32).astype(jnp.bfloat16)
    clip_proj = projected.reshape(CLIPS, FRAMES, FRAME_TOKENS, 3, HEADS, HD)
    clip_grad = grad_out.reshape(CLIPS, FRAMES, FRAME_TOKENS, HEADS, HD)

    def one_clip(inputs_pair):
        proj_clip, grad_clip = inputs_pair
        return jnp.stack(temporal_grads(proj_clip[:, :, 0], proj_clip[:, :, 1], proj_clip[:, :, 2], grad_clip), axis=2)
    d_proj = lax.map(one_clip, (clip_proj, clip_grad)).reshape(-1, 3 * D)
    grad_qkv = contract_first(unit_rows, d_proj)
    d_stream = norm_backward(contract_last(d_proj, qkv_weight), normed, inverse, norm_gain).astype(jnp.bfloat16)
    grad_proj = contract_first(spatial_out.reshape(-1, D), d_stream)
    d_spatial = contract_last(d_stream, out_weight).astype(jnp.bfloat16)
    frame_qkv = spatial_qkv.reshape(CLIPS * FRAMES, FRAME_TOKENS, 3, HEADS, HD)
    frame_grad = d_spatial.reshape(CLIPS * FRAMES, FRAME_TOKENS, HEADS, HD)
    per_head = jax.vmap(spatial_grads, in_axes=1, out_axes=1)

    def one_frame(inputs_pair):
        qkv_frame, grad_frame = inputs_pair
        return jnp.stack(per_head(qkv_frame[:, 0], qkv_frame[:, 1], qkv_frame[:, 2], grad_frame), axis=1)
    d_qkv = lax.map(one_frame, (frame_qkv, frame_grad)).reshape(CLIPS, FRAMES, FRAME_TOKENS, 3 * D)
    return (d_qkv, d_stream.reshape(CLIPS, FRAMES, FRAME_TOKENS, D), grad_qkv, grad_proj)
```

```python
import functools
import math

import jax
import jax.numpy as jnp
from jax import lax
from jax.experimental import pallas as pl
from jax.experimental.pallas import tpu as pltpu
from jax.sharding import Mesh, PartitionSpec as P

D = 1152
HEADS = 16
HD = 72
ROWS = 128
CLIPS = 4
FRAMES = 4
CHUNK = 32
GROUP = 4
GO_PAD = 384
TOKENS = 2048
BLOCK = 256
EPS = 1e-06
SCALE = HD ** (-0.5)
F32 = jnp.float32
BF16 = jnp.bfloat16
MIB = 1 << 20


def dot(left, right, left_dim, right_dim):
    return lax.dot_general(
        left, right, (((left_dim,), (right_dim,)), ((), ())), preferred_element_type=F32
    )


def call(kernel, out_shape, args, flops, scratch=(), vmem=40, **kw):
    outs = out_shape if isinstance(out_shape, (list, tuple)) else [out_shape]
    moved = sum(math.prod(a.shape) * a.dtype.itemsize for a in [*args, *outs])
    return pl.pallas_call(
        kernel,
        out_shape=out_shape,
        scratch_shapes=list(scratch),
        cost_estimate=pl.CostEstimate(flops=int(flops), bytes_accessed=moved, transcendentals=0),
        compiler_params=pltpu.CompilerParams(vmem_limit_bytes=vmem * MIB),
        **kw,
    )(*args)


def norm_rows(rows):
    centred = rows - jnp.mean(rows, axis=-1, keepdims=True)
    spread = jnp.mean(centred * centred, axis=-1, keepdims=True)
    inverse = lax.rsqrt(spread + EPS)
    return centred * inverse, inverse


def unit_kernel(resid_ref, gain_ref, unit_ref):
    normed, _ = norm_rows(resid_ref[...].astype(F32))
    unit = (normed * gain_ref[...]).astype(BF16)
    for f in range(FRAMES):
        for d in range(CLIPS):
            unit_ref[d, f] = unit[f * CHUNK : (f + 1) * CHUNK]


def grad_kernel(grad_ref, out_ref):
    features = grad_ref[...].astype(F32).T
    gap = jnp.zeros((GO_PAD - GROUP * HD, ROWS), F32)
    for g in range(CLIPS):
        heads = [features[(4 * i + g) * HD : (4 * i + g + 1) * HD] for i in range(GROUP)]
        rows = jnp.concatenate([*heads, gap], axis=0).T.astype(BF16)
        for f in range(FRAMES):
            out_ref[g, f] = rows[f * CHUNK : (f + 1) * CHUNK]


def qkv_kernel(qkv_ref, out_ref, work):
    for t in range(3 * D // 128):
        work[t * 128 : (t + 1) * 128, :] = qkv_ref[:, t * 128 : (t + 1) * 128].astype(F32).T
    for h in range(HEADS):
        parts = [work[(p * HEADS + h) * HD : (p * HEADS + h + 1) * HD, :] for p in range(3)]
        out_ref[h] = jnp.concatenate(parts, axis=0).astype(BF16)


def temporal_kernel(unit_ref, go_ref, w_ref, up_ref, all_ref, dproj_ref, proj, grad, dproj):
    for f in range(FRAMES):
        for c in range(CLIPS):
            at = (f * CLIPS + c) * CHUNK
            all_ref[at : at + CHUNK, :] = unit_ref[c, f]
        rows = jnp.concatenate([go_ref[c, f] for c in range(CLIPS)], axis=0).astype(F32)
        grad[:, f * ROWS : (f + 1) * ROWS] = rows.T[: GROUP * HD]
    proj[...] = dot(w_ref[...], all_ref[...], 1, 1).astype(BF16).astype(F32)

    def one_head(n, carry):
        def load(ref, base):
            at = pl.ds(pl.multiple_of(base + n * HD, 8), HD)
            return [ref[at, f * ROWS : (f + 1) * ROWS] for f in range(FRAMES)]

        q, k, v = (load(proj, p * GROUP * HD) for p in range(3))
        g = load(grad, 0)

        def total(a, b):
            return jnp.sum(a * b, axis=0, keepdims=True)

        span = range(FRAMES)
        ds, p_low = [], []
        for f in span:
            s = [total(q[f], k[j]) * SCALE for j in span]
            top = functools.reduce(jnp.maximum, s)
            e = [jnp.exp(x - top) for x in s]
            below = functools.reduce(jnp.add, e)
            prob = [x / below for x in e]
            dp = [total(g[f], v[j]) for j in span]
            mid = functools.reduce(jnp.add, [x * y for x, y in zip(prob, dp)])
            ds.append([(x * (y - mid)).astype(BF16).astype(F32) for x, y in zip(prob, dp)])
            p_low.append([x.astype(BF16).astype(F32) for x in prob])

        def put(base, f, value):
            at = pl.ds(pl.multiple_of(base + n * HD, 8), HD)
            dproj[at, f * ROWS : (f + 1) * ROWS] = value

        def mix(weights, values):
            return functools.reduce(jnp.add, [w * x for w, x in zip(weights, values)])

        for f in span:
            put(0, f, mix(ds[f], k) * SCALE)
            put(GROUP * HD, f, mix([ds[j][f] for j in span], q) * SCALE)
            put(2 * GROUP * HD, f, mix([p_low[j][f] for j in span], g))
        return carry

    lax.fori_loop(0, GROUP, one_head, 0)
    low = dproj[...].T.astype(BF16)
    dproj_ref[...] = low
    up = dot(low, w_ref[...], 1, 0).astype(BF16)
    for f in range(FRAMES):
        for c in range(CLIPS):
            at = (f * CLIPS + c) * CHUNK
            up_ref[c, f] = up[at : at + CHUNK]


def stream_kernel(up_ref, resid_ref, gain_ref, w_ref, stream_ref, cols_ref, head_ref):
    parts = []
    for f in range(FRAMES):
        parts.append(functools.reduce(jnp.add, [up_ref[g, f].astype(F32) for g in range(CLIPS)]))
    up = jnp.concatenate(parts, axis=0)
    normed, inverse = norm_rows(resid_ref[...].astype(F32))
    scaled = up * gain_ref[...]
    mean_up = jnp.mean(scaled, axis=-1, keepdims=True)
    mean_cross = jnp.mean(scaled * normed, axis=-1, keepdims=True)
    stream = (inverse * (scaled - mean_up - normed * mean_cross)).astype(BF16)
    stream_ref[...] = stream
    spatial = dot(w_ref[...], stream, 1, 1)
    for h in range(HEADS):
        head_ref[h] = spatial[h * HD : (h + 1) * HD].astype(BF16)
    wide = stream.astype(F32)
    for d in range(CLIPS):
        turned = wide if d == 0 else pltpu.roll(wide, D - d * (D // CLIPS), 1)
        cols_ref[d] = turned[:, :GO_PAD].astype(BF16)


def pad_rows(x, rows):
    return jnp.concatenate([x, jnp.zeros((rows - x.shape[0], x.shape[1]), x.dtype)], axis=0)


def probs_kernel(qkv_ref, p_ref, o_ref, k_ref, qt_ref, vt_ref, q_rows, kt, v_rows):
    @pl.when(pl.program_id(0) == 0)
    def _():
        for b in range(HEADS):
            at = slice(b * ROWS, (b + 1) * ROWS)
            block = qkv_ref[b].astype(F32)
            q, k, v = (pad_rows(block[p * HD : (p + 1) * HD], 128) for p in range(3))
            q_rows[at, :] = q.T.astype(BF16)
            k_ref[at, :] = k.T.astype(BF16)
            v_rows[at, :] = v.T.astype(BF16)
            kt[:, at] = k.astype(BF16)
            vt_ref[:, at] = v.astype(BF16)
            qt_ref[:, at] = q[:80].astype(BF16)

    at = pl.multiple_of(pl.program_id(0) * BLOCK, BLOCK)
    scores = dot(q_rows[pl.ds(at, BLOCK), :], kt[...], 1, 0)
    top = jnp.max(scores, axis=-1, keepdims=True)
    factor = SCALE * math.log2(math.e)
    e = jnp.exp2((scores - top) * factor)
    low = (e * (1.0 / jnp.sum(e, axis=-1, keepdims=True))).astype(BF16)
    p_ref[...] = low
    o_ref[...] = dot(low, v_rows[...], 1, 0)


def spatial_kernel(
    do_ref, p_ref, o_ref, k_ref, qt_ref, vt_ref, out_ref, do_rows, dot_cols, dq, dk, dv
):
    step = pl.program_id(0)

    @pl.when(step == 0)
    def _():
        for b in range(HEADS):
            at = slice(b * ROWS, (b + 1) * ROWS)
            block = pad_rows(do_ref[b].astype(F32), 128)
            do_rows[at, :] = block.T.astype(BF16)
            dot_cols[:, at] = block[:80].astype(BF16)
        dk[...] = jnp.zeros_like(dk)
        dv[...] = jnp.zeros_like(dv)

    at = pl.ds(pl.multiple_of(step * BLOCK, BLOCK), BLOCK)
    do = do_rows[at, :]
    probs = p_ref[...]
    dp = dot(do, vt_ref[...], 1, 0)
    mid = jnp.sum(do.astype(F32) * o_ref[...], axis=-1, keepdims=True)
    ds = (probs.astype(F32) * (dp - mid)).astype(BF16)
    dq[:, at] = (dot(ds, k_ref[...], 1, 0) * SCALE).T[:HD]
    dk[...] += dot(qt_ref[...], ds, 1, 0)
    dv[...] += dot(dot_cols[:, at], probs, 1, 0)

    @pl.when(step == pl.num_programs(0) - 1)
    def _():
        for b in range(HEADS):
            at = slice(b * ROWS, (b + 1) * ROWS)
            parts = [dq[:, at], dk[:HD, at] * SCALE, dv[:HD, at]]
            out_ref[b] = jnp.concatenate(parts, axis=0).astype(BF16)


def home_kernel(in_ref, out_ref, work):
    for h in range(HEADS):
        block = in_ref[h].astype(F32)
        for p in range(3):
            at = (p * HEADS + h) * HD
            work[at : at + HD, :] = block[p * HD : (p + 1) * HD]
    for t in range(3 * D // 128):
        at = slice(t * 128, (t + 1) * 128)
        out_ref[:, at] = work[at, :].T.astype(BF16)


def scatter_sum(part):
    columns = part.shape[1]
    halves = part.reshape(2, 2, D // 4, columns)
    core = lax.axis_index("core")
    keep = lax.dynamic_index_in_dim(halves, core, 1, keepdims=False)
    away = lax.dynamic_index_in_dim(halves, 1 - core, 1, keepdims=False)
    came = lax.ppermute(away, "core", [(0, 1), (1, 0)])
    pair = (keep.astype(F32) + came.astype(F32)).astype(BF16).reshape(4, D // 8, columns)
    over_x = lax.all_to_all(pair, ("xh", "xl"), 0, 0, tiled=True)
    rows = jnp.sum(over_x.astype(F32), axis=0).reshape(8, 18, columns)
    rows = jnp.pad(rows, ((0, 0), (0, 14), (0, 0))).astype(BF16)
    over_z = lax.all_to_all(rows, "z", 0, 0, tiled=True)
    return jnp.sum(over_z[:, :18].astype(F32), axis=0)


def per_device(spatial_qkv, spatial_out, resid, norm_gain, qkv_weight, out_weight, grad_out):
    every = ("dp", "xh", "core")
    heads = ("xl", "z")
    shape = jax.ShapeDtypeStruct
    resid = resid.reshape(ROWS, D)
    grad_out = grad_out.reshape(ROWS, D)
    qkv_rows = spatial_qkv.reshape(ROWS, 3 * D)
    out_rows = spatial_out.reshape(ROWS, D)
    gain = norm_gain.reshape(1, D)

    unit_out = call(
        unit_kernel, shape((CLIPS, FRAMES, CHUNK, D), BF16), (resid, gain), ROWS * D * 10
    )
    unit_in = lax.all_to_all(
        unit_out.reshape(16, CHUNK, D), every, 0, 0, tiled=True
    ).reshape(CLIPS, FRAMES, CHUNK, D)
    w_out = qkv_weight.T.reshape(3, CLIPS, HD, D).transpose(1, 0, 2, 3)
    w_in = lax.all_to_all(
        w_out.reshape(CLIPS, 3 * HD, D), "dp", 0, 0, tiled=True
    ).reshape(3 * GROUP * HD, D)
    go_out = call(
        grad_kernel, shape((CLIPS, FRAMES, CHUNK, GO_PAD), BF16), (grad_out,), ROWS * D * 10
    )
    go_in = lax.all_to_all(
        go_out.reshape(16, CHUNK, GO_PAD), every, 0, 0, tiled=True
    ).reshape(CLIPS, FRAMES, CHUNK, GO_PAD)
    qkv_out = call(
        qkv_kernel,
        shape((HEADS, 3 * HD, ROWS), BF16),
        (qkv_rows,),
        ROWS * D * 10,
        scratch=[pltpu.VMEM((3 * D, ROWS), F32)],
    )
    qkv_in = lax.all_to_all(qkv_out, heads, 0, 0, tiled=True)
    every_out = lax.all_gather(out_rows, "dp", axis=0, tiled=True)

    rows = CLIPS * ROWS
    width = 3 * GROUP * HD
    up_out, unit_all, d_proj = call(
        temporal_kernel,
        [
            shape((CLIPS, FRAMES, CHUNK, D), BF16),
            shape((rows, D), BF16),
            shape((rows, width), BF16),
        ],
        (unit_in, go_in, w_in),
        4 * rows * D * width,
        scratch=[
            pltpu.VMEM((width, rows), F32),
            pltpu.VMEM((GROUP * HD, rows), F32),
            pltpu.VMEM((width, rows), F32),
        ],
    )
    up_in = lax.all_to_all(
        up_out.reshape(16, CHUNK, D), every, 0, 0, tiled=True
    ).reshape(CLIPS, FRAMES, CHUNK, D)

    whole = lambda *dims: pl.BlockSpec(dims, lambda i: (0,) * len(dims))
    by_row = lambda wide: pl.BlockSpec((BLOCK, wide), lambda i: (i, 0))
    probs, mixed, keys, queries_t, values_t = call(
        probs_kernel,
        [
            shape((TOKENS, TOKENS), BF16),
            shape((TOKENS, 128), F32),
            shape((TOKENS, 128), BF16),
            shape((80, TOKENS), BF16),
            shape((128, TOKENS), BF16),
        ],
        (qkv_in,),
        4 * TOKENS * TOKENS * 128,
        scratch=[
            pltpu.VMEM((TOKENS, 128), BF16),
            pltpu.VMEM((128, TOKENS), BF16),
            pltpu.VMEM((TOKENS, 128), BF16),
        ],
        grid=(TOKENS // BLOCK,),
        in_specs=[whole(HEADS, 3 * HD, ROWS)],
        out_specs=[
            by_row(TOKENS),
            by_row(128),
            whole(TOKENS, 128),
            whole(80, TOKENS),
            whole(128, TOKENS),
        ],
    )
    grad_term = dot(unit_all, d_proj, 0, 0).astype(BF16)
    grad_rows = scatter_sum(grad_term)
    grad_slots = jnp.pad(
        grad_rows.reshape(18, CLIPS, 3 * HD).transpose(1, 0, 2), ((0, 0), (0, 6), (0, 40))
    )
    grad_slots = lax.all_to_all(grad_slots, "dp", 0, 0, tiled=True)[:, :18, : 3 * HD]
    grad_qkv = (
        grad_slots.reshape(CLIPS, 18, 3, HD).transpose(1, 2, 0, 3).reshape(18, 3 * D // CLIPS)
    )

    stream, cols_out, head_out = call(
        stream_kernel,
        [
            shape((ROWS, D), BF16),
            shape((CLIPS, ROWS, GO_PAD), BF16),
            shape((HEADS, HD, ROWS), BF16),
        ],
        (up_in, resid, gain, out_weight),
        2 * ROWS * D * D,
    )
    head_in = lax.all_to_all(head_out, heads, 0, 0, tiled=True)
    cols_in = lax.all_to_all(cols_out, "dp", 0, 0, tiled=True).reshape(rows, GO_PAD)
    proj_term = dot(every_out, cols_in, 0, 0).astype(BF16)
    grad_proj = scatter_sum(proj_term)[:, : D // CLIPS]

    d_out = call(
        spatial_kernel,
        shape((HEADS, 3 * HD, ROWS), BF16),
        (head_in, probs, mixed, keys, queries_t, values_t),
        8 * TOKENS * TOKENS * 128,
        scratch=[
            pltpu.VMEM((TOKENS, 128), BF16),
            pltpu.VMEM((80, TOKENS), BF16),
            pltpu.VMEM((HD, TOKENS), F32),
            pltpu.VMEM((80, TOKENS), F32),
            pltpu.VMEM((80, TOKENS), F32),
        ],
        grid=(TOKENS // BLOCK,),
        in_specs=[
            whole(HEADS, HD, ROWS),
            by_row(TOKENS),
            by_row(128),
            whole(TOKENS, 128),
            pl.BlockSpec((80, BLOCK), lambda i: (0, i)),
            whole(128, TOKENS),
        ],
        out_specs=whole(HEADS, 3 * HD, ROWS),
    )
    d_in = lax.all_to_all(d_out, heads, 0, 0, tiled=True)
    d_qkv = call(
        home_kernel,
        shape((ROWS, 3 * D), BF16),
        (d_in,),
        ROWS * D * 10,
        scratch=[pltpu.VMEM((3 * D, ROWS), F32)],
    )
    return (
        d_qkv.reshape(1, 1, ROWS, 3 * D),
        stream.reshape(1, 1, ROWS, D),
        grad_qkv,
        grad_proj,
    )


def solution(mesh):
    fine = Mesh(mesh.devices.reshape(4, 2, 2, 2, 8), ("dp", "xh", "core", "xl", "z"))
    frame = ("xh", "core")
    head = ("xl", "z")
    rows = P("dp", frame, head, None)
    return jax.shard_map(
        per_device,
        mesh=fine,
        in_specs=(rows, rows, rows, P(), P(None, "dp"), P(), rows),
        out_specs=(rows, rows, P(frame + head, "dp"), P(frame + head, "dp")),
        check_vma=False,
    )
```

```python
import functools
import math

import jax
import jax.numpy as jnp
from jax import lax
from jax.experimental import pallas as pl
from jax.experimental.pallas import tpu as pltpu
from jax.sharding import Mesh, PartitionSpec as P

D = 1152
HEADS = 16
HD = 72
ROWS = 128
CLIPS = 4
FRAMES = 4
CHUNK = 32
GROUP = 4
GO_PAD = 384
WIDE = 896
TOKENS = 2048
BLOCK = 256
EPS = 1e-06
SCALE = HD ** (-0.5)
F32 = jnp.float32
BF16 = jnp.bfloat16
MIB = 1 << 20


def dot(left, right, left_dim, right_dim):
    return lax.dot_general(
        left, right, (((left_dim,), (right_dim,)), ((), ())), preferred_element_type=F32
    )


def call(kernel, out_shape, args, flops, scratch=(), vmem=40, **kw):
    outs = out_shape if isinstance(out_shape, (list, tuple)) else [out_shape]
    moved = sum(math.prod(a.shape) * a.dtype.itemsize for a in [*args, *outs])
    return pl.pallas_call(
        kernel,
        out_shape=out_shape,
        scratch_shapes=list(scratch),
        cost_estimate=pl.CostEstimate(flops=int(flops), bytes_accessed=moved, transcendentals=0),
        compiler_params=pltpu.CompilerParams(vmem_limit_bytes=vmem * MIB),
        **kw,
    )(*args)


def norm_rows(rows):
    centred = rows - jnp.mean(rows, axis=-1, keepdims=True)
    spread = jnp.mean(centred * centred, axis=-1, keepdims=True)
    inverse = lax.rsqrt(spread + EPS)
    return centred * inverse, inverse


def place(name):
    return lax.axis_index(name)


def frame_index():
    return place("xh") * 2 + place("core")


def x_index():
    return place("xh") * 2 + place("xl")


def unit_kernel(resid_ref, gain_ref, grad_ref, *outs):
    normed, _ = norm_rows(resid_ref[...].astype(F32))
    work = outs[-1]
    work[:, :D] = normed * gain_ref[...]
    work[:, D:] = grad_ref[...].astype(F32)
    f = frame_index()
    for k in range(FRAMES):
        at = pl.multiple_of((f ^ k) * CHUNK, CHUNK)
        outs[k][...] = work[pl.ds(at, CHUNK), :].astype(BF16)


def group_kernel(*refs):
    ins, outs, work = refs[:FRAMES], refs[FRAMES : FRAMES + CLIPS], refs[-1]
    for k in range(FRAMES):
        at = slice(k * CHUNK, (k + 1) * CHUNK)
        for o in range(CLIPS):
            outs[o][at, :D] = ins[k][:, :D]
    grad = jnp.concatenate([ins[k][:, D:] for k in range(FRAMES)], axis=0).astype(F32)
    for t in range(D // 128):
        at = slice(t * 128, (t + 1) * 128)
        work[at, :] = grad[:, at].T
    d = place("dp")
    gap = jnp.zeros((GO_PAD - GROUP * HD, ROWS), F32)
    for o in range(CLIPS):
        g = lax.rem(d + o, CLIPS)
        heads = [
            work[pl.ds(pl.multiple_of((4 * i + g) * HD, 8), HD), :] for i in range(GROUP)
        ]
        outs[o][:, D:] = jnp.concatenate([*heads, gap], axis=0).T.astype(BF16)


def weight_kernel(w_ref, *refs):
    outs, work = refs[:CLIPS], refs[-1]
    work[...] = w_ref[...].astype(F32)
    d = place("dp")
    for o in range(CLIPS):
        g = lax.rem(d + o, CLIPS)
        heads = [work[pl.ds(pl.multiple_of((4 * j + g) * HD, 8), HD), :] for j in range(3)]
        outs[o][...] = jnp.concatenate(heads, axis=0).astype(BF16)


def qkv_kernel(qkv_ref, out_ref, work):
    for t in range(3 * D // 128):
        work[t * 128 : (t + 1) * 128, :] = qkv_ref[:, t * 128 : (t + 1) * 128].astype(F32).T
    for h in range(HEADS):
        parts = [work[(p * HEADS + h) * HD : (p * HEADS + h + 1) * HD, :] for p in range(3)]
        out_ref[h] = jnp.concatenate(parts, axis=0).astype(BF16)


def temporal_kernel(*refs):
    rows_in, w_in = refs[:CLIPS], refs[CLIPS : 2 * CLIPS]
    up_ref, all_ref, dproj_ref, proj, grad, dproj, wide, w_ref = refs[2 * CLIPS :]
    d, frame = place("dp"), frame_index()
    for o in range(CLIPS):
        s = lax.rem(d + CLIPS - o, CLIPS)
        wide[pl.ds(pl.multiple_of(s * 3 * HD, 8), 3 * HD), :] = w_in[o][...].astype(F32)
    w_ref[...] = wide[...].astype(BF16)
    for k in range(FRAMES):
        at = slice(k * CHUNK, (k + 1) * CHUNK)
        for o in range(CLIPS):
            to = (k * CLIPS + o) * CHUNK
            all_ref[to : to + CHUNK, :] = rows_in[o][at, :D]
        rows = jnp.concatenate([rows_in[o][at, D:] for o in range(CLIPS)], axis=0).astype(F32)
        grad[:, k * ROWS : (k + 1) * ROWS] = rows.T[: GROUP * HD]
    proj[...] = dot(w_ref[...], all_ref[...], 1, 1).astype(BF16).astype(F32)

    def one_head(n, carry):
        def load(ref, base):
            at = pl.ds(pl.multiple_of(base + n * HD, 8), HD)
            return [ref[at, f * ROWS : (f + 1) * ROWS] for f in range(FRAMES)]

        q, k, v = (load(proj, p * GROUP * HD) for p in range(3))
        g = load(grad, 0)

        def total(a, b):
            return jnp.sum(a * b, axis=0, keepdims=True)

        span = range(FRAMES)
        ds, p_low = [], []
        for f in span:
            s = [total(q[f], k[j]) * SCALE for j in span]
            top = functools.reduce(jnp.maximum, s)
            e = [jnp.exp(x - top) for x in s]
            below = functools.reduce(jnp.add, e)
            prob = [x / below for x in e]
            dp = [total(g[f], v[j]) for j in span]
            mid = functools.reduce(jnp.add, [x * y for x, y in zip(prob, dp)])
            ds.append([(x * (y - mid)).astype(BF16).astype(F32) for x, y in zip(prob, dp)])
            p_low.append([x.astype(BF16).astype(F32) for x in prob])

        def put(base, f, value):
            at = pl.ds(pl.multiple_of(base + n * HD, 8), HD)
            dproj[at, f * ROWS : (f + 1) * ROWS] = value

        def mix(weights, values):
            return functools.reduce(jnp.add, [w * x for w, x in zip(weights, values)])

        for f in span:
            put(0, f, mix(ds[f], k) * SCALE)
            put(GROUP * HD, f, mix([ds[j][f] for j in span], q) * SCALE)
            put(2 * GROUP * HD, f, mix([p_low[j][f] for j in span], g))
        return carry

    lax.fori_loop(0, GROUP, one_head, 0)
    width = 3 * GROUP * HD
    gap = jnp.zeros((WIDE - width, CLIPS * ROWS), F32)
    low = jnp.concatenate([dproj[...], gap], axis=0).T.astype(BF16)
    dproj_ref[...] = low
    up = dot(low[:, :width], w_ref[...], 1, 0).astype(BF16)
    for k in range(FRAMES):
        for o in range(CLIPS):
            at = (k * CLIPS + o) * CHUNK
            up_ref[lax.rem(d + CLIPS - o, CLIPS), frame ^ k] = up[at : at + CHUNK]


def stream_kernel(up_ref, resid_ref, gain_ref, w_ref, stream_ref, head_ref, *cols):
    parts = []
    for f in range(FRAMES):
        parts.append(functools.reduce(jnp.add, [up_ref[g, f].astype(F32) for g in range(CLIPS)]))
    up = jnp.concatenate(parts, axis=0)
    normed, inverse = norm_rows(resid_ref[...].astype(F32))
    scaled = up * gain_ref[...]
    mean_up = jnp.mean(scaled, axis=-1, keepdims=True)
    mean_cross = jnp.mean(scaled * normed, axis=-1, keepdims=True)
    stream = (inverse * (scaled - mean_up - normed * mean_cross)).astype(BF16)
    stream_ref[...] = stream
    spatial = dot(w_ref[...], stream, 1, 1)
    for h in range(HEADS):
        head_ref[h] = spatial[h * HD : (h + 1) * HD].astype(BF16)
    wide = stream.astype(F32)
    d = place("dp")
    own = lax.broadcasted_iota(jnp.int32, (ROWS, GO_PAD), 1) >= GO_PAD - D // CLIPS
    for o in range(CLIPS):
        g = lax.rem(d + o, CLIPS)
        turned = pltpu.roll(wide, lax.rem(D + 96 - (D // CLIPS) * g, D), 1)
        cols[o][...] = jnp.where(own, turned[:, :GO_PAD], 0.0).astype(BF16)


def weight_grad_kernel(unit_ref, dproj_ref, out_ref, *refs):
    cols, (keep_ref, away_ref, total) = refs[:CLIPS], refs[CLIPS:]
    d, core = place("dp"), place("core")
    first = dot(unit_ref[...].astype(F32).T.astype(BF16), dproj_ref[...], 1, 0)
    clips = [out_ref[lax.rem(d + CLIPS - o, CLIPS)] for o in range(CLIPS)]
    outs = jnp.concatenate(clips, axis=0).astype(F32).T.astype(BF16)
    second = dot(outs, jnp.concatenate([cols[o][...] for o in range(CLIPS)], axis=0), 1, 0)
    total[:, :768] = first[:, :768]
    total[:, 768:WIDE] = first[:, 768:] + second[:, :128]
    total[:, WIDE:] = second[:, 128:]
    for xh in range(2):
        for ref, which in ((keep_ref, core), (away_ref, 1 - core)):
            at = pl.multiple_of((xh * 2 + which) * 288, 8)
            ref[xh] = total[pl.ds(at, 288), :].astype(BF16)


def pair_kernel(keep_ref, came_ref, *outs):
    x = x_index()
    for k in range(4):
        to = x ^ k
        outs[k][...] = (keep_ref[to].astype(F32) + came_ref[to].astype(F32)).astype(BF16)


def line_kernel(*refs):
    ins, outs, work, blocks = refs[:4], refs[4:12], refs[12], refs[13]
    work[:144, :] = functools.reduce(jnp.add, [r[...].astype(F32) for r in ins])
    work[144:, :] = jnp.zeros((8, D), F32)
    for z in range(8):
        blocks[z, :24] = work[z * 18 : z * 18 + 24, :]
    z = place("z")
    gap = jnp.zeros((8, D), F32)
    for o in range(8):
        to = lax.rem(z + o, 8)
        outs[o][...] = jnp.concatenate([blocks[to, :24], gap], axis=0).astype(BF16)


def last_kernel(*refs):
    ins, outs, proj_ref = refs[:8], refs[8 : 8 + CLIPS], refs[-1]
    total = functools.reduce(jnp.add, [r[...].astype(F32) for r in ins])[:24]
    proj_ref[...] = pltpu.roll(total, D // CLIPS, 1)[:18, : D // CLIPS]
    d = place("dp")
    for o in range(CLIPS):
        g = lax.rem(d + o, CLIPS)
        outs[o][...] = pltpu.roll(total, lax.rem(D - 3 * HD * g, D), 1)[:, :256]


def pad_rows(x, rows):
    return jnp.concatenate([x, jnp.zeros((rows - x.shape[0], x.shape[1]), x.dtype)], axis=0)


def probs_kernel(qkv_ref, p_ref, o_ref, k_ref, qt_ref, vt_ref, q_rows, kt, v_rows):
    @pl.when(pl.program_id(0) == 0)
    def _():
        for b in range(HEADS):
            at = slice(b * ROWS, (b + 1) * ROWS)
            block = qkv_ref[b].astype(F32)
            q, k, v = (pad_rows(block[p * HD : (p + 1) * HD], 128) for p in range(3))
            q_rows[at, :] = q.T.astype(BF16)
            k_ref[at, :] = k.T.astype(BF16)
            v_rows[at, :] = v.T.astype(BF16)
            kt[:, at] = k.astype(BF16)
            vt_ref[:, at] = v.astype(BF16)
            qt_ref[:, at] = q[:80].astype(BF16)

    at = pl.multiple_of(pl.program_id(0) * BLOCK, BLOCK)
    scores = dot(q_rows[pl.ds(at, BLOCK), :], kt[...], 1, 0)
    top = jnp.max(scores, axis=-1, keepdims=True)
    factor = SCALE * math.log2(math.e)
    e = jnp.exp2((scores - top) * factor)
    low = (e * (1.0 / jnp.sum(e, axis=-1, keepdims=True))).astype(BF16)
    p_ref[...] = low
    o_ref[...] = dot(low, v_rows[...], 1, 0)


def spatial_kernel(
    do_ref, p_ref, o_ref, k_ref, qt_ref, vt_ref, out_ref, do_rows, dot_cols, dq, dk, dv
):
    step = pl.program_id(0)

    @pl.when(step == 0)
    def _():
        for b in range(HEADS):
            at = slice(b * ROWS, (b + 1) * ROWS)
            block = pad_rows(do_ref[b].astype(F32), 128)
            do_rows[at, :] = block.T.astype(BF16)
            dot_cols[:, at] = block[:80].astype(BF16)
        dk[...] = jnp.zeros_like(dk)
        dv[...] = jnp.zeros_like(dv)

    at = pl.ds(pl.multiple_of(step * BLOCK, BLOCK), BLOCK)
    do = do_rows[at, :]
    probs = p_ref[...]
    dp = dot(do, vt_ref[...], 1, 0)
    mid = jnp.sum(do.astype(F32) * o_ref[...], axis=-1, keepdims=True)
    ds = (probs.astype(F32) * (dp - mid)).astype(BF16)
    dq[:, at] = (dot(ds, k_ref[...], 1, 0) * SCALE).T[:HD]
    dk[...] += dot(qt_ref[...], ds, 1, 0)
    dv[...] += dot(dot_cols[:, at], probs, 1, 0)

    @pl.when(step == pl.num_programs(0) - 1)
    def _():
        for b in range(HEADS):
            at = slice(b * ROWS, (b + 1) * ROWS)
            parts = [dq[:, at], dk[:HD, at] * SCALE, dv[:HD, at]]
            out_ref[b] = jnp.concatenate(parts, axis=0).astype(BF16)


def home_kernel(in_ref, out_ref, work):
    for h in range(HEADS):
        block = in_ref[h].astype(F32)
        for p in range(3):
            at = (p * HEADS + h) * HD
            work[at : at + HD, :] = block[p * HD : (p + 1) * HD]
    for t in range(3 * D // 128):
        at = slice(t * 128, (t + 1) * 128)
        out_ref[:, at] = work[at, :].T.astype(BF16)


def around(x, axis, size, step):
    return lax.ppermute(x, axis, [(i, (i + step) % size) for i in range(size)])


def across(x, axis, size, flip):
    return lax.ppermute(x, axis, [(i, i ^ flip) for i in range(size)])


def per_device(spatial_qkv, spatial_out, resid, norm_gain, qkv_weight, out_weight, grad_out):
    every = ("dp", "xh", "core")
    heads = ("xl", "z")
    frame = ("xh", "core")
    line = ("xh", "xl")
    shape = jax.ShapeDtypeStruct
    resid = resid.reshape(ROWS, D)
    grad_out = grad_out.reshape(ROWS, D)
    qkv_rows = spatial_qkv.reshape(ROWS, 3 * D)
    out_rows = spatial_out.reshape(ROWS, D)
    gain = norm_gain.reshape(1, D)
    rows = CLIPS * ROWS
    width = 3 * GROUP * HD

    w_blocks = call(
        weight_kernel,
        [shape((3 * HD, D), BF16)] * CLIPS,
        (qkv_weight.T,),
        ROWS * D * 10,
        scratch=[pltpu.VMEM((width, D), F32)],
    )
    w_blocks = [b if o == 0 else around(b, "dp", CLIPS, o) for o, b in enumerate(w_blocks)]
    mine = call(
        unit_kernel,
        [shape((CHUNK, 2 * D), BF16)] * FRAMES,
        (resid, gain, grad_out),
        ROWS * D * 10,
        scratch=[pltpu.VMEM((ROWS, 2 * D), F32)],
    )
    mine = [b if k == 0 else across(b, frame, FRAMES, k) for k, b in enumerate(mine)]
    groups = call(
        group_kernel,
        [shape((ROWS, D + GO_PAD), BF16)] * CLIPS,
        tuple(mine),
        ROWS * D * 10,
        scratch=[pltpu.VMEM((D, ROWS), F32)],
    )
    groups = [b if o == 0 else around(b, "dp", CLIPS, o) for o, b in enumerate(groups)]
    qkv_out = call(
        qkv_kernel,
        shape((HEADS, 3 * HD, ROWS), BF16),
        (qkv_rows,),
        ROWS * D * 10,
        scratch=[pltpu.VMEM((3 * D, ROWS), F32)],
    )
    qkv_in = lax.all_to_all(qkv_out, heads, 0, 0, tiled=True)
    every_out = lax.all_gather(out_rows, "dp", axis=0)

    up_out, unit_all, d_proj = call(
        temporal_kernel,
        [
            shape((CLIPS, FRAMES, CHUNK, D), BF16),
            shape((rows, D), BF16),
            shape((rows, WIDE), BF16),
        ],
        (*groups, *w_blocks),
        4 * rows * D * width,
        scratch=[
            pltpu.VMEM((width, rows), F32),
            pltpu.VMEM((GROUP * HD, rows), F32),
            pltpu.VMEM((width, rows), F32),
            pltpu.VMEM((width, D), F32),
            pltpu.VMEM((width, D), BF16),
        ],
    )
    up_in = lax.all_to_all(
        up_out.reshape(16, CHUNK, D), every, 0, 0, tiled=True
    ).reshape(CLIPS, FRAMES, CHUNK, D)

    whole = lambda *dims: pl.BlockSpec(dims, lambda i: (0,) * len(dims))
    by_row = lambda wide: pl.BlockSpec((BLOCK, wide), lambda i: (i, 0))
    probs, mixed, keys, queries_t, values_t = call(
        probs_kernel,
        [
            shape((TOKENS, TOKENS), BF16),
            shape((TOKENS, 128), F32),
            shape((TOKENS, 128), BF16),
            shape((80, TOKENS), BF16),
            shape((128, TOKENS), BF16),
        ],
        (qkv_in,),
        4 * TOKENS * TOKENS * 128,
        scratch=[
            pltpu.VMEM((TOKENS, 128), BF16),
            pltpu.VMEM((128, TOKENS), BF16),
            pltpu.VMEM((TOKENS, 128), BF16),
        ],
        grid=(TOKENS // BLOCK,),
        in_specs=[whole(HEADS, 3 * HD, ROWS)],
        out_specs=[
            by_row(TOKENS),
            by_row(128),
            whole(TOKENS, 128),
            whole(80, TOKENS),
            whole(128, TOKENS),
        ],
    )
    stream, head_out, *cols = call(
        stream_kernel,
        [shape((ROWS, D), BF16), shape((HEADS, HD, ROWS), BF16)]
        + [shape((ROWS, GO_PAD), BF16)] * CLIPS,
        (up_in, resid, gain, out_weight),
        2 * ROWS * D * D,
    )
    head_in = lax.all_to_all(head_out, heads, 0, 0, tiled=True)

    cols = [b if o == 0 else around(b, "dp", CLIPS, o) for o, b in enumerate(cols)]
    keep, away = call(
        weight_grad_kernel,
        [shape((2, 288, D), BF16)] * 2,
        (unit_all, d_proj, every_out, *cols),
        2 * rows * D * (WIDE + GO_PAD),
        scratch=[pltpu.VMEM((D, D), F32)],
    )
    came = across(away, "core", 2, 1)
    blocks = call(
        pair_kernel,
        [shape((144, D), BF16)] * 4,
        (keep.reshape(4, 144, D), came.reshape(4, 144, D)),
        ROWS * D * 10,
    )
    blocks = [b if k == 0 else across(b, line, 4, k) for k, b in enumerate(blocks)]
    blocks = call(
        line_kernel,
        [shape((32, D), BF16)] * 8,
        tuple(blocks),
        ROWS * D * 10,
        scratch=[pltpu.VMEM((152, D), F32), pltpu.VMEM((8, 24, D), F32)],
    )
    blocks = [b if o == 0 else around(b, "z", 8, o) for o, b in enumerate(blocks)]
    *slots, grad_proj = call(
        last_kernel,
        [shape((24, 256), F32)] * CLIPS + [shape((18, D // CLIPS), F32)],
        tuple(blocks),
        ROWS * D,
    )
    slots = [b if o == 0 else around(b, "dp", CLIPS, o) for o, b in enumerate(slots)]
    back = jnp.stack([slots[(CLIPS - o) % CLIPS] for o in range(CLIPS)] * 2)
    start = lax.rem(CLIPS - place("dp"), CLIPS)
    ordered = lax.dynamic_slice_in_dim(back, start, CLIPS, 0)[:, :18, : 3 * HD]
    grad_qkv = (
        ordered.reshape(CLIPS, 18, 3, HD).transpose(1, 2, 0, 3).reshape(18, 3 * D // CLIPS)
    )

    d_out = call(
        spatial_kernel,
        shape((HEADS, 3 * HD, ROWS), BF16),
        (head_in, probs, mixed, keys, queries_t, values_t),
        8 * TOKENS * TOKENS * 128,
        scratch=[
            pltpu.VMEM((TOKENS, 128), BF16),
            pltpu.VMEM((80, TOKENS), BF16),
            pltpu.VMEM((HD, TOKENS), F32),
            pltpu.VMEM((80, TOKENS), F32),
            pltpu.VMEM((80, TOKENS), F32),
        ],
        grid=(TOKENS // BLOCK,),
        in_specs=[
            whole(HEADS, HD, ROWS),
            by_row(TOKENS),
            by_row(128),
            whole(TOKENS, 128),
            pl.BlockSpec((80, BLOCK), lambda i: (0, i)),
            whole(128, TOKENS),
        ],
        out_specs=whole(HEADS, 3 * HD, ROWS),
    )
    d_in = lax.all_to_all(d_out, heads, 0, 0, tiled=True)
    d_qkv = call(
        home_kernel,
        shape((ROWS, 3 * D), BF16),
        (d_in,),
        ROWS * D * 10,
        scratch=[pltpu.VMEM((3 * D, ROWS), F32)],
    )
    return (
        d_qkv.reshape(1, 1, ROWS, 3 * D),
        stream.reshape(1, 1, ROWS, D),
        grad_qkv,
        grad_proj,
    )


def solution(mesh):
    fine = Mesh(mesh.devices.reshape(4, 2, 2, 2, 8), ("dp", "xh", "core", "xl", "z"))
    frame = ("xh", "core")
    head = ("xl", "z")
    rows = P("dp", frame, head, None)
    return jax.shard_map(
        per_device,
        mesh=fine,
        in_specs=(rows, rows, rows, P(), P(None, "dp"), P(), rows),
        out_specs=(rows, rows, P(frame + head, "dp"), P(frame + head, "dp")),
        check_vma=False,
    )
```

```python
import functools
import math

import jax
import jax.numpy as jnp
from jax import lax
from jax.experimental import pallas as pl
from jax.experimental.pallas import tpu as pltpu
from jax.sharding import Mesh, PartitionSpec as P

D = 1152
HEADS = 16
HD = 72
ROWS = 128
CLIPS = 4
FRAMES = 4
CHUNK = 32
GROUP = 4
GO_PAD = 384
WIDE = 896
HALF = 640
CHUNK_OUT = 272
TOKENS = 2048
BLOCK = 256
EPS = 1e-06
SCALE = HD ** (-0.5)
F32 = jnp.float32
BF16 = jnp.bfloat16
MIB = 1 << 20


def dot(left, right, left_dim, right_dim):
    return lax.dot_general(
        left, right, (((left_dim,), (right_dim,)), ((), ())), preferred_element_type=F32
    )


def call(kernel, out_shape, args, us, scratch=(), vmem=40, after=(), in_specs=None, **kw):
    held, extra = len(args), len(after)
    specs = in_specs or [pl.BlockSpec(memory_space=pltpu.VMEM)] * held

    def body(*refs):
        kernel(*refs[:held], *refs[held + extra :])

    return pl.pallas_call(
        body,
        out_shape=out_shape,
        in_specs=[*specs, *[pl.BlockSpec(memory_space=pltpu.HBM)] * extra],
        scratch_shapes=list(scratch),
        cost_estimate=pl.CostEstimate(
            flops=int(us * 1.1e9), bytes_accessed=int(us * 1e6), transcendentals=0
        ),
        compiler_params=pltpu.CompilerParams(vmem_limit_bytes=vmem * MIB),
        **kw,
    )(*args, *after)


def norm_rows(rows):
    centred = rows - jnp.mean(rows, axis=-1, keepdims=True)
    spread = jnp.mean(centred * centred, axis=-1, keepdims=True)
    inverse = lax.rsqrt(spread + EPS)
    return centred * inverse, inverse


def place(name):
    return lax.axis_index(name)


def frame_index():
    return place("xh") * 2 + place("core")


def x_index():
    return place("xh") * 2 + place("xl")


def unit_kernel(resid_ref, gain_ref, grad_ref, *outs):
    normed, _ = norm_rows(resid_ref[...].astype(F32))
    work = outs[-1]
    work[:, :D] = normed * gain_ref[...]
    work[:, D:] = grad_ref[...].astype(F32)
    f = frame_index()
    for k in range(FRAMES):
        at = pl.multiple_of((f ^ k) * CHUNK, CHUNK)
        outs[k][...] = work[pl.ds(at, CHUNK), :].astype(BF16)


def group_kernel(*refs):
    ins, outs, work = refs[:FRAMES], refs[FRAMES : FRAMES + CLIPS], refs[-1]
    for k in range(FRAMES):
        at = slice(k * CHUNK, (k + 1) * CHUNK)
        for o in range(CLIPS):
            outs[o][at, :D] = ins[k][:, :D]
    grad = jnp.concatenate([ins[k][:, D:] for k in range(FRAMES)], axis=0).astype(F32)
    for t in range(D // 128):
        at = slice(t * 128, (t + 1) * 128)
        work[at, :] = grad[:, at].T
    d = place("dp")
    gap = jnp.zeros((GO_PAD - GROUP * HD, ROWS), F32)
    for o in range(CLIPS):
        g = lax.rem(d + o, CLIPS)
        heads = [
            work[pl.ds(pl.multiple_of((4 * i + g) * HD, 8), HD), :] for i in range(GROUP)
        ]
        outs[o][:, D:] = jnp.concatenate([*heads, gap], axis=0).T.astype(BF16)


def weight_kernel(w_ref, *refs):
    outs, work = refs[:CLIPS], refs[-1]
    work[...] = w_ref[...].astype(F32)
    d = place("dp")
    lanes = pl.ds(pl.multiple_of(place("core") * (D - HALF), 128), HALF)
    for o in range(CLIPS):
        g = lax.rem(d + o, CLIPS)
        heads = [work[pl.ds(pl.multiple_of((4 * j + g) * HD, 8), HD), lanes] for j in range(3)]
        outs[o][...] = jnp.concatenate(heads, axis=0).astype(BF16)


def join_kernel(*refs):
    ins, out_ref, work = refs[:CLIPS], refs[CLIPS], refs[-1]
    d = place("dp")
    for o in range(CLIPS):
        s = lax.rem(d + CLIPS - o, CLIPS)
        work[pl.ds(pl.multiple_of(s * 3 * HD, 8), 3 * HD), :] = ins[o][...].astype(F32)
    out_ref[...] = work[...].astype(BF16)


def qkv_kernel(qkv_ref, out_ref, work):
    for t in range(3 * D // 128):
        work[t * 128 : (t + 1) * 128, :] = qkv_ref[:, t * 128 : (t + 1) * 128].astype(F32).T
    for h in range(HEADS):
        parts = [work[(p * HEADS + h) * HD : (p * HEADS + h + 1) * HD, :] for p in range(3)]
        out_ref[h] = jnp.concatenate(parts, axis=0).astype(BF16)


def temporal_kernel(*refs):
    rows_in, halves = refs[:CLIPS], refs[CLIPS : CLIPS + 2]
    up_ref, all_ref, dproj_ref, proj, grad, dproj, w_ref = refs[CLIPS + 2 :]
    d, frame = place("dp"), frame_index()
    for core in range(2):

        @pl.when(place("core") == core)
        def _():
            w_ref[:, :HALF] = halves[core][...]
            w_ref[:, D - HALF :] = halves[1 - core][...]

    for k in range(FRAMES):
        at = slice(k * CHUNK, (k + 1) * CHUNK)
        for o in range(CLIPS):
            to = (k * CLIPS + o) * CHUNK
            all_ref[to : to + CHUNK, :] = rows_in[o][at, :D]
        rows = jnp.concatenate([rows_in[o][at, D:] for o in range(CLIPS)], axis=0).astype(F32)
        grad[:, k * ROWS : (k + 1) * ROWS] = rows.T[: GROUP * HD]
    proj[...] = dot(w_ref[...], all_ref[...], 1, 1).astype(BF16).astype(F32)

    def one_head(n, carry):
        def load(ref, base):
            at = pl.ds(pl.multiple_of(base + n * HD, 8), HD)
            return [ref[at, f * ROWS : (f + 1) * ROWS] for f in range(FRAMES)]

        q, k, v = (load(proj, p * GROUP * HD) for p in range(3))
        g = load(grad, 0)

        def total(a, b):
            return jnp.sum(a * b, axis=0, keepdims=True)

        span = range(FRAMES)
        ds, p_low = [], []
        for f in span:
            s = [total(q[f], k[j]) * SCALE for j in span]
            top = functools.reduce(jnp.maximum, s)
            e = [jnp.exp(x - top) for x in s]
            below = functools.reduce(jnp.add, e)
            prob = [x / below for x in e]
            dp = [total(g[f], v[j]) for j in span]
            mid = functools.reduce(jnp.add, [x * y for x, y in zip(prob, dp)])
            ds.append([(x * (y - mid)).astype(BF16).astype(F32) for x, y in zip(prob, dp)])
            p_low.append([x.astype(BF16).astype(F32) for x in prob])

        def put(base, f, value):
            at = pl.ds(pl.multiple_of(base + n * HD, 8), HD)
            dproj[at, f * ROWS : (f + 1) * ROWS] = value

        def mix(weights, values):
            return functools.reduce(jnp.add, [w * x for w, x in zip(weights, values)])

        for f in span:
            put(0, f, mix(ds[f], k) * SCALE)
            put(GROUP * HD, f, mix([ds[j][f] for j in span], q) * SCALE)
            put(2 * GROUP * HD, f, mix([p_low[j][f] for j in span], g))
        return carry

    lax.fori_loop(0, GROUP, one_head, 0)
    width = 3 * GROUP * HD
    gap = jnp.zeros((WIDE - width, CLIPS * ROWS), F32)
    low = jnp.concatenate([dproj[...], gap], axis=0).T.astype(BF16)
    dproj_ref[...] = low
    up = dot(low[:, :width], w_ref[...], 1, 0).astype(BF16)
    for k in range(FRAMES):
        for o in range(CLIPS):
            at = (k * CLIPS + o) * CHUNK
            up_ref[lax.rem(d + CLIPS - o, CLIPS), frame ^ k] = up[at : at + CHUNK]


def stream_kernel(up_ref, resid_ref, gain_ref, w_ref, stream_ref, head_ref, *cols):
    parts = []
    for f in range(FRAMES):
        parts.append(functools.reduce(jnp.add, [up_ref[g, f].astype(F32) for g in range(CLIPS)]))
    up = jnp.concatenate(parts, axis=0)
    normed, inverse = norm_rows(resid_ref[...].astype(F32))
    scaled = up * gain_ref[...]
    mean_up = jnp.mean(scaled, axis=-1, keepdims=True)
    mean_cross = jnp.mean(scaled * normed, axis=-1, keepdims=True)
    stream = (inverse * (scaled - mean_up - normed * mean_cross)).astype(BF16)
    stream_ref[...] = stream
    spatial = dot(w_ref[...], stream, 1, 1)
    for h in range(HEADS):
        head_ref[h] = spatial[h * HD : (h + 1) * HD].astype(BF16)
    wide = stream.astype(F32)
    d = place("dp")
    for o in range(CLIPS):
        g = lax.rem(d + o, CLIPS)
        turned = pltpu.roll(wide, lax.rem(D - (D // CLIPS) * g, D), 1)
        cols[o][...] = turned[:, :GO_PAD].astype(BF16)


def split_core(total, keep_ref, away_ref):
    core = place("core")
    for xh in range(2):
        for ref, which in ((keep_ref, core), (away_ref, 1 - core)):
            at = pl.multiple_of((xh * 2 + which) * 288, 8)
            ref[xh] = total[pl.ds(at, 288), :].astype(BF16)


def qkv_grad_kernel(unit_ref, dproj_ref, keep_ref, away_ref, total):
    total[...] = dot(unit_ref[...].astype(F32).T.astype(BF16), dproj_ref[...], 1, 0)
    split_core(total, keep_ref, away_ref)


def qkv_pair_kernel(keep_ref, came_ref, out_ref, total, line):
    for xh in range(2):
        at = slice(xh * 288, (xh + 1) * 288)
        total[at, :] = keep_ref[xh].astype(F32) + came_ref[xh].astype(F32)
    for z in range(8):
        for b in range(4):
            at = b * 144 + z * 18
            line[b * 18 : (b + 1) * 18, :] = total[at : at + 18, :]
        out_ref[z] = line[...].astype(BF16)


def spread_kernel(in_ref, out_ref, work):
    work[...] = in_ref[...].astype(F32)
    gap = jnp.zeros((14, WIDE), F32)
    for b in range(4):
        out_ref[b] = jnp.concatenate([work[b * 18 : (b + 1) * 18, :], gap], axis=0).astype(BF16)


def slot_kernel(in_ref, *outs):
    total = in_ref[:24, :].astype(F32)
    wide = jnp.concatenate([total, jnp.zeros((24, 128), F32)], axis=1)
    d = place("dp")
    for o in range(CLIPS):
        g = lax.rem(d + o, CLIPS)
        turned = pltpu.roll(wide, lax.rem(WIDE + 128 - 3 * HD * g, WIDE + 128), 1)
        outs[o][...] = turned[:, :256]


def proj_grad_kernel(out_ref, *refs):
    cols, (keep_ref, away_ref, total) = refs[:CLIPS], refs[CLIPS:]
    d = place("dp")
    clips = [out_ref[lax.rem(d + CLIPS - o, CLIPS)] for o in range(CLIPS)]
    outs = jnp.concatenate(clips, axis=0).astype(F32).T.astype(BF16)
    total[...] = dot(outs, jnp.concatenate([cols[o][...] for o in range(CLIPS)], axis=0), 1, 0)
    split_core(total, keep_ref, away_ref)


def proj_pair_kernel(keep_ref, came_ref, near_ref, far_ref):
    xh = place("xh")
    for ref, which in ((near_ref, xh), (far_ref, 1 - xh)):
        ref[...] = (keep_ref[which].astype(F32) + came_ref[which].astype(F32)).astype(BF16)


def pad_rows(x, rows):
    return jnp.concatenate([x, jnp.zeros((rows - x.shape[0], x.shape[1]), x.dtype)], axis=0)


def probs_kernel(qkv_ref, p_ref, o_ref, k_ref, qt_ref, vt_ref, q_rows, kt, v_rows):
    @pl.when(pl.program_id(0) == 0)
    def _():
        for b in range(HEADS):
            at = slice(b * ROWS, (b + 1) * ROWS)
            block = qkv_ref[b].astype(F32)
            q, k, v = (pad_rows(block[p * HD : (p + 1) * HD], 128) for p in range(3))
            q_rows[at, :] = q.T.astype(BF16)
            k_ref[at, :] = k.T.astype(BF16)
            v_rows[at, :] = v.T.astype(BF16)
            kt[:, at] = k.astype(BF16)
            vt_ref[:, at] = v.astype(BF16)
            qt_ref[:, at] = q[:80].astype(BF16)

    at = pl.multiple_of(pl.program_id(0) * BLOCK, BLOCK)
    scores = dot(q_rows[pl.ds(at, BLOCK), :], kt[...], 1, 0)
    top = jnp.max(scores, axis=-1, keepdims=True)
    factor = SCALE * math.log2(math.e)
    e = jnp.exp2((scores - top) * factor)
    low = (e * (1.0 / jnp.sum(e, axis=-1, keepdims=True))).astype(BF16)
    p_ref[...] = low
    o_ref[...] = dot(low, v_rows[...], 1, 0)


def spatial_kernel(
    do_ref,
    p_ref,
    o_ref,
    k_ref,
    qt_ref,
    vt_ref,
    near_ref,
    far_ref,
    out_ref,
    do_rows,
    dot_cols,
    dq,
    dk,
    dv,
    proj,
    pack,
):
    step = pl.program_id(0)

    @pl.when(step == 0)
    def _():
        for b in range(HEADS):
            at = slice(b * ROWS, (b + 1) * ROWS)
            block = pad_rows(do_ref[b].astype(F32), 128)
            do_rows[at, :] = block.T.astype(BF16)
            dot_cols[:, at] = block[:80].astype(BF16)
        dk[...] = jnp.zeros_like(dk)
        dv[...] = jnp.zeros_like(dv)
        proj[...] = near_ref[...].astype(F32) + far_ref[...].astype(F32)
        pack[...] = jnp.zeros_like(pack)

    at = pl.ds(pl.multiple_of(step * BLOCK, BLOCK), BLOCK)
    do = do_rows[at, :]
    probs = p_ref[...]
    dp = dot(do, vt_ref[...], 1, 0)
    mid = jnp.sum(do.astype(F32) * o_ref[...], axis=-1, keepdims=True)
    ds = (probs.astype(F32) * (dp - mid)).astype(BF16)
    dq[:, at] = (dot(ds, k_ref[...], 1, 0) * SCALE).T[:HD]
    dk[...] += dot(qt_ref[...], ds, 1, 0)
    dv[...] += dot(dot_cols[:, at], probs, 1, 0)

    @pl.when(step == pl.num_programs(0) - 1)
    def _():
        for b in range(HEADS):
            at = slice(b * ROWS, (b + 1) * ROWS)
            for i in range(3):
                part = proj[b * 18 : (b + 1) * 18, i * 128 : (i + 1) * 128]
                pack[i * 18 : (i + 1) * 18, :] = part
            parts = [dq[:, at], dk[:HD, at] * SCALE, dv[:HD, at], pack[...]]
            out_ref[b] = jnp.concatenate(parts, axis=0).astype(BF16)


def home_kernel(in_ref, out_ref, proj_ref, work, pack):
    for h in range(HEADS):
        block = in_ref[h].astype(F32)
        extra = block[3 * HD :]
        pack[...] = extra if h == 0 else pack[...] + extra
        for p in range(3):
            at = (p * HEADS + h) * HD
            work[at : at + HD, :] = block[p * HD : (p + 1) * HD]
    for t in range(3 * D // 128):
        at = slice(t * 128, (t + 1) * 128)
        out_ref[:, at] = work[at, :].T.astype(BF16)
    for i, wide in enumerate((128, 128, 32)):
        proj_ref[:, i * 128 : i * 128 + wide] = pack[i * 18 : (i + 1) * 18, :wide]


def around(x, axis, size, step):
    return lax.ppermute(x, axis, [(i, (i + step) % size) for i in range(size)])


def across(x, axis, size, flip):
    return lax.ppermute(x, axis, [(i, i ^ flip) for i in range(size)])


def per_device(spatial_qkv, spatial_out, resid, norm_gain, qkv_weight, out_weight, grad_out):
    every = ("dp", "xh", "core")
    heads = ("xl", "z")
    frame = ("xh", "core")
    line = ("xh", "xl")
    shape = jax.ShapeDtypeStruct
    resid = resid.reshape(ROWS, D)
    grad_out = grad_out.reshape(ROWS, D)
    qkv_rows = spatial_qkv.reshape(ROWS, 3 * D)
    out_rows = spatial_out.reshape(ROWS, D)
    gain = norm_gain.reshape(1, D)
    rows = CLIPS * ROWS
    width = 3 * GROUP * HD

    whole = lambda *dims: pl.BlockSpec(dims, lambda i: (0,) * len(dims))
    by_row = lambda wide: pl.BlockSpec((BLOCK, wide), lambda i: (i, 0))

    mine = call(
        unit_kernel,
        [shape((CHUNK, 2 * D), BF16)] * FRAMES,
        (resid, gain, grad_out),
        0.5,
        scratch=[pltpu.VMEM((ROWS, 2 * D), F32)],
    )
    ours = [b if k == 0 else across(b, frame, FRAMES, k) for k, b in enumerate(mine)]
    w_blocks = call(
        weight_kernel,
        [shape((3 * HD, HALF), BF16)] * CLIPS,
        (qkv_weight.T,),
        0.5,
        scratch=[pltpu.VMEM((width, D), F32)],
        after=[mine[0]],
    )
    w_in = [b if o == 0 else around(b, "dp", CLIPS, o) for o, b in enumerate(w_blocks)]
    qkv_out = call(
        qkv_kernel,
        shape((HEADS, 3 * HD, ROWS), BF16),
        (qkv_rows,),
        1.2,
        scratch=[pltpu.VMEM((3 * D, ROWS), F32)],
        after=[w_blocks[0]],
    )
    qkv_in = lax.all_to_all(qkv_out, heads, 0, 0, tiled=True)
    groups = call(
        group_kernel,
        [shape((ROWS, D + GO_PAD), BF16)] * CLIPS,
        tuple(ours),
        0.5,
        scratch=[pltpu.VMEM((D, ROWS), F32)],
        after=[qkv_out],
    )
    rows_in = [b if o == 0 else around(b, "dp", CLIPS, o) for o, b in enumerate(groups)]
    w_half = call(
        join_kernel,
        shape((width, HALF), BF16),
        tuple(w_in),
        0.5,
        scratch=[pltpu.VMEM((width, HALF), F32)],
        after=[groups[0]],
    )
    w_other = across(w_half, "core", 2, 1)
    out_rows = lax.optimization_barrier((out_rows, rows_in[1]))[0]
    every_out = lax.all_gather(out_rows, "dp", axis=0)

    up_out, unit_all, d_proj = call(
        temporal_kernel,
        [
            shape((CLIPS, FRAMES, CHUNK, D), BF16),
            shape((rows, D), BF16),
            shape((rows, WIDE), BF16),
        ],
        (*rows_in, w_half, w_other),
        0.1,
        scratch=[
            pltpu.VMEM((width, rows), F32),
            pltpu.VMEM((GROUP * HD, rows), F32),
            pltpu.VMEM((width, rows), F32),
            pltpu.VMEM((width, D), BF16),
        ],
    )
    up_out, qkv_in = lax.optimization_barrier((up_out, qkv_in))
    up_in = lax.all_to_all(
        up_out.reshape(16, CHUNK, D), every, 0, 0, tiled=True
    ).reshape(CLIPS, FRAMES, CHUNK, D)
    keep, away = call(
        qkv_grad_kernel,
        [shape((2, 288, WIDE), BF16)] * 2,
        (unit_all, d_proj),
        2.5,
        scratch=[pltpu.VMEM((D, WIDE), F32)],
    )
    came = across(away, "core", 2, 1)
    term = call(
        qkv_pair_kernel,
        shape((8, 72, WIDE), BF16),
        (keep, came),
        1,
        scratch=[pltpu.VMEM((D // 2, WIDE), F32), pltpu.VMEM((72, WIDE), F32)],
    )
    over_z = lax.psum_scatter(term, "z", scatter_dimension=0)
    probs, mixed, keys, queries_t, values_t = call(
        probs_kernel,
        [
            shape((TOKENS, TOKENS), BF16),
            shape((TOKENS, 128), F32),
            shape((TOKENS, 128), BF16),
            shape((80, TOKENS), BF16),
            shape((128, TOKENS), BF16),
        ],
        (qkv_in,),
        10.5,
        vmem=58,
        scratch=[
            pltpu.VMEM((TOKENS, 128), BF16),
            pltpu.VMEM((128, TOKENS), BF16),
            pltpu.VMEM((TOKENS, 128), BF16),
        ],
        after=[keep],
        grid=(TOKENS // BLOCK,),
        in_specs=[whole(HEADS, 3 * HD, ROWS)],
        out_specs=[
            by_row(TOKENS),
            by_row(128),
            whole(TOKENS, 128),
            whole(80, TOKENS),
            whole(128, TOKENS),
        ],
    )

    stream, head_out, *cols = call(
        stream_kernel,
        [shape((ROWS, D), BF16), shape((HEADS, HD, ROWS), BF16)]
        + [shape((ROWS, GO_PAD), BF16)] * CLIPS,
        (up_in, resid, gain, out_weight),
        2.2,
        after=[queries_t],
    )
    head_in = lax.all_to_all(head_out, heads, 0, 0, tiled=True)

    cols = [b if o == 0 else around(b, "dp", CLIPS, o) for o, b in enumerate(cols)]
    keep, away = call(
        proj_grad_kernel,
        [shape((2, 288, GO_PAD), BF16)] * 2,
        (every_out, *cols),
        2,
        scratch=[pltpu.VMEM((D, GO_PAD), F32)],
    )
    came = across(away, "core", 2, 1)
    near, far = call(
        proj_pair_kernel, [shape((288, GO_PAD), BF16)] * 2, (keep, came), 0.5
    )
    far = across(far, "xh", 2, 1)

    d_out = call(
        spatial_kernel,
        shape((HEADS, CHUNK_OUT, ROWS), BF16),
        (head_in, probs, mixed, keys, queries_t, values_t, near, far),
        10.5,
        vmem=58,
        scratch=[
            pltpu.VMEM((TOKENS, 128), BF16),
            pltpu.VMEM((80, TOKENS), BF16),
            pltpu.VMEM((HD, TOKENS), F32),
            pltpu.VMEM((80, TOKENS), F32),
            pltpu.VMEM((80, TOKENS), F32),
            pltpu.VMEM((288, GO_PAD), F32),
            pltpu.VMEM((56, 128), F32),
        ],
        grid=(TOKENS // BLOCK,),
        in_specs=[
            whole(HEADS, HD, ROWS),
            by_row(TOKENS),
            by_row(128),
            whole(TOKENS, 128),
            pl.BlockSpec((80, BLOCK), lambda i: (0, i)),
            whole(128, TOKENS),
            whole(288, GO_PAD),
            whole(288, GO_PAD),
        ],
        out_specs=whole(HEADS, CHUNK_OUT, ROWS),
    )
    d_in = lax.all_to_all(d_out, heads, 0, 0, tiled=True)
    spread = call(
        spread_kernel,
        shape((4, 32, WIDE), BF16),
        (over_z,),
        0.5,
        scratch=[pltpu.VMEM((72, WIDE), F32)],
    )
    own = lax.psum_scatter(spread, line, scatter_dimension=0)
    slots = call(slot_kernel, [shape((24, 256), F32)] * CLIPS, (own,), 0.5)
    slots = [b if o == 0 else around(b, "dp", CLIPS, o) for o, b in enumerate(slots)]
    back = jnp.stack([slots[(CLIPS - o) % CLIPS] for o in range(CLIPS)] * 2)
    start = lax.rem(CLIPS - place("dp"), CLIPS)
    ordered = lax.dynamic_slice_in_dim(back, start, CLIPS, 0)[:, :18, : 3 * HD]
    grad_qkv = (
        ordered.reshape(CLIPS, 18, 3, HD).transpose(1, 2, 0, 3).reshape(18, 3 * D // CLIPS)
    )

    d_qkv, grad_proj = call(
        home_kernel,
        [shape((ROWS, 3 * D), BF16), shape((18, D // CLIPS), F32)],
        (d_in,),
        1.2,
        scratch=[pltpu.VMEM((3 * D, ROWS), F32), pltpu.VMEM((56, 128), F32)],
    )
    return (
        d_qkv.reshape(1, 1, ROWS, 3 * D),
        stream.reshape(1, 1, ROWS, D),
        grad_qkv,
        grad_proj,
    )


def solution(mesh):
    fine = Mesh(mesh.devices.reshape(4, 2, 2, 2, 8), ("dp", "xh", "core", "xl", "z"))
    frame = ("xh", "core")
    head = ("xl", "z")
    rows = P("dp", frame, head, None)
    return jax.shard_map(
        per_device,
        mesh=fine,
        in_specs=(rows, rows, rows, P(), P(None, "dp"), P(), rows),
        out_specs=(rows, rows, P(frame + head, "dp"), P(frame + head, "dp")),
        check_vma=False,
    )
```

```python
import functools
import math

import jax
import jax.numpy as jnp
from jax import lax
from jax.experimental import pallas as pl
from jax.experimental.pallas import tpu as pltpu
from jax.sharding import Mesh, PartitionSpec as P

D = 1152
HEADS = 16
HD = 72
ROWS = 128
CLIPS = 4
FRAMES = 4
CHUNK = 32
GROUP = 4
GO_PAD = 384
WIDE = 896
HALF = 640
MERGED = 4 * 256 + GO_PAD
TOKENS = 2048
BLOCK = 256
EPS = 1e-06
SCALE = HD ** (-0.5)
F32 = jnp.float32
BF16 = jnp.bfloat16
MIB = 1 << 20


def dot(left, right, left_dim, right_dim):
    return lax.dot_general(
        left, right, (((left_dim,), (right_dim,)), ((), ())), preferred_element_type=F32
    )


def call(kernel, out_shape, args, us, scratch=(), vmem=40, after=(), in_specs=None, **kw):
    held, extra = len(args), len(after)
    specs = in_specs or [pl.BlockSpec(memory_space=pltpu.VMEM)] * held

    def body(*refs):
        kernel(*refs[:held], *refs[held + extra :])

    return pl.pallas_call(
        body,
        out_shape=out_shape,
        in_specs=[*specs, *[pl.BlockSpec(memory_space=pltpu.HBM)] * extra],
        scratch_shapes=list(scratch),
        cost_estimate=pl.CostEstimate(
            flops=int(us * 1.1e9), bytes_accessed=int(us * 1e6), transcendentals=0
        ),
        compiler_params=pltpu.CompilerParams(vmem_limit_bytes=vmem * MIB),
        **kw,
    )(*args, *after)


def norm_rows(rows):
    centred = rows - jnp.mean(rows, axis=-1, keepdims=True)
    spread = jnp.mean(centred * centred, axis=-1, keepdims=True)
    inverse = lax.rsqrt(spread + EPS)
    return centred * inverse, inverse


def place(name):
    return lax.axis_index(name)


def frame_index():
    return place("xh") * 2 + place("core")


def x_index():
    return place("xh") * 2 + place("xl")


def unit_kernel(resid_ref, gain_ref, grad_ref, *outs):
    normed, _ = norm_rows(resid_ref[...].astype(F32))
    work = outs[-1]
    work[:, :D] = normed * gain_ref[...]
    work[:, D:] = grad_ref[...].astype(F32)
    f = frame_index()
    for k in range(FRAMES):
        at = pl.multiple_of((f ^ k) * CHUNK, CHUNK)
        outs[k][...] = work[pl.ds(at, CHUNK), :].astype(BF16)


def group_kernel(*refs):
    ins, outs, work = refs[:FRAMES], refs[FRAMES : FRAMES + CLIPS], refs[-1]
    for k in range(FRAMES):
        at = slice(k * CHUNK, (k + 1) * CHUNK)
        for o in range(CLIPS):
            outs[o][at, :D] = ins[k][:, :D]
    grad = jnp.concatenate([ins[k][:, D:] for k in range(FRAMES)], axis=0).astype(F32)
    for t in range(D // 128):
        at = slice(t * 128, (t + 1) * 128)
        work[at, :] = grad[:, at].T
    d = place("dp")
    gap = jnp.zeros((GO_PAD - GROUP * HD, ROWS), F32)
    for o in range(CLIPS):
        g = lax.rem(d + o, CLIPS)
        heads = [
            work[pl.ds(pl.multiple_of((4 * i + g) * HD, 8), HD), :] for i in range(GROUP)
        ]
        outs[o][:, D:] = jnp.concatenate([*heads, gap], axis=0).T.astype(BF16)


def weight_kernel(w_ref, *refs):
    outs, work = refs[:CLIPS], refs[-1]
    work[...] = w_ref[...].astype(F32)
    d = place("dp")
    lanes = pl.ds(pl.multiple_of(place("core") * (D - HALF), 128), HALF)
    for o in range(CLIPS):
        g = lax.rem(d + o, CLIPS)
        heads = [work[pl.ds(pl.multiple_of((4 * j + g) * HD, 8), HD), lanes] for j in range(3)]
        outs[o][...] = jnp.concatenate(heads, axis=0).astype(BF16)


def join_kernel(*refs):
    ins, out_ref, work = refs[:CLIPS], refs[CLIPS], refs[-1]
    d = place("dp")
    for o in range(CLIPS):
        s = lax.rem(d + CLIPS - o, CLIPS)
        work[pl.ds(pl.multiple_of(s * 3 * HD, 8), 3 * HD), :] = ins[o][...].astype(F32)
    out_ref[...] = work[...].astype(BF16)


def qkv_kernel(qkv_ref, out_ref, work):
    for t in range(3 * D // 128):
        work[t * 128 : (t + 1) * 128, :] = qkv_ref[:, t * 128 : (t + 1) * 128].astype(F32).T
    for h in range(HEADS):
        parts = [work[(p * HEADS + h) * HD : (p * HEADS + h + 1) * HD, :] for p in range(3)]
        out_ref[h] = jnp.concatenate(parts, axis=0).astype(BF16)


def temporal_kernel(*refs):
    rows_in, halves = refs[:CLIPS], refs[CLIPS : CLIPS + 2]
    ups, (all_ref, dproj_ref, proj, grad, dproj, w_ref) = refs[CLIPS + 2 : -6], refs[-6:]
    for core in range(2):

        @pl.when(place("core") == core)
        def _():
            w_ref[:, :HALF] = halves[core][...]
            w_ref[:, D - HALF :] = halves[1 - core][...]

    for k in range(FRAMES):
        at = slice(k * CHUNK, (k + 1) * CHUNK)
        for o in range(CLIPS):
            to = (k * CLIPS + o) * CHUNK
            all_ref[to : to + CHUNK, :] = rows_in[o][at, :D]
        rows = jnp.concatenate([rows_in[o][at, D:] for o in range(CLIPS)], axis=0).astype(F32)
        grad[:, k * ROWS : (k + 1) * ROWS] = rows.T[: GROUP * HD]
    proj[...] = dot(w_ref[...], all_ref[...], 1, 1).astype(BF16).astype(F32)

    def one_head(n, carry):
        def load(ref, base):
            at = pl.ds(pl.multiple_of(base + n * HD, 8), HD)
            return [ref[at, f * ROWS : (f + 1) * ROWS] for f in range(FRAMES)]

        q, k, v = (load(proj, p * GROUP * HD) for p in range(3))
        g = load(grad, 0)

        def total(a, b):
            return jnp.sum(a * b, axis=0, keepdims=True)

        span = range(FRAMES)
        ds, p_low = [], []
        for f in span:
            s = [total(q[f], k[j]) * SCALE for j in span]
            top = functools.reduce(jnp.maximum, s)
            e = [jnp.exp(x - top) for x in s]
            below = functools.reduce(jnp.add, e)
            prob = [x / below for x in e]
            dp = [total(g[f], v[j]) for j in span]
            mid = functools.reduce(jnp.add, [x * y for x, y in zip(prob, dp)])
            ds.append([(x * (y - mid)).astype(BF16).astype(F32) for x, y in zip(prob, dp)])
            p_low.append([x.astype(BF16).astype(F32) for x in prob])

        def put(base, f, value):
            at = pl.ds(pl.multiple_of(base + n * HD, 8), HD)
            dproj[at, f * ROWS : (f + 1) * ROWS] = value

        def mix(weights, values):
            return functools.reduce(jnp.add, [w * x for w, x in zip(weights, values)])

        for f in span:
            put(0, f, mix(ds[f], k) * SCALE)
            put(GROUP * HD, f, mix([ds[j][f] for j in span], q) * SCALE)
            put(2 * GROUP * HD, f, mix([p_low[j][f] for j in span], g))
        return carry

    lax.fori_loop(0, GROUP, one_head, 0)
    width = 3 * GROUP * HD
    gap = jnp.zeros((WIDE - width, CLIPS * ROWS), F32)
    low = jnp.concatenate([dproj[...], gap], axis=0).T.astype(BF16)
    dproj_ref[...] = low
    up = dot(low[:, :width], w_ref[...], 1, 0).astype(BF16)
    for k in range(FRAMES):
        for o in range(CLIPS):
            at = (k * CLIPS + o) * CHUNK
            ups[o][k * CHUNK : (k + 1) * CHUNK, :] = up[at : at + CHUNK]


def home_rows_kernel(*refs):
    ins, outs = refs[:CLIPS], refs[CLIPS:]
    total = functools.reduce(jnp.add, [r[...].astype(F32) for r in ins]).astype(BF16)
    for k in range(FRAMES):
        outs[k][...] = total[k * CHUNK : (k + 1) * CHUNK]


def stream_kernel(*refs):
    ins, (resid_ref, gain_ref, w_ref, stream_ref, head_ref) = refs[:FRAMES], refs[FRAMES : FRAMES + 5]
    cols, work = refs[FRAMES + 5 : -1], refs[-1]
    f = frame_index()
    for k in range(FRAMES):
        at = pl.multiple_of((f ^ k) * CHUNK, CHUNK)
        work[pl.ds(at, CHUNK), :] = ins[k][...].astype(F32)
    up = work[...]
    normed, inverse = norm_rows(resid_ref[...].astype(F32))
    scaled = up * gain_ref[...]
    mean_up = jnp.mean(scaled, axis=-1, keepdims=True)
    mean_cross = jnp.mean(scaled * normed, axis=-1, keepdims=True)
    stream = (inverse * (scaled - mean_up - normed * mean_cross)).astype(BF16)
    stream_ref[...] = stream
    spatial = dot(w_ref[...], stream, 1, 1)
    for h in range(HEADS):
        head_ref[h] = spatial[h * HD : (h + 1) * HD].astype(BF16)
    wide = stream.astype(F32)
    d = place("dp")
    for o in range(CLIPS):
        g = lax.rem(d + o, CLIPS)
        turned = pltpu.roll(wide, lax.rem(D - (D // CLIPS) * g, D), 1)
        cols[o][...] = turned[:, :GO_PAD].astype(BF16)


def split_core(total, keep_ref, away_ref):
    core = place("core")
    for xh in range(2):
        for ref, which in ((keep_ref, core), (away_ref, 1 - core)):
            at = pl.multiple_of((xh * 2 + which) * 288, 8)
            ref[xh] = total[pl.ds(at, 288), :].astype(BF16)


def qkv_grad_kernel(unit_ref, dproj_ref, keep_ref, away_ref, total):
    total[...] = dot(unit_ref[...].astype(F32).T.astype(BF16), dproj_ref[...], 1, 0)
    split_core(total, keep_ref, away_ref)


def proj_grad_kernel(*refs):
    rows, cols, (keep_ref, away_ref, total) = refs[:CLIPS], refs[CLIPS : 2 * CLIPS], refs[-3:]
    outs = jnp.concatenate([r[...] for r in rows], axis=0).astype(F32).T.astype(BF16)
    total[...] = dot(outs, jnp.concatenate([c[...] for c in cols], axis=0), 1, 0)
    split_core(total, keep_ref, away_ref)


def split_line_kernel(keep_ref, came_ref, near_ref, far_ref):
    xl = place("xl")
    for xh in range(2):
        for ref, which in ((near_ref, xl), (far_ref, 1 - xl)):
            at = pl.ds(pl.multiple_of(which * 144, 16), 144)
            both = keep_ref[xh, at, :].astype(F32) + came_ref[xh, at, :].astype(F32)
            ref[xh] = both.astype(BF16)


def split_far_kernel(keep_ref, came_ref, near_ref, far_ref):
    xh = place("xh")
    for ref, which in ((near_ref, xh), (far_ref, 1 - xh)):
        ref[...] = (keep_ref[which].astype(F32) + came_ref[which].astype(F32)).astype(BF16)


def slot_kernel(keep_ref, came_ref, *outs):
    total = keep_ref[...].astype(F32) + came_ref[...].astype(F32)
    wide = jnp.concatenate([total, jnp.zeros((144, 128), F32)], axis=1)
    d = place("dp")
    for o in range(CLIPS):
        g = lax.rem(d + o, CLIPS)
        turned = pltpu.roll(wide, lax.rem(WIDE + 128 - 3 * HD * g, WIDE + 128), 1)
        outs[o][...] = turned[:, :256].astype(BF16)


def merge_kernel(*refs):
    slots, (keep_ref, came_ref, near_ref, far_ref, total, blocks) = refs[:CLIPS], refs[CLIPS:]
    total[144:, :] = jnp.zeros((8, MERGED), F32)
    for o in range(CLIPS):
        total[:144, o * 256 : (o + 1) * 256] = slots[o][...].astype(F32)
    total[:144, CLIPS * 256 :] = keep_ref[...].astype(F32) + came_ref[...].astype(F32)
    for z in range(8):
        blocks[z] = total[z * 18 : z * 18 + 24, :]
    half = place("z") // 4
    for i in range(4):
        near_ref[i] = blocks[half * 4 + i].astype(BF16)
        far_ref[i] = blocks[(1 - half) * 4 + i].astype(BF16)


def halve_kernel(keep_ref, came_ref, near_ref, far_ref):
    half = near_ref.shape[0]
    mine = lax.rem(place("z") // half, 2)
    for i in range(half):
        for ref, which in ((near_ref, mine), (far_ref, 1 - mine)):
            at = which * half + i
            ref[i] = (keep_ref[at].astype(F32) + came_ref[at].astype(F32)).astype(BF16)


def last_kernel(keep_ref, came_ref, slots_ref, proj_ref):
    total = keep_ref[0].astype(F32) + came_ref[0].astype(F32)
    d = place("dp")
    for o in range(CLIPS):
        slots_ref[lax.rem(d + CLIPS - o, CLIPS)] = total[:18, o * 256 : o * 256 + 3 * HD]
    proj_ref[...] = total[:18, CLIPS * 256 : CLIPS * 256 + D // CLIPS]


def pad_rows(x, rows):
    return jnp.concatenate([x, jnp.zeros((rows - x.shape[0], x.shape[1]), x.dtype)], axis=0)


def probs_kernel(qkv_ref, p_ref, o_ref, k_ref, qt_ref, vt_ref, q_rows, kt, v_rows):
    @pl.when(pl.program_id(0) == 0)
    def _():
        for b in range(HEADS):
            at = slice(b * ROWS, (b + 1) * ROWS)
            block = qkv_ref[b].astype(F32)
            q, k, v = (pad_rows(block[p * HD : (p + 1) * HD], 128) for p in range(3))
            q_rows[at, :] = q.T.astype(BF16)
            k_ref[at, :] = k.T.astype(BF16)
            v_rows[at, :] = v.T.astype(BF16)
            kt[:, at] = k.astype(BF16)
            vt_ref[:, at] = v.astype(BF16)
            qt_ref[:, at] = q[:80].astype(BF16)

    at = pl.multiple_of(pl.program_id(0) * BLOCK, BLOCK)
    scores = dot(q_rows[pl.ds(at, BLOCK), :], kt[...], 1, 0)
    top = jnp.max(scores, axis=-1, keepdims=True)
    factor = SCALE * math.log2(math.e)
    e = jnp.exp2((scores - top) * factor)
    low = (e * (1.0 / jnp.sum(e, axis=-1, keepdims=True))).astype(BF16)
    p_ref[...] = low
    o_ref[...] = dot(low, v_rows[...], 1, 0)


def spatial_kernel(
    do_ref,
    p_ref,
    o_ref,
    k_ref,
    qt_ref,
    vt_ref,
    out_ref,
    do_rows,
    dot_cols,
    dq,
    dk,
    dv,
):
    step = pl.program_id(0)

    @pl.when(step == 0)
    def _():
        for b in range(HEADS):
            at = slice(b * ROWS, (b + 1) * ROWS)
            block = pad_rows(do_ref[b].astype(F32), 128)
            do_rows[at, :] = block.T.astype(BF16)
            dot_cols[:, at] = block[:80].astype(BF16)
        dk[...] = jnp.zeros_like(dk)
        dv[...] = jnp.zeros_like(dv)

    at = pl.ds(pl.multiple_of(step * BLOCK, BLOCK), BLOCK)
    do = do_rows[at, :]
    probs = p_ref[...]
    dp = dot(do, vt_ref[...], 1, 0)
    mid = jnp.sum(do.astype(F32) * o_ref[...], axis=-1, keepdims=True)
    ds = (probs.astype(F32) * (dp - mid)).astype(BF16)
    dq[:, at] = (dot(ds, k_ref[...], 1, 0) * SCALE).T[:HD]
    dk[...] += dot(qt_ref[...], ds, 1, 0)
    dv[...] += dot(dot_cols[:, at], probs, 1, 0)

    @pl.when(step == pl.num_programs(0) - 1)
    def _():
        for b in range(HEADS):
            at = slice(b * ROWS, (b + 1) * ROWS)
            parts = [dq[:, at], dk[:HD, at] * SCALE, dv[:HD, at]]
            out_ref[b] = jnp.concatenate(parts, axis=0).astype(BF16)


def home_kernel(in_ref, out_ref, work):
    for h in range(HEADS):
        block = in_ref[h].astype(F32)
        for p in range(3):
            at = (p * HEADS + h) * HD
            work[at : at + HD, :] = block[p * HD : (p + 1) * HD]
    for t in range(3 * D // 128):
        at = slice(t * 128, (t + 1) * 128)
        out_ref[:, at] = work[at, :].T.astype(BF16)


def around(x, axis, size, step):
    return lax.ppermute(x, axis, [(i, (i + step) % size) for i in range(size)])


def across(x, axis, size, flip):
    return lax.ppermute(x, axis, [(i, i ^ flip) for i in range(size)])


def per_device(spatial_qkv, spatial_out, resid, norm_gain, qkv_weight, out_weight, grad_out):
    every = ("dp", "xh", "core")
    heads = ("xl", "z")
    frame = ("xh", "core")
    line = ("xh", "xl")
    shape = jax.ShapeDtypeStruct
    resid = resid.reshape(ROWS, D)
    grad_out = grad_out.reshape(ROWS, D)
    qkv_rows = spatial_qkv.reshape(ROWS, 3 * D)
    out_rows = spatial_out.reshape(ROWS, D)
    gain = norm_gain.reshape(1, D)
    rows = CLIPS * ROWS
    width = 3 * GROUP * HD

    whole = lambda *dims: pl.BlockSpec(dims, lambda i: (0,) * len(dims))
    by_row = lambda wide: pl.BlockSpec((BLOCK, wide), lambda i: (i, 0))

    mine = call(
        unit_kernel,
        [shape((CHUNK, 2 * D), BF16)] * FRAMES,
        (resid, gain, grad_out),
        0.5,
        scratch=[pltpu.VMEM((ROWS, 2 * D), F32)],
    )
    ours = [b if k == 0 else across(b, frame, FRAMES, k) for k, b in enumerate(mine)]
    qkv_out = call(
        qkv_kernel,
        shape((HEADS, 3 * HD, ROWS), BF16),
        (qkv_rows,),
        1.2,
        scratch=[pltpu.VMEM((3 * D, ROWS), F32)],
        after=[mine[0]],
    )
    qkv_in = lax.all_to_all(qkv_out, heads, 0, 0, tiled=True)
    w_blocks = call(
        weight_kernel,
        [shape((3 * HD, HALF), BF16)] * CLIPS,
        (qkv_weight.T,),
        0.5,
        scratch=[pltpu.VMEM((width, D), F32)],
        after=[ours[1]],
    )
    w_in = [b if o == 0 else around(b, "dp", CLIPS, o) for o, b in enumerate(w_blocks)]
    groups = call(
        group_kernel,
        [shape((ROWS, D + GO_PAD), BF16)] * CLIPS,
        tuple(ours),
        0.5,
        scratch=[pltpu.VMEM((D, ROWS), F32)],
    )
    rows_in = [b if o == 0 else around(b, "dp", CLIPS, o) for o, b in enumerate(groups)]
    w_half = call(
        join_kernel,
        shape((width, HALF), BF16),
        tuple(w_in),
        0.5,
        scratch=[pltpu.VMEM((width, HALF), F32)],
        after=[groups[0]],
    )
    w_other = across(w_half, "core", 2, 1)

    *ups, unit_all, d_proj = call(
        temporal_kernel,
        [shape((ROWS, D), BF16)] * CLIPS + [shape((rows, D), BF16), shape((rows, WIDE), BF16)],
        (*rows_in, w_half, w_other),
        5,
        scratch=[
            pltpu.VMEM((width, rows), F32),
            pltpu.VMEM((GROUP * HD, rows), F32),
            pltpu.VMEM((width, rows), F32),
            pltpu.VMEM((width, D), BF16),
        ],
    )
    ups = [b if o == 0 else around(b, "dp", CLIPS, CLIPS - o) for o, b in enumerate(ups)]
    home = call(home_rows_kernel, [shape((CHUNK, D), BF16)] * FRAMES, tuple(ups), 0.5)
    up_in = [b if k == 0 else across(b, frame, FRAMES, k) for k, b in enumerate(home)]
    out_rows = lax.optimization_barrier((out_rows, home[0]))[0]
    out_in = [out_rows if o == 0 else around(out_rows, "dp", CLIPS, o) for o in range(CLIPS)]
    keep, away = call(
        qkv_grad_kernel,
        [shape((2, 288, WIDE), BF16)] * 2,
        (unit_all, d_proj),
        2.5,
        scratch=[pltpu.VMEM((D, WIDE), F32)],
    )

    def split_to_x(keep, away):
        wide = keep.shape[2]
        came = across(away, "core", 2, 1)
        near, far = call(
            split_line_kernel, [shape((2, 144, wide), BF16)] * 2, (keep, came), 0.7
        )
        came = across(far, "xl", 2, 1)
        near, far = call(split_far_kernel, [shape((144, wide), BF16)] * 2, (near, came), 0.5)
        return near, across(far, "xh", 2, 1)

    slots = call(
        slot_kernel, [shape((144, 256), BF16)] * CLIPS, split_to_x(keep, away), 0.7
    )
    slots = [b if o == 0 else around(b, "dp", CLIPS, o) for o, b in enumerate(slots)]
    probs, mixed, keys, queries_t, values_t = call(
        probs_kernel,
        [
            shape((TOKENS, TOKENS), BF16),
            shape((TOKENS, 128), F32),
            shape((TOKENS, 128), BF16),
            shape((80, TOKENS), BF16),
            shape((128, TOKENS), BF16),
        ],
        (qkv_in,),
        10.5,
        vmem=58,
        scratch=[
            pltpu.VMEM((TOKENS, 128), BF16),
            pltpu.VMEM((128, TOKENS), BF16),
            pltpu.VMEM((TOKENS, 128), BF16),
        ],
        after=[keep],
        grid=(TOKENS // BLOCK,),
        in_specs=[whole(HEADS, 3 * HD, ROWS)],
        out_specs=[
            by_row(TOKENS),
            by_row(128),
            whole(TOKENS, 128),
            whole(80, TOKENS),
            whole(128, TOKENS),
        ],
    )

    stream, head_out, *cols = call(
        stream_kernel,
        [shape((ROWS, D), BF16), shape((HEADS, HD, ROWS), BF16)]
        + [shape((ROWS, GO_PAD), BF16)] * CLIPS,
        (*up_in, resid, gain, out_weight),
        2.2,
        scratch=[pltpu.VMEM((ROWS, D), F32)],
        after=[queries_t],
    )
    head_in = lax.all_to_all(head_out, heads, 0, 0, tiled=True)

    cols = [b if o == 0 else around(b, "dp", CLIPS, o) for o, b in enumerate(cols)]
    keep, away = call(
        proj_grad_kernel,
        [shape((2, 288, GO_PAD), BF16)] * 2,
        (*out_in, *cols),
        2,
        scratch=[pltpu.VMEM((D, GO_PAD), F32)],
    )
    near, far = call(
        merge_kernel,
        [shape((4, 24, MERGED), BF16)] * 2,
        (*slots, *split_to_x(keep, away)),
        1,
        scratch=[pltpu.VMEM((152, MERGED), F32), pltpu.VMEM((8, 24, MERGED), F32)],
    )
    for half in (2, 1):
        came = across(far, "z", 8, 2 * half)
        near, far = call(
            halve_kernel, [shape((half, 24, MERGED), BF16)] * 2, (near, came), 0.5
        )
    came = across(far, "z", 8, 1)
    ordered, grad_proj = call(
        last_kernel,
        [shape((CLIPS, 18, 3 * HD), F32), shape((18, D // CLIPS), F32)],
        (near, came),
        0.5,
    )
    grad_qkv = (
        ordered.reshape(CLIPS, 18, 3, HD).transpose(1, 2, 0, 3).reshape(18, 3 * D // CLIPS)
    )

    d_out = call(
        spatial_kernel,
        shape((HEADS, 3 * HD, ROWS), BF16),
        (head_in, probs, mixed, keys, queries_t, values_t),
        10.5,
        vmem=58,
        scratch=[
            pltpu.VMEM((TOKENS, 128), BF16),
            pltpu.VMEM((80, TOKENS), BF16),
            pltpu.VMEM((HD, TOKENS), F32),
            pltpu.VMEM((80, TOKENS), F32),
            pltpu.VMEM((80, TOKENS), F32),
        ],
        grid=(TOKENS // BLOCK,),
        in_specs=[
            whole(HEADS, HD, ROWS),
            by_row(TOKENS),
            by_row(128),
            whole(TOKENS, 128),
            pl.BlockSpec((80, BLOCK), lambda i: (0, i)),
            whole(128, TOKENS),
        ],
        out_specs=whole(HEADS, 3 * HD, ROWS),
    )
    d_in = lax.all_to_all(d_out, heads, 0, 0, tiled=True)
    d_qkv = call(
        home_kernel,
        shape((ROWS, 3 * D), BF16),
        (d_in,),
        1.2,
        scratch=[pltpu.VMEM((3 * D, ROWS), F32)],
    )
    return (
        d_qkv.reshape(1, 1, ROWS, 3 * D),
        stream.reshape(1, 1, ROWS, D),
        grad_qkv,
        grad_proj,
    )


def solution(mesh):
    fine = Mesh(mesh.devices.reshape(4, 2, 2, 2, 8), ("dp", "xh", "core", "xl", "z"))
    frame = ("xh", "core")
    head = ("xl", "z")
    rows = P("dp", frame, head, None)
    return jax.shard_map(
        per_device,
        mesh=fine,
        in_specs=(rows, rows, rows, P(), P(None, "dp"), P(), rows),
        out_specs=(rows, rows, P(frame + head, "dp"), P(frame + head, "dp")),
        check_vma=False,
    )
```

```python
import functools
import math

import jax
import jax.numpy as jnp
from jax import lax
from jax.experimental import pallas as pl
from jax.experimental.pallas import tpu as pltpu
from jax.sharding import Mesh, PartitionSpec as P

D = 1152
HEADS = 16
HD = 72
ROWS = 128
CLIPS = 4
FRAMES = 4
CHUNK = 32
GROUP = 4
GO_PAD = 384
WIDE = 896
HALF = 640
TOKENS = 2048
BLOCK = 256
EPS = 1e-06
LOW = 0.001
RIDE = 56
SCALE = HD ** (-0.5)
F32 = jnp.float32
BF16 = jnp.bfloat16
MIB = 1 << 20


def dot(left, right, left_dim, right_dim):
    return lax.dot_general(
        left, right, (((left_dim,), (right_dim,)), ((), ())), preferred_element_type=F32
    )


def call(kernel, out_shape, args, us, scratch=(), vmem=40, after=(), hold=(), in_specs=None, out_specs=None, **kw):
    held, extra, made = len(args), len(after) + len(hold), len(out_shape)
    vmem_spec, any_spec, hbm_spec = (
        pl.BlockSpec(memory_space=m) for m in (pltpu.VMEM, pl.ANY, pltpu.HBM)
    )
    token = jax.ShapeDtypeStruct((8, 128), F32)

    def body(*refs):
        ins, rest = refs[:held], refs[held + extra :]
        kernel(*ins, *rest[:made], *rest[made + 1 :])

    *outs, done = pl.pallas_call(
        body,
        out_shape=[*out_shape, token],
        in_specs=[*(in_specs or [vmem_spec] * held), *[any_spec] * len(after), *[hbm_spec] * len(hold)],
        out_specs=[*(out_specs or [vmem_spec] * made), any_spec],
        scratch_shapes=list(scratch),
        cost_estimate=pl.CostEstimate(
            flops=int(us * 1.1e9), bytes_accessed=int(us * 1e6), transcendentals=0
        ),
        compiler_params=pltpu.CompilerParams(vmem_limit_bytes=vmem * MIB),
        **kw,
    )(*args, *after, *hold)
    return outs, done


def norm_rows(rows):
    centred = rows - jnp.mean(rows, axis=-1, keepdims=True)
    spread = jnp.mean(centred * centred, axis=-1, keepdims=True)
    inverse = lax.rsqrt(spread + EPS)
    return centred * inverse, inverse


def place(name):
    return lax.axis_index(name)


def frame_index():
    return place("xh") * 2 + place("core")


def x_index():
    return place("xh") * 2 + place("xl")


def unit_kernel(resid_ref, gain_ref, grad_ref, *outs):
    normed, _ = norm_rows(resid_ref[...].astype(F32))
    work = outs[-1]
    work[:, :D] = normed * gain_ref[...]
    work[:, D:] = grad_ref[...].astype(F32)
    f = frame_index()
    for k in range(FRAMES):
        at = pl.multiple_of((f ^ k) * CHUNK, CHUNK)
        outs[k][...] = work[pl.ds(at, CHUNK), :].astype(BF16)


def group_kernel(*refs):
    ins, outs, work = refs[:FRAMES], refs[FRAMES : FRAMES + CLIPS], refs[-1]
    for k in range(FRAMES):
        at = slice(k * CHUNK, (k + 1) * CHUNK)
        for o in range(CLIPS):
            outs[o][at, :D] = ins[k][:, :D]
    grad = jnp.concatenate([ins[k][:, D:] for k in range(FRAMES)], axis=0).astype(F32)
    for t in range(D // 128):
        at = slice(t * 128, (t + 1) * 128)
        work[at, :] = grad[:, at].T
    d = place("dp")
    gap = jnp.zeros((GO_PAD - GROUP * HD, ROWS), F32)
    for o in range(CLIPS):
        g = lax.rem(d + o, CLIPS)
        heads = [
            work[pl.ds(pl.multiple_of((4 * i + g) * HD, 8), HD), :] for i in range(GROUP)
        ]
        outs[o][:, D:] = jnp.concatenate([*heads, gap], axis=0).T.astype(BF16)


def weight_kernel(w_ref, *refs):
    outs, work = refs[:CLIPS], refs[-1]
    work[...] = w_ref[...].astype(F32)
    d = place("dp")
    lanes = pl.ds(pl.multiple_of(place("core") * (D - HALF), 128), HALF)
    for o in range(CLIPS):
        g = lax.rem(d + o, CLIPS)
        heads = [work[pl.ds(pl.multiple_of((4 * j + g) * HD, 8), HD), lanes] for j in range(3)]
        outs[o][...] = jnp.concatenate(heads, axis=0).astype(BF16)


def join_kernel(*refs):
    ins, out_ref, work = refs[:CLIPS], refs[CLIPS], refs[-1]
    d = place("dp")
    for o in range(CLIPS):
        s = lax.rem(d + CLIPS - o, CLIPS)
        work[pl.ds(pl.multiple_of(s * 3 * HD, 8), 3 * HD), :] = ins[o][...].astype(F32)
    out_ref[...] = work[...].astype(BF16)


def qkv_kernel(qkv_ref, out_ref, work):
    for t in range(3 * D // 128):
        work[t * 128 : (t + 1) * 128, :] = qkv_ref[:, t * 128 : (t + 1) * 128].astype(F32).T
    for h in range(HEADS):
        parts = [work[(p * HEADS + h) * HD : (p * HEADS + h + 1) * HD, :] for p in range(3)]
        out_ref[h] = jnp.concatenate(parts, axis=0).astype(BF16)


def temporal_kernel(*refs):
    rows_in, halves = refs[:CLIPS], refs[CLIPS : CLIPS + 2]
    up_ref, all_ref, dproj_ref, proj, grad, dproj, w_ref = refs[CLIPS + 2 :]
    d, frame = place("dp"), frame_index()
    for core in range(2):

        @pl.when(place("core") == core)
        def _():
            w_ref[:, :HALF] = halves[core][...]
            w_ref[:, D - HALF :] = halves[1 - core][...]

    for k in range(FRAMES):
        at = slice(k * CHUNK, (k + 1) * CHUNK)
        for o in range(CLIPS):
            to = (k * CLIPS + o) * CHUNK
            all_ref[to : to + CHUNK, :] = rows_in[o][at, :D]
        rows = jnp.concatenate([rows_in[o][at, D:] for o in range(CLIPS)], axis=0).astype(F32)
        grad[:, k * ROWS : (k + 1) * ROWS] = rows.T[: GROUP * HD]
    proj[...] = dot(w_ref[...], all_ref[...], 1, 1).astype(BF16).astype(F32)

    def one_head(n, carry):
        def load(ref, base):
            at = pl.ds(pl.multiple_of(base + n * HD, 8), HD)
            return [ref[at, f * ROWS : (f + 1) * ROWS] for f in range(FRAMES)]

        q, k, v = (load(proj, p * GROUP * HD) for p in range(3))
        g = load(grad, 0)

        def total(a, b):
            return jnp.sum(a * b, axis=0, keepdims=True)

        span = range(FRAMES)
        ds, p_low = [], []
        for f in span:
            s = [total(q[f], k[j]) * SCALE for j in span]
            top = functools.reduce(jnp.maximum, s)
            e = [jnp.exp(x - top) for x in s]
            below = functools.reduce(jnp.add, e)
            prob = [x / below for x in e]
            dp = [total(g[f], v[j]) for j in span]
            mid = functools.reduce(jnp.add, [x * y for x, y in zip(prob, dp)])
            ds.append([(x * (y - mid)).astype(BF16).astype(F32) for x, y in zip(prob, dp)])
            p_low.append([x.astype(BF16).astype(F32) for x in prob])

        def put(base, f, value):
            at = pl.ds(pl.multiple_of(base + n * HD, 8), HD)
            dproj[at, f * ROWS : (f + 1) * ROWS] = value

        def mix(weights, values):
            return functools.reduce(jnp.add, [w * x for w, x in zip(weights, values)])

        for f in span:
            put(0, f, mix(ds[f], k) * SCALE)
            put(GROUP * HD, f, mix([ds[j][f] for j in span], q) * SCALE)
            put(2 * GROUP * HD, f, mix([p_low[j][f] for j in span], g))
        return carry

    lax.fori_loop(0, GROUP, one_head, 0)
    width = 3 * GROUP * HD
    gap = jnp.zeros((WIDE - width, CLIPS * ROWS), F32)
    low = jnp.concatenate([dproj[...], gap], axis=0).T.astype(BF16)
    dproj_ref[...] = low
    up = dot(low[:, :width], w_ref[...], 1, 0).astype(BF16)
    for k in range(FRAMES):
        for o in range(CLIPS):
            at = (k * CLIPS + o) * CHUNK
            up_ref[lax.rem(d + CLIPS - o, CLIPS), frame ^ k] = up[at : at + CHUNK]


def stream_kernel(up_ref, resid_ref, gain_ref, w_hbm, stream_ref, head_ref, w_ref, sem):
    copy = pltpu.make_async_copy(w_hbm, w_ref, sem)
    copy.start()
    parts = []
    for f in range(FRAMES):
        parts.append(functools.reduce(jnp.add, [up_ref[g, f].astype(F32) for g in range(CLIPS)]))
    up = jnp.concatenate(parts, axis=0)
    normed, inverse = norm_rows(resid_ref[...].astype(F32))
    scaled = up * gain_ref[...]
    mean_up = jnp.mean(scaled, axis=-1, keepdims=True)
    mean_cross = jnp.mean(scaled * normed, axis=-1, keepdims=True)
    stream = (inverse * (scaled - mean_up - normed * mean_cross)).astype(BF16)
    stream_ref[...] = stream
    copy.wait()
    spatial = dot(w_ref[...], stream, 1, 1)
    for h in range(HEADS):
        head_ref[h] = spatial[h * HD : (h + 1) * HD].astype(BF16)


def cols_kernel(stream_ref, *cols):
    wide = stream_ref[...].astype(F32)
    d = place("dp")
    for o in range(CLIPS):
        g = lax.rem(d + o, CLIPS)
        turned = pltpu.roll(wide, lax.rem(D - (D // CLIPS) * g, D), 1)
        cols[o][...] = turned[:, :GO_PAD].astype(BF16)


def split_core(total, keep_ref, away_ref):
    core = place("core")
    for xh in range(2):
        for ref, which in ((keep_ref, core), (away_ref, 1 - core)):
            at = pl.multiple_of((xh * 2 + which) * 288, 8)
            ref[xh] = total[pl.ds(at, 288), :].astype(BF16)


def qkv_grad_kernel(unit_ref, dproj_ref, keep_ref, away_ref, total):
    total[...] = dot(unit_ref[...].astype(F32).T.astype(BF16), dproj_ref[...], 1, 0)
    split_core(total, keep_ref, away_ref)


def proj_grad_kernel(*refs):
    outs, cols, (keep_ref, away_ref, total, rows, sems) = refs[:CLIPS], refs[CLIPS : 2 * CLIPS], refs[-5:]
    copies = [
        pltpu.make_async_copy(ref, rows.at[pl.ds(o * ROWS, ROWS)], sems.at[o])
        for o, ref in enumerate(outs)
    ]
    for copy in copies:
        copy.start()
    columns = jnp.concatenate([c[...] for c in cols], axis=0)
    for copy in copies:
        copy.wait()
    total[...] = dot(rows[...].astype(F32).T.astype(BF16), columns, 1, 0)
    split_core(total, keep_ref, away_ref)


def z_split_kernel(keep_ref, came_ref, near_ref, far_ref):
    half = place("z") // 4
    for xh in range(2):
        for xl in range(2):
            for ref, which in ((near_ref, half), (far_ref, 1 - half)):
                at = pl.ds(pl.multiple_of(xl * 144 + which * 72, 8), 72)
                both = keep_ref[xh, at, :].astype(F32) + came_ref[xh, at, :].astype(F32)
                ref[xh * 2 + xl] = both.astype(BF16)


def z_halve_kernel(keep_ref, came_ref, near_ref, far_ref):
    first = near_ref.shape[1] == 36
    high = lax.rem(place("z") // (1 if first else 2), 2) == 1
    for b in range(4):
        both = keep_ref[b].astype(F32) + came_ref[b].astype(F32)
        if first:
            upper = jnp.concatenate([both[18:36], both[54:]], axis=0)
            lower = jnp.concatenate([both[:18], both[36:54]], axis=0)
        else:
            upper, lower = both[18:], both[:18]
        near_ref[b] = jnp.where(high, upper, lower).astype(BF16)
        far_ref[b] = jnp.where(high, lower, upper).astype(BF16)


def xl_kernel(keep_ref, came_ref, near_ref, far_ref):
    xl = place("xl")
    for xh in range(2):
        for ref, which in ((near_ref, xl), (far_ref, 1 - xl)):
            at = xh * 2 + which
            ref[xh] = (keep_ref[at].astype(F32) + came_ref[at].astype(F32)).astype(BF16)


def pair_kernel(keep_ref, came_ref, near_ref, far_ref):
    xh = place("xh")
    for ref, which in ((near_ref, xh), (far_ref, 1 - xh)):
        ref[...] = (keep_ref[which].astype(F32) + came_ref[which].astype(F32)).astype(BF16)


def slot_kernel(keep_ref, came_ref, *outs):
    total = keep_ref[...].astype(F32) + came_ref[...].astype(F32)
    wide = jnp.concatenate([total, jnp.zeros((18, 128), F32)], axis=1)
    wide = jnp.concatenate([wide, jnp.zeros((6, WIDE + 128), F32)], axis=0)
    d = place("dp")
    for o in range(CLIPS):
        g = lax.rem(d + o, CLIPS)
        turned = pltpu.roll(wide, lax.rem(WIDE + 128 - 3 * HD * g, WIDE + 128), 1)
        outs[o][...] = turned[:, :256]


def order_kernel(*refs):
    slots, out_ref = refs[:CLIPS], refs[CLIPS]
    d = place("dp")
    for o in range(CLIPS):
        out_ref[lax.rem(d + CLIPS - o, CLIPS)] = slots[o][:18, : 3 * HD]


def pack_kernel(d_ref, near_ref, far_ref, out_ref, total):
    total[...] = near_ref[...].astype(F32) + far_ref[...].astype(F32)
    rest = jnp.zeros((RIDE - 54, 128), F32)
    for b in range(HEADS):
        at = slice(b * 18, (b + 1) * 18)
        parts = [total[at, i * 128 : (i + 1) * 128] for i in range(3)]
        block = [*parts, rest, d_ref[b].astype(F32)]
        out_ref[b] = jnp.concatenate(block, axis=0).astype(BF16)


def pad_rows(x, rows):
    return jnp.concatenate([x, jnp.zeros((rows - x.shape[0], x.shape[1]), x.dtype)], axis=0)


def probs_kernel(qkv_ref, p_ref, o_ref, k_ref, qt_ref, vt_ref, q_rows, kt, v_rows):
    @pl.when(pl.program_id(0) == 0)
    def _():
        for b in range(HEADS):
            at = slice(b * ROWS, (b + 1) * ROWS)
            block = qkv_ref[b].astype(F32)
            q, k, v = (pad_rows(block[p * HD : (p + 1) * HD], 128) for p in range(3))
            q_rows[at, :] = q.T.astype(BF16)
            k_ref[at, :] = k.T.astype(BF16)
            v_rows[at, :] = v.T.astype(BF16)
            kt[:, at] = k.astype(BF16)
            vt_ref[:, at] = v.astype(BF16)
            qt_ref[:, at] = q[:80].astype(BF16)

    at = pl.multiple_of(pl.program_id(0) * BLOCK, BLOCK)
    scores = dot(q_rows[pl.ds(at, BLOCK), :], kt[...], 1, 0)
    top = jnp.max(scores, axis=-1, keepdims=True)
    factor = SCALE * math.log2(math.e)
    e = jnp.exp2((scores - top) * factor)
    low = e.astype(BF16)
    p_ref[...] = low
    part = 1.0 / jnp.sum(e, axis=-1, keepdims=True)
    mixed = dot(low, v_rows[...], 1, 0) * part
    lane = lax.broadcasted_iota(jnp.int32, (BLOCK, 128), 1)
    o_ref[...] = jnp.where(lane == 127, part, mixed)


def prepare_kernel(do_ref, rows_ref):
    for b in range(HEADS):
        at = slice(b * ROWS, (b + 1) * ROWS)
        block = pad_rows(do_ref[b].astype(F32), 128)
        rows_ref[at, :] = block.T.astype(BF16)


def spatial_kernel(
    do_ref, p_ref, o_ref, k_ref, qt_ref, vt_ref, out_ref, dq, dk, dv
):
    step = pl.program_id(0)

    @pl.when(step == 0)
    def _():
        dk[...] = jnp.zeros_like(dk)
        dv[...] = jnp.zeros_like(dv)

    at = pl.ds(pl.multiple_of(step * BLOCK, BLOCK), BLOCK)
    mixed = o_ref[...]
    wide = do_ref[...].astype(F32) * mixed[:, 127:]
    do = wide.astype(BF16)
    probs = p_ref[...]
    dp = dot(do, vt_ref[...], 1, 0)
    mid = jnp.sum(wide * mixed, axis=-1, keepdims=True)
    ds = (probs.astype(F32) * (dp - mid)).astype(BF16)
    dq[:, at] = (dot(ds, k_ref[...], 1, 0) * SCALE).T[:HD]
    dk[...] += dot(qt_ref[...], ds, 1, 0)
    dv[...] += dot(wide.T[:80].astype(BF16), probs, 1, 0)

    @pl.when(step == pl.num_programs(0) - 1)
    def _():
        for b in range(HEADS):
            at = slice(b * ROWS, (b + 1) * ROWS)
            parts = [dq[:, at], dk[:HD, at] * SCALE, dv[:HD, at]]
            out_ref[b] = jnp.concatenate(parts, axis=0).astype(BF16)


def home_kernel(in_ref, out_ref, proj_ref, work, pack):
    for h in range(HEADS):
        block = in_ref[h].astype(F32)
        extra = block[:RIDE]
        pack[...] = extra if h == 0 else pack[...] + extra
        for p in range(3):
            at = (p * HEADS + h) * HD
            work[at : at + HD, :] = block[RIDE + p * HD : RIDE + (p + 1) * HD]
    for t in range(3 * D // 128):
        at = slice(t * 128, (t + 1) * 128)
        out_ref[:, at] = work[at, :].T.astype(BF16)
    for i, wide in enumerate((128, 128, 32)):
        proj_ref[:, i * 128 : i * 128 + wide] = pack[i * 18 : (i + 1) * 18, :wide]


def around(x, axis, size, step):
    return lax.ppermute(x, axis, [(i, (i + step) % size) for i in range(size)])


def across(x, axis, size, flip):
    return lax.ppermute(x, axis, [(i, i ^ flip) for i in range(size)])


def per_device(spatial_qkv, spatial_out, resid, norm_gain, qkv_weight, out_weight, grad_out):
    every = ("dp", "xh", "core")
    heads = ("xl", "z")
    frame = ("xh", "core")
    line = ("xh", "xl")
    shape = jax.ShapeDtypeStruct
    resid = resid.reshape(ROWS, D)
    grad_out = grad_out.reshape(ROWS, D)
    qkv_rows = spatial_qkv.reshape(ROWS, 3 * D)
    out_rows = spatial_out.reshape(ROWS, D)
    gain = norm_gain.reshape(1, D)
    rows = CLIPS * ROWS
    width = 3 * GROUP * HD

    hbm = pl.BlockSpec(memory_space=pltpu.HBM)
    vmem_spec = pl.BlockSpec(memory_space=pltpu.VMEM)
    bf16 = lambda *dims: shape(dims, BF16)
    f32 = lambda *dims: pltpu.VMEM(dims, F32)
    near_by = lambda blocks: [
        b if o == 0 else around(b, "dp", CLIPS, o) for o, b in enumerate(blocks)
    ]
    over_frame = lambda blocks: [
        b if k == 0 else across(b, frame, FRAMES, k) for k, b in enumerate(blocks)
    ]

    mine, t_unit = call(
        unit_kernel,
        [bf16(CHUNK, 2 * D)] * FRAMES,
        (resid, gain, grad_out),
        LOW,
        scratch=[f32(ROWS, 2 * D)],
    )
    ours = over_frame(mine)
    (qkv_out,), t_qkv = call(
        qkv_kernel,
        [bf16(HEADS, 3 * HD, ROWS)],
        (qkv_rows,),
        LOW,
        scratch=[f32(3 * D, ROWS)],
        after=[t_unit],
    )
    qkv_in = lax.all_to_all(qkv_out, heads, 0, 0, tiled=True)
    w_blocks, t_weight = call(
        weight_kernel,
        [bf16(3 * HD, HALF)] * CLIPS,
        (qkv_weight.T,),
        LOW,
        scratch=[f32(width, D)],
        after=[t_qkv],
    )
    w_in = near_by(w_blocks)
    groups, t_group = call(
        group_kernel,
        [bf16(ROWS, D + GO_PAD)] * CLIPS,
        tuple(ours),
        LOW,
        scratch=[f32(D, ROWS)],
        after=[t_weight],
    )
    rows_in = near_by(groups)
    (w_half,), t_join = call(
        join_kernel,
        [bf16(width, HALF)],
        tuple(w_in),
        LOW,
        scratch=[f32(width, HALF)],
        after=[t_group],
    )
    w_other = across(w_half, "core", 2, 1)
    (up_out, unit_all, d_proj), t_temporal = call(
        temporal_kernel,
        [bf16(CLIPS, FRAMES, CHUNK, D), bf16(rows, D), bf16(rows, WIDE)],
        (*rows_in, w_half, w_other),
        LOW,
        scratch=[
            f32(width, rows),
            f32(GROUP * HD, rows),
            f32(width, rows),
            pltpu.VMEM((width, D), BF16),
        ],
    )
    up_out, qkv_in = lax.optimization_barrier((up_out, qkv_in))
    up_in = lax.all_to_all(
        up_out.reshape(16, CHUNK, D), every, 0, 0, tiled=True
    ).reshape(CLIPS, FRAMES, CHUNK, D)
    out_rows = lax.optimization_barrier((out_rows, *rows_in))[0]
    out_in = near_by([out_rows] * CLIPS)

    (keep, away), t_grad = call(
        qkv_grad_kernel,
        [bf16(2, 288, WIDE)] * 2,
        (unit_all, d_proj),
        LOW,
        scratch=[f32(D, WIDE)],
        after=[t_temporal],
    )
    came = across(away, "core", 2, 1)
    (near, far), t_split = call(
        z_split_kernel, [bf16(4, 72, WIDE)] * 2, (keep, came), LOW, after=[t_grad]
    )
    came = across(far, "z", 8, 4)

    whole = lambda *dims: pl.BlockSpec(dims, lambda i: (0,) * len(dims))
    by_row = lambda wide: pl.BlockSpec((BLOCK, wide), lambda i: (i, 0))
    (probs, mixed, keys, queries_t, values_t), t_probs = call(
        probs_kernel,
        [
            bf16(TOKENS, TOKENS),
            shape((TOKENS, 128), F32),
            bf16(TOKENS, 128),
            bf16(80, TOKENS),
            bf16(128, TOKENS),
        ],
        (qkv_in,),
        LOW,
        vmem=58,
        scratch=[
            pltpu.VMEM((TOKENS, 128), BF16),
            pltpu.VMEM((128, TOKENS), BF16),
            pltpu.VMEM((TOKENS, 128), BF16),
        ],
        grid=(TOKENS // BLOCK,),
        in_specs=[whole(HEADS, 3 * HD, ROWS)],
        out_specs=[
            by_row(TOKENS),
            by_row(128),
            whole(TOKENS, 128),
            whole(80, TOKENS),
            whole(128, TOKENS),
        ],
    )
    (stream, head_out), t_stream = call(
        stream_kernel,
        [bf16(ROWS, D), bf16(HEADS, HD, ROWS)],
        (up_in, resid, gain, out_weight),
        LOW,
        after=[t_probs],
        scratch=[pltpu.VMEM((D, D), BF16), pltpu.SemaphoreType.DMA],
        in_specs=[vmem_spec, vmem_spec, vmem_spec, hbm],
    )
    head_in = lax.all_to_all(head_out, heads, 0, 0, tiled=True)
    cols, t_cols = call(cols_kernel, [bf16(ROWS, GO_PAD)] * CLIPS, (stream,), LOW)
    cols = near_by(cols)
    (near, far), t_halve = call(
        z_halve_kernel, [bf16(4, 36, WIDE)] * 2, (near, came), LOW, after=[t_cols]
    )
    came = across(far, "z", 8, 1)
    (p_keep, p_away), t_proj = call(
        proj_grad_kernel,
        [bf16(2, 288, GO_PAD)] * 2,
        (*out_in, *cols),
        LOW,
        scratch=[
            f32(D, GO_PAD),
            pltpu.VMEM((rows, D), BF16),
            pltpu.SemaphoreType.DMA((CLIPS,)),
        ],
        after=[t_halve],
        in_specs=[hbm] * CLIPS + [vmem_spec] * CLIPS,
    )
    p_came = across(p_away, "core", 2, 1)

    (do_rows,), t_prepare = call(
        prepare_kernel,
        [bf16(TOKENS, 128)],
        (head_in,),
        LOW,
        after=[t_proj],
    )
    (p_near, p_far), t_pair = call(
        pair_kernel, [bf16(288, GO_PAD)] * 2, (p_keep, p_came), LOW, after=[t_prepare]
    )
    p_came = across(p_far, "xh", 2, 1)

    (near, far), t_halve = call(
        z_halve_kernel, [bf16(4, 18, WIDE)] * 2, (near, came), LOW, after=[t_pair]
    )
    came = across(far, "z", 8, 2)

    (d_out,), t_spatial = call(
        spatial_kernel,
        [bf16(HEADS, 3 * HD, ROWS)],
        (do_rows, probs, mixed, keys, queries_t, values_t),
        LOW,
        vmem=58,
        scratch=[
            f32(HD, TOKENS),
            f32(80, TOKENS),
            f32(80, TOKENS),
        ],
        grid=(TOKENS // BLOCK,),
        in_specs=[
            by_row(128),
            by_row(TOKENS),
            by_row(128),
            whole(TOKENS, 128),
            pl.BlockSpec((80, BLOCK), lambda i: (0, i)),
            whole(128, TOKENS),
        ],
        out_specs=[whole(HEADS, 3 * HD, ROWS)],
    )
    (near, far), t_line = call(
        xl_kernel, [bf16(2, 18, WIDE)] * 2, (near, came), LOW, after=[t_spatial]
    )
    came = across(far, "xl", 2, 1)
    (d_out,), t_pack = call(
        pack_kernel,
        [bf16(HEADS, RIDE + 3 * HD, ROWS)],
        (d_out, p_near, p_came),
        LOW,
        scratch=[f32(288, GO_PAD)],
        after=[t_line],
    )
    d_in = lax.all_to_all(d_out, heads, 0, 0, tiled=True)

    (near, far), t_far = call(
        pair_kernel, [bf16(18, WIDE)] * 2, (near, came), LOW, after=[t_pack]
    )
    came = across(far, "xh", 2, 1)
    slots, t_slot = call(slot_kernel, [shape((24, 256), F32)] * CLIPS, (near, came), LOW)
    slots = near_by(slots)
    (ordered,), t_order = call(
        order_kernel, [shape((CLIPS, 18, 3 * HD), F32)], tuple(slots), LOW
    )
    grad_qkv = (
        ordered.reshape(CLIPS, 18, 3, HD).transpose(1, 2, 0, 3).reshape(18, 3 * D // CLIPS)
    )
    (d_qkv, grad_proj), _ = call(
        home_kernel,
        [bf16(ROWS, 3 * D), shape((18, D // CLIPS), F32)],
        (d_in,),
        LOW,
        scratch=[f32(3 * D, ROWS), f32(RIDE, 128)],
    )
    return (
        d_qkv.reshape(1, 1, ROWS, 3 * D),
        stream.reshape(1, 1, ROWS, D),
        grad_qkv,
        grad_proj,
    )


def solution(mesh):
    fine = Mesh(mesh.devices.reshape(4, 2, 2, 2, 8), ("dp", "xh", "core", "xl", "z"))
    frame = ("xh", "core")
    head = ("xl", "z")
    rows = P("dp", frame, head, None)
    return jax.shard_map(
        per_device,
        mesh=fine,
        in_specs=(rows, rows, rows, P(), P(None, "dp"), P(), rows),
        out_specs=(rows, rows, P(frame + head, "dp"), P(frame + head, "dp")),
        check_vma=False,
    )
```

```python
import functools
import math

import jax
import jax.numpy as jnp
from jax import lax
from jax.experimental import pallas as pl
from jax.experimental.pallas import tpu as pltpu
from jax.sharding import Mesh, PartitionSpec as P

D = 1152
HEADS = 16
HD = 72
ROWS = 128
CLIPS = 4
FRAMES = 4
CHUNK = 32
GROUP = 4
GO_PAD = 384
WIDE = 896
HALF = 640
TOKENS = 2048
BLOCK = 256
STEP = 512
EPS = 1e-06
LOW = 0.001
EARLY = 0.001
TAIL = 18
RIDE = 56
SCALE = HD ** (-0.5)
F32 = jnp.float32
BF16 = jnp.bfloat16
MIB = 1 << 20


def dot(left, right, left_dim, right_dim):
    return lax.dot_general(
        left, right, (((left_dim,), (right_dim,)), ((), ())), preferred_element_type=F32
    )


def call(kernel, out_shape, args, us, scratch=(), vmem=40, after=(), hold=(), in_specs=None, out_specs=None, **kw):
    held, extra, made = len(args), len(after) + len(hold), len(out_shape)
    vmem_spec, any_spec, hbm_spec = (
        pl.BlockSpec(memory_space=m) for m in (pltpu.VMEM, pl.ANY, pltpu.HBM)
    )
    token = jax.ShapeDtypeStruct((8, 128), F32)

    def body(*refs):
        ins, rest = refs[:held], refs[held + extra :]
        kernel(*ins, *rest[:made], *rest[made + 1 :])

    *outs, done = pl.pallas_call(
        body,
        out_shape=[*out_shape, token],
        in_specs=[*(in_specs or [vmem_spec] * held), *[any_spec] * len(after), *[hbm_spec] * len(hold)],
        out_specs=[*(out_specs or [vmem_spec] * made), any_spec],
        scratch_shapes=list(scratch),
        cost_estimate=pl.CostEstimate(
            flops=int(us * 1.1e9), bytes_accessed=int(us * 1e6), transcendentals=0
        ),
        compiler_params=pltpu.CompilerParams(vmem_limit_bytes=vmem * MIB),
        **kw,
    )(*args, *after, *hold)
    return outs, done


def norm_rows(rows):
    centred = rows - jnp.mean(rows, axis=-1, keepdims=True)
    spread = jnp.mean(centred * centred, axis=-1, keepdims=True)
    inverse = lax.rsqrt(spread + EPS)
    return centred * inverse, inverse


def place(name):
    return lax.axis_index(name)


def frame_index():
    return place("xh") * 2 + place("core")


def x_index():
    return place("xh") * 2 + place("xl")


def unit_kernel(resid_ref, gain_ref, grad_ref, *outs):
    normed, _ = norm_rows(resid_ref[...].astype(F32))
    work = outs[-1]
    work[:, :D] = normed * gain_ref[...]
    work[:, D:] = grad_ref[...].astype(F32)
    f = frame_index()
    for k in range(FRAMES):
        at = pl.multiple_of((f ^ k) * CHUNK, CHUNK)
        outs[k][...] = work[pl.ds(at, CHUNK), :].astype(BF16)


def group_kernel(*refs):
    ins, outs, work = refs[:FRAMES], refs[FRAMES : FRAMES + CLIPS], refs[-1]
    for k in range(FRAMES):
        at = slice(k * CHUNK, (k + 1) * CHUNK)
        for o in range(CLIPS):
            outs[o][at, :D] = ins[k][:, :D]
    grad = jnp.concatenate([ins[k][:, D:] for k in range(FRAMES)], axis=0).astype(F32)
    for t in range(D // 128):
        at = slice(t * 128, (t + 1) * 128)
        work[at, :] = grad[:, at].T
    d = place("dp")
    gap = jnp.zeros((GO_PAD - GROUP * HD, ROWS), F32)
    for o in range(CLIPS):
        g = lax.rem(d + o, CLIPS)
        heads = [
            work[pl.ds(pl.multiple_of((4 * i + g) * HD, 8), HD), :] for i in range(GROUP)
        ]
        outs[o][:, D:] = jnp.concatenate([*heads, gap], axis=0).T.astype(BF16)


def weight_kernel(w_ref, *refs):
    outs, work = refs[:CLIPS], refs[-1]
    work[...] = w_ref[...].astype(F32)
    d = place("dp")
    lanes = pl.ds(pl.multiple_of(place("core") * (D - HALF), 128), HALF)
    for o in range(CLIPS):
        g = lax.rem(d + o, CLIPS)
        heads = [work[pl.ds(pl.multiple_of((4 * j + g) * HD, 8), HD), lanes] for j in range(3)]
        outs[o][...] = jnp.concatenate(heads, axis=0).astype(BF16)


def join_kernel(*refs):
    ins, out_ref, work = refs[:CLIPS], refs[CLIPS], refs[-1]
    d = place("dp")
    for o in range(CLIPS):
        s = lax.rem(d + CLIPS - o, CLIPS)
        work[pl.ds(pl.multiple_of(s * 3 * HD, 8), 3 * HD), :] = ins[o][...].astype(F32)
    out_ref[...] = work[...].astype(BF16)


def qkv_kernel(qkv_ref, out_ref, work):
    for t in range(3 * D // 128):
        work[t * 128 : (t + 1) * 128, :] = qkv_ref[:, t * 128 : (t + 1) * 128].astype(F32).T
    for h in range(HEADS):
        parts = [work[(p * HEADS + h) * HD : (p * HEADS + h + 1) * HD, :] for p in range(3)]
        out_ref[h] = jnp.concatenate(parts, axis=0).astype(BF16)


def temporal_kernel(*refs):
    rows_in, halves = refs[:CLIPS], refs[CLIPS : CLIPS + 2]
    up_ref, all_ref, dproj_ref, proj, grad, dproj, w_ref = refs[CLIPS + 2 :]
    d, frame = place("dp"), frame_index()
    for core in range(2):

        @pl.when(place("core") == core)
        def _():
            w_ref[:, :HALF] = halves[core][...]
            w_ref[:, D - HALF :] = halves[1 - core][...]

    for k in range(FRAMES):
        at = slice(k * CHUNK, (k + 1) * CHUNK)
        for o in range(CLIPS):
            to = (k * CLIPS + o) * CHUNK
            all_ref[to : to + CHUNK, :] = rows_in[o][at, :D]
        rows = jnp.concatenate([rows_in[o][at, D:] for o in range(CLIPS)], axis=0).astype(F32)
        grad[:, k * ROWS : (k + 1) * ROWS] = rows.T[: GROUP * HD]
    proj[...] = dot(w_ref[...], all_ref[...], 1, 1).astype(BF16).astype(F32)

    def one_head(n, carry):
        def load(ref, base):
            at = pl.ds(pl.multiple_of(base + n * HD, 8), HD)
            return [ref[at, f * ROWS : (f + 1) * ROWS] for f in range(FRAMES)]

        q, k, v = (load(proj, p * GROUP * HD) for p in range(3))
        g = load(grad, 0)

        def total(a, b):
            return jnp.sum(a * b, axis=0, keepdims=True)

        span = range(FRAMES)
        ds, p_low = [], []
        for f in span:
            s = [total(q[f], k[j]) * SCALE for j in span]
            top = functools.reduce(jnp.maximum, s)
            e = [jnp.exp(x - top) for x in s]
            below = functools.reduce(jnp.add, e)
            prob = [x / below for x in e]
            dp = [total(g[f], v[j]) for j in span]
            mid = functools.reduce(jnp.add, [x * y for x, y in zip(prob, dp)])
            ds.append([(x * (y - mid)).astype(BF16).astype(F32) for x, y in zip(prob, dp)])
            p_low.append([x.astype(BF16).astype(F32) for x in prob])

        def put(base, f, value):
            at = pl.ds(pl.multiple_of(base + n * HD, 8), HD)
            dproj[at, f * ROWS : (f + 1) * ROWS] = value

        def mix(weights, values):
            return functools.reduce(jnp.add, [w * x for w, x in zip(weights, values)])

        for f in span:
            put(0, f, mix(ds[f], k) * SCALE)
            put(GROUP * HD, f, mix([ds[j][f] for j in span], q) * SCALE)
            put(2 * GROUP * HD, f, mix([p_low[j][f] for j in span], g))
        return carry

    lax.fori_loop(0, GROUP, one_head, 0)
    width = 3 * GROUP * HD
    gap = jnp.zeros((WIDE - width, CLIPS * ROWS), F32)
    low = jnp.concatenate([dproj[...], gap], axis=0).T.astype(BF16)
    dproj_ref[...] = low
    up = dot(low[:, :width], w_ref[...], 1, 0).astype(BF16)
    for k in range(FRAMES):
        for o in range(CLIPS):
            at = (k * CLIPS + o) * CHUNK
            up_ref[lax.rem(d + CLIPS - o, CLIPS), frame ^ k] = up[at : at + CHUNK]


def stream_kernel(up_ref, resid_ref, gain_ref, w_hbm, stream_ref, head_ref, w_ref, sem):
    copy = pltpu.make_async_copy(w_hbm, w_ref, sem)
    copy.start()
    parts = []
    for f in range(FRAMES):
        parts.append(functools.reduce(jnp.add, [up_ref[g, f].astype(F32) for g in range(CLIPS)]))
    up = jnp.concatenate(parts, axis=0)
    normed, inverse = norm_rows(resid_ref[...].astype(F32))
    scaled = up * gain_ref[...]
    mean_up = jnp.mean(scaled, axis=-1, keepdims=True)
    mean_cross = jnp.mean(scaled * normed, axis=-1, keepdims=True)
    stream = (inverse * (scaled - mean_up - normed * mean_cross)).astype(BF16)
    stream_ref[...] = stream
    copy.wait()
    spatial = dot(w_ref[...], stream, 1, 1)
    for h in range(HEADS):
        head_ref[h] = spatial[h * HD : (h + 1) * HD].astype(BF16)


def cols_kernel(stream_ref, *cols):
    wide = stream_ref[...].astype(F32)
    d = place("dp")
    for o in range(CLIPS):
        g = lax.rem(d + o, CLIPS)
        turned = pltpu.roll(wide, lax.rem(D - (D // CLIPS) * g, D), 1)
        cols[o][...] = turned[:, :GO_PAD].astype(BF16)


def split_core(total, keep_ref, away_ref):
    core = place("core")
    for xh in range(2):
        for ref, which in ((keep_ref, core), (away_ref, 1 - core)):
            at = pl.multiple_of((xh * 2 + which) * 288, 8)
            ref[xh] = total[pl.ds(at, 288), :].astype(BF16)


def qkv_grad_kernel(unit_ref, dproj_ref, keep_ref, away_ref, total):
    total[...] = dot(unit_ref[...].astype(F32).T.astype(BF16), dproj_ref[...], 1, 0)
    split_core(total, keep_ref, away_ref)


def proj_grad_kernel(*refs):
    outs, cols, (keep_ref, away_ref, total, rows, sems) = refs[:CLIPS], refs[CLIPS : 2 * CLIPS], refs[-5:]
    copies = [
        pltpu.make_async_copy(ref, rows.at[pl.ds(o * ROWS, ROWS)], sems.at[o])
        for o, ref in enumerate(outs)
    ]
    for copy in copies:
        copy.start()
    columns = jnp.concatenate([c[...] for c in cols], axis=0)
    for copy in copies:
        copy.wait()
    total[...] = dot(rows[...].astype(F32).T.astype(BF16), columns, 1, 0)
    split_core(total, keep_ref, away_ref)


def z_split_kernel(keep_ref, came_ref, near_ref, far_ref):
    half = place("z") // 4
    for xh in range(2):
        for xl in range(2):
            for ref, which in ((near_ref, half), (far_ref, 1 - half)):
                at = pl.ds(pl.multiple_of(xl * 144 + which * 72, 8), 72)
                both = keep_ref[xh, at, :].astype(F32) + came_ref[xh, at, :].astype(F32)
                ref[xh * 2 + xl] = both.astype(BF16)


def z_halve_kernel(keep_ref, came_ref, near_ref, far_ref):
    first = near_ref.shape[1] == 36
    high = lax.rem(place("z") // (1 if first else 2), 2) == 1
    for b in range(4):
        both = keep_ref[b].astype(F32) + came_ref[b].astype(F32)
        if first:
            upper = jnp.concatenate([both[18:36], both[54:]], axis=0)
            lower = jnp.concatenate([both[:18], both[36:54]], axis=0)
        else:
            upper, lower = both[18:], both[:18]
        near_ref[b] = jnp.where(high, upper, lower).astype(BF16)
        far_ref[b] = jnp.where(high, lower, upper).astype(BF16)


def xl_kernel(keep_ref, came_ref, near_ref, far_ref):
    xl = place("xl")
    for xh in range(2):
        for ref, which in ((near_ref, xl), (far_ref, 1 - xl)):
            at = xh * 2 + which
            ref[xh] = (keep_ref[at].astype(F32) + came_ref[at].astype(F32)).astype(BF16)


def pair_kernel(keep_ref, came_ref, near_ref, far_ref):
    xh = place("xh")
    for ref, which in ((near_ref, xh), (far_ref, 1 - xh)):
        ref[...] = (keep_ref[which].astype(F32) + came_ref[which].astype(F32)).astype(BF16)


def slot_kernel(keep_ref, came_ref, *outs):
    total = keep_ref[...].astype(F32) + came_ref[...].astype(F32)
    wide = jnp.concatenate([total, jnp.zeros((18, 128), F32)], axis=1)
    wide = jnp.concatenate([wide, jnp.zeros((6, WIDE + 128), F32)], axis=0)
    d = place("dp")
    for o in range(CLIPS):
        g = lax.rem(d + o, CLIPS)
        turned = pltpu.roll(wide, lax.rem(WIDE + 128 - 3 * HD * g, WIDE + 128), 1)
        outs[o][...] = turned[:, :256]


def order_kernel(*refs):
    slots, out_ref = refs[:CLIPS], refs[CLIPS]
    d = place("dp")
    for o in range(CLIPS):
        out_ref[lax.rem(d + CLIPS - o, CLIPS)] = slots[o][:18, : 3 * HD]


def pack_kernel(d_ref, near_ref, far_ref, out_ref, total):
    total[...] = near_ref[...].astype(F32) + far_ref[...].astype(F32)
    rest = jnp.zeros((RIDE - 54, 128), F32)
    for b in range(HEADS):
        at = slice(b * 18, (b + 1) * 18)
        parts = [total[at, i * 128 : (i + 1) * 128] for i in range(3)]
        block = [*parts, rest, d_ref[b].astype(F32)]
        out_ref[b] = jnp.concatenate(block, axis=0).astype(BF16)


def pad_rows(x, rows):
    return jnp.concatenate([x, jnp.zeros((rows - x.shape[0], x.shape[1]), x.dtype)], axis=0)


def probs_kernel(qkv_ref, p_ref, o_ref, k_ref, qt_ref, vt_ref, q_rows, kt, v_rows):
    @pl.when(pl.program_id(0) == 0)
    def _():
        for b in range(HEADS):
            at = slice(b * ROWS, (b + 1) * ROWS)
            block = qkv_ref[b].astype(F32)
            q, k, v = (pad_rows(block[p * HD : (p + 1) * HD], 128) for p in range(3))
            q_rows[at, :] = q.T.astype(BF16)
            k_ref[at, :] = k.T.astype(BF16)
            v_rows[at, :] = v.T.astype(BF16)
            kt[:, at] = k.astype(BF16)
            vt_ref[:, at] = v.astype(BF16)
            qt_ref[:, at] = q[:80].astype(BF16)

    at = pl.multiple_of(pl.program_id(0) * BLOCK, BLOCK)
    scores = dot(q_rows[pl.ds(at, BLOCK), :], kt[...], 1, 0)
    top = jnp.max(scores, axis=-1, keepdims=True)
    factor = SCALE * math.log2(math.e)
    e = jnp.exp2((scores - top) * factor)
    low = e.astype(BF16)
    p_ref[...] = low
    part = 1.0 / jnp.sum(e, axis=-1, keepdims=True)
    mixed = dot(low, v_rows[...], 1, 0) * part
    lane = lax.broadcasted_iota(jnp.int32, (BLOCK, 128), 1)
    o_ref[...] = jnp.where(lane == 127, part, mixed)


def prepare_kernel(do_ref, rows_ref):
    for b in range(HEADS):
        at = slice(b * ROWS, (b + 1) * ROWS)
        block = pad_rows(do_ref[b].astype(F32), 128)
        rows_ref[at, :] = block.T.astype(BF16)


def spatial_kernel(
    do_ref, p_ref, o_ref, k_ref, qt_ref, vt_ref, out_ref, dq, dk, dv
):
    step = pl.program_id(0)

    @pl.when(step == 0)
    def _():
        dk[...] = jnp.zeros_like(dk)
        dv[...] = jnp.zeros_like(dv)

    at = pl.ds(pl.multiple_of(step * STEP, STEP), STEP)
    mixed = o_ref[...]
    wide = do_ref[...].astype(F32) * mixed[:, 127:]
    do = wide.astype(BF16)
    probs = p_ref[...]
    dp = dot(do, vt_ref[...], 1, 0)
    mid = jnp.sum(wide * mixed, axis=-1, keepdims=True)
    ds = (probs.astype(F32) * (dp - mid)).astype(BF16)
    dq[:, at] = (dot(ds, k_ref[...], 1, 0) * SCALE).T[:HD]
    dk[...] += dot(qt_ref[...], ds, 1, 0)
    dv[...] += dot(wide.T[:80].astype(BF16), probs, 1, 0)

    @pl.when(step == pl.num_programs(0) - 1)
    def _():
        for b in range(HEADS):
            at = slice(b * ROWS, (b + 1) * ROWS)
            parts = [dq[:, at], dk[:HD, at] * SCALE, dv[:HD, at]]
            out_ref[b] = jnp.concatenate(parts, axis=0).astype(BF16)


def home_kernel(in_ref, out_ref, proj_ref, work, pack):
    for h in range(HEADS):
        block = in_ref[h].astype(F32)
        extra = block[:RIDE]
        pack[...] = extra if h == 0 else pack[...] + extra
        for p in range(3):
            at = (p * HEADS + h) * HD
            work[at : at + HD, :] = block[RIDE + p * HD : RIDE + (p + 1) * HD]
    for t in range(3 * D // 128):
        at = slice(t * 128, (t + 1) * 128)
        out_ref[:, at] = work[at, :].T.astype(BF16)
    for i, wide in enumerate((128, 128, 32)):
        proj_ref[:, i * 128 : i * 128 + wide] = pack[i * 18 : (i + 1) * 18, :wide]


def around(x, axis, size, step):
    return lax.ppermute(x, axis, [(i, (i + step) % size) for i in range(size)])


def across(x, axis, size, flip):
    return lax.ppermute(x, axis, [(i, i ^ flip) for i in range(size)])


def per_device(spatial_qkv, spatial_out, resid, norm_gain, qkv_weight, out_weight, grad_out):
    every = ("dp", "xh", "core")
    heads = ("xl", "z")
    frame = ("xh", "core")
    line = ("xh", "xl")
    shape = jax.ShapeDtypeStruct
    resid = resid.reshape(ROWS, D)
    grad_out = grad_out.reshape(ROWS, D)
    qkv_rows = spatial_qkv.reshape(ROWS, 3 * D)
    out_rows = spatial_out.reshape(ROWS, D)
    gain = norm_gain.reshape(1, D)
    rows = CLIPS * ROWS
    width = 3 * GROUP * HD

    hbm = pl.BlockSpec(memory_space=pltpu.HBM)
    vmem_spec = pl.BlockSpec(memory_space=pltpu.VMEM)
    bf16 = lambda *dims: shape(dims, BF16)
    f32 = lambda *dims: pltpu.VMEM(dims, F32)
    near_by = lambda blocks: [
        b if o == 0 else around(b, "dp", CLIPS, o) for o, b in enumerate(blocks)
    ]
    over_frame = lambda blocks: [
        b if k == 0 else across(b, frame, FRAMES, k) for k, b in enumerate(blocks)
    ]

    mine, t_unit = call(
        unit_kernel,
        [bf16(CHUNK, 2 * D)] * FRAMES,
        (resid, gain, grad_out),
        LOW,
        scratch=[f32(ROWS, 2 * D)],
    )
    ours = over_frame(mine)
    (qkv_out,), t_qkv = call(
        qkv_kernel,
        [bf16(HEADS, 3 * HD, ROWS)],
        (qkv_rows,),
        LOW,
        scratch=[f32(3 * D, ROWS)],
        after=[t_unit],
    )
    qkv_in = lax.all_to_all(qkv_out, heads, 0, 0, tiled=True)
    w_blocks, t_weight = call(
        weight_kernel,
        [bf16(3 * HD, HALF)] * CLIPS,
        (qkv_weight.T,),
        LOW,
        scratch=[f32(width, D)],
        after=[t_qkv],
    )
    w_in = near_by(w_blocks)
    groups, t_group = call(
        group_kernel,
        [bf16(ROWS, D + GO_PAD)] * CLIPS,
        tuple(ours),
        LOW,
        scratch=[f32(D, ROWS)],
        after=[t_weight],
    )
    rows_in = near_by(groups)
    (w_half,), t_join = call(
        join_kernel,
        [bf16(width, HALF)],
        tuple(w_in),
        LOW,
        scratch=[f32(width, HALF)],
        after=[t_group],
    )
    w_other = across(w_half, "core", 2, 1)
    (up_out, unit_all, d_proj), t_temporal = call(
        temporal_kernel,
        [bf16(CLIPS, FRAMES, CHUNK, D), bf16(rows, D), bf16(rows, WIDE)],
        (*rows_in, w_half, w_other),
        EARLY,
        scratch=[
            f32(width, rows),
            f32(GROUP * HD, rows),
            f32(width, rows),
            pltpu.VMEM((width, D), BF16),
        ],
    )
    up_out, qkv_in = lax.optimization_barrier((up_out, qkv_in))
    up_in = lax.all_to_all(
        up_out.reshape(16, CHUNK, D), every, 0, 0, tiled=True
    ).reshape(CLIPS, FRAMES, CHUNK, D)
    out_rows = lax.optimization_barrier((out_rows, *rows_in))[0]
    out_in = near_by([out_rows] * CLIPS)

    (keep, away), t_grad = call(
        qkv_grad_kernel,
        [bf16(2, 288, WIDE)] * 2,
        (unit_all, d_proj),
        LOW,
        scratch=[f32(D, WIDE)],
        after=[t_temporal],
    )
    came = across(away, "core", 2, 1)
    (near, far), t_split = call(
        z_split_kernel, [bf16(4, 72, WIDE)] * 2, (keep, came), LOW, after=[t_grad]
    )
    came = across(far, "z", 8, 4)

    whole = lambda *dims: pl.BlockSpec(dims, lambda i: (0,) * len(dims))
    by_row = lambda wide: pl.BlockSpec((BLOCK, wide), lambda i: (i, 0))
    (probs, mixed, keys, queries_t, values_t), t_probs = call(
        probs_kernel,
        [
            bf16(TOKENS, TOKENS),
            shape((TOKENS, 128), F32),
            bf16(TOKENS, 128),
            bf16(80, TOKENS),
            bf16(128, TOKENS),
        ],
        (qkv_in,),
        LOW,
        vmem=53,
        scratch=[
            pltpu.VMEM((TOKENS, 128), BF16),
            pltpu.VMEM((128, TOKENS), BF16),
            pltpu.VMEM((TOKENS, 128), BF16),
        ],
        grid=(TOKENS // BLOCK,),
        in_specs=[whole(HEADS, 3 * HD, ROWS)],
        out_specs=[
            by_row(TOKENS),
            by_row(128),
            whole(TOKENS, 128),
            whole(80, TOKENS),
            whole(128, TOKENS),
        ],
    )
    (stream, head_out), t_stream = call(
        stream_kernel,
        [bf16(ROWS, D), bf16(HEADS, HD, ROWS)],
        (up_in, resid, gain, out_weight),
        LOW,
        after=[t_probs],
        scratch=[pltpu.VMEM((D, D), BF16), pltpu.SemaphoreType.DMA],
        in_specs=[vmem_spec, vmem_spec, vmem_spec, hbm],
    )
    head_in = lax.all_to_all(head_out, heads, 0, 0, tiled=True)
    cols, t_cols = call(cols_kernel, [bf16(ROWS, GO_PAD)] * CLIPS, (stream,), LOW)
    cols = near_by(cols)
    (near, far), t_halve = call(
        z_halve_kernel, [bf16(4, 36, WIDE)] * 2, (near, came), LOW, after=[t_cols]
    )
    came = across(far, "z", 8, 1)
    (p_keep, p_away), t_proj = call(
        proj_grad_kernel,
        [bf16(2, 288, GO_PAD)] * 2,
        (*out_in, *cols),
        LOW,
        scratch=[
            f32(D, GO_PAD),
            pltpu.VMEM((rows, D), BF16),
            pltpu.SemaphoreType.DMA((CLIPS,)),
        ],
        after=[t_halve],
        in_specs=[hbm] * CLIPS + [vmem_spec] * CLIPS,
    )
    p_came = across(p_away, "core", 2, 1)

    (do_rows,), t_prepare = call(
        prepare_kernel,
        [bf16(TOKENS, 128)],
        (head_in,),
        LOW,
        after=[t_proj],
    )
    (p_near, p_far), t_pair = call(
        pair_kernel, [bf16(288, GO_PAD)] * 2, (p_keep, p_came), LOW, after=[t_prepare]
    )
    p_came = across(p_far, "xh", 2, 1)

    by_step = lambda wide: pl.BlockSpec((STEP, wide), lambda i: (i, 0))
    (d_out,), t_spatial = call(
        spatial_kernel,
        [bf16(HEADS, 3 * HD, ROWS)],
        (do_rows, probs, mixed, keys, queries_t, values_t),
        LOW,
        vmem=53,
        scratch=[
            f32(HD, TOKENS),
            f32(80, TOKENS),
            f32(80, TOKENS),
        ],
        grid=(TOKENS // STEP,),
        in_specs=[
            by_step(128),
            by_step(TOKENS),
            by_step(128),
            whole(TOKENS, 128),
            pl.BlockSpec((80, STEP), lambda i: (0, i)),
            whole(128, TOKENS),
        ],
        out_specs=[whole(HEADS, 3 * HD, ROWS)],
    )
    (near, far), t_halve = call(
        z_halve_kernel, [bf16(4, 18, WIDE)] * 2, (near, came), LOW, after=[t_spatial]
    )
    came = across(far, "z", 8, 2)

    (d_out,), t_pack = call(
        pack_kernel,
        [bf16(HEADS, RIDE + 3 * HD, ROWS)],
        (d_out, p_near, p_came),
        LOW,
        scratch=[f32(288, GO_PAD)],
        after=[t_halve],
    )
    d_in = lax.all_to_all(d_out, heads, 0, 0, tiled=True)

    (near, far), t_line = call(
        xl_kernel, [bf16(2, 18, WIDE)] * 2, (near, came), LOW, after=[t_pack]
    )
    came = across(far, "xl", 2, 1)
    (near, far), t_far = call(
        pair_kernel, [bf16(18, WIDE)] * 2, (near, came), LOW, after=[t_line]
    )
    came = across(far, "xh", 2, 1)
    slots, t_slot = call(slot_kernel, [shape((24, 256), F32)] * CLIPS, (near, came), TAIL)
    slots = near_by(slots)
    (ordered,), t_order = call(
        order_kernel, [shape((CLIPS, 18, 3 * HD), F32)], tuple(slots), LOW
    )
    grad_qkv = (
        ordered.reshape(CLIPS, 18, 3, HD).transpose(1, 2, 0, 3).reshape(18, 3 * D // CLIPS)
    )
    (d_qkv, grad_proj), _ = call(
        home_kernel,
        [bf16(ROWS, 3 * D), shape((18, D // CLIPS), F32)],
        (d_in,),
        LOW,
        scratch=[f32(3 * D, ROWS), f32(RIDE, 128)],
    )
    return (
        d_qkv.reshape(1, 1, ROWS, 3 * D),
        stream.reshape(1, 1, ROWS, D),
        grad_qkv,
        grad_proj,
    )


def solution(mesh):
    fine = Mesh(mesh.devices.reshape(4, 2, 2, 2, 8), ("dp", "xh", "core", "xl", "z"))
    frame = ("xh", "core")
    head = ("xl", "z")
    rows = P("dp", frame, head, None)
    return jax.shard_map(
        per_device,
        mesh=fine,
        in_specs=(rows, rows, rows, P(), P(None, "dp"), P(), rows),
        out_specs=(rows, rows, P(frame + head, "dp"), P(frame + head, "dp")),
        check_vma=False,
    )
```

```python
import functools
import math

import jax
import jax.numpy as jnp
from jax import lax
from jax.experimental import pallas as pl
from jax.experimental.pallas import tpu as pltpu
from jax.sharding import Mesh, PartitionSpec as P

D = 1152
HEADS = 16
HD = 72
ROWS = 128
CLIPS = 4
FRAMES = 4
CHUNK = 32
GROUP = 4
GO_PAD = 384
WIDE = 896
HALF = 640
TOKENS = 2048
BLOCK = 512
PART = 256
STEP = 512
EPS = 1e-06
LOW = 0.001
EARLY = 0.001
TAIL = 18
RIDE = 56
SCALE = HD ** (-0.5)
F32 = jnp.float32
BF16 = jnp.bfloat16
MIB = 1 << 20


def dot(left, right, left_dim, right_dim):
    return lax.dot_general(
        left, right, (((left_dim,), (right_dim,)), ((), ())), preferred_element_type=F32
    )


def call(kernel, out_shape, args, us, scratch=(), vmem=40, after=(), hold=(), in_specs=None, out_specs=None, **kw):
    held, extra, made = len(args), len(after) + len(hold), len(out_shape)
    vmem_spec, any_spec, hbm_spec = (
        pl.BlockSpec(memory_space=m) for m in (pltpu.VMEM, pl.ANY, pltpu.HBM)
    )
    token = jax.ShapeDtypeStruct((8, 128), F32)

    def body(*refs):
        ins, rest = refs[:held], refs[held + extra :]
        kernel(*ins, *rest[:made], *rest[made + 1 :])

    *outs, done = pl.pallas_call(
        body,
        out_shape=[*out_shape, token],
        in_specs=[*(in_specs or [vmem_spec] * held), *[any_spec] * len(after), *[hbm_spec] * len(hold)],
        out_specs=[*(out_specs or [vmem_spec] * made), any_spec],
        scratch_shapes=list(scratch),
        cost_estimate=pl.CostEstimate(
            flops=int(us * 1.1e9), bytes_accessed=int(us * 1e6), transcendentals=0
        ),
        compiler_params=pltpu.CompilerParams(vmem_limit_bytes=vmem * MIB),
        **kw,
    )(*args, *after, *hold)
    return outs, done


def norm_rows(rows):
    centred = rows - jnp.mean(rows, axis=-1, keepdims=True)
    spread = jnp.mean(centred * centred, axis=-1, keepdims=True)
    inverse = lax.rsqrt(spread + EPS)
    return centred * inverse, inverse


def place(name):
    return lax.axis_index(name)


def frame_index():
    return place("xh") * 2 + place("core")


def x_index():
    return place("xh") * 2 + place("xl")


def unit_kernel(resid_ref, gain_ref, grad_ref, *outs):
    normed, _ = norm_rows(resid_ref[...].astype(F32))
    work = outs[-1]
    work[:, :D] = normed * gain_ref[...]
    work[:, D:] = grad_ref[...].astype(F32)
    f = frame_index()
    for k in range(FRAMES):
        at = pl.multiple_of((f ^ k) * CHUNK, CHUNK)
        outs[k][...] = work[pl.ds(at, CHUNK), :].astype(BF16)


def group_kernel(*refs):
    ins, outs, work = refs[:FRAMES], refs[FRAMES : FRAMES + CLIPS], refs[-1]
    for k in range(FRAMES):
        at = slice(k * CHUNK, (k + 1) * CHUNK)
        for o in range(CLIPS):
            outs[o][at, :D] = ins[k][:, :D]
    grad = jnp.concatenate([ins[k][:, D:] for k in range(FRAMES)], axis=0).astype(F32)
    for t in range(D // 128):
        at = slice(t * 128, (t + 1) * 128)
        work[at, :] = grad[:, at].T
    d = place("dp")
    gap = jnp.zeros((GO_PAD - GROUP * HD, ROWS), F32)
    for o in range(CLIPS):
        g = lax.rem(d + o, CLIPS)
        heads = [
            work[pl.ds(pl.multiple_of((4 * i + g) * HD, 8), HD), :] for i in range(GROUP)
        ]
        outs[o][:, D:] = jnp.concatenate([*heads, gap], axis=0).T.astype(BF16)


def weight_kernel(w_ref, *refs):
    outs, work = refs[:CLIPS], refs[-1]
    work[...] = w_ref[...].astype(F32)
    d = place("dp")
    lanes = pl.ds(pl.multiple_of(place("core") * (D - HALF), 128), HALF)
    for o in range(CLIPS):
        g = lax.rem(d + o, CLIPS)
        heads = [work[pl.ds(pl.multiple_of((4 * j + g) * HD, 8), HD), lanes] for j in range(3)]
        outs[o][...] = jnp.concatenate(heads, axis=0).astype(BF16)


def join_kernel(*refs):
    ins, out_ref, work = refs[:CLIPS], refs[CLIPS], refs[-1]
    d = place("dp")
    for o in range(CLIPS):
        s = lax.rem(d + CLIPS - o, CLIPS)
        work[pl.ds(pl.multiple_of(s * 3 * HD, 8), 3 * HD), :] = ins[o][...].astype(F32)
    out_ref[...] = work[...].astype(BF16)


def qkv_kernel(qkv_ref, out_ref, work):
    for t in range(3 * D // 128):
        work[t * 128 : (t + 1) * 128, :] = qkv_ref[:, t * 128 : (t + 1) * 128].astype(F32).T
    for h in range(HEADS):
        parts = [work[(p * HEADS + h) * HD : (p * HEADS + h + 1) * HD, :] for p in range(3)]
        out_ref[h] = jnp.concatenate(parts, axis=0).astype(BF16)


def temporal_kernel(*refs):
    rows_in, halves = refs[:CLIPS], refs[CLIPS : CLIPS + 2]
    up_ref, all_ref, dproj_ref, proj, grad, dproj, w_ref = refs[CLIPS + 2 :]
    d, frame = place("dp"), frame_index()
    for core in range(2):

        @pl.when(place("core") == core)
        def _():
            w_ref[:, :HALF] = halves[core][...]
            w_ref[:, D - HALF :] = halves[1 - core][...]

    for k in range(FRAMES):
        at = slice(k * CHUNK, (k + 1) * CHUNK)
        for o in range(CLIPS):
            to = (k * CLIPS + o) * CHUNK
            all_ref[to : to + CHUNK, :] = rows_in[o][at, :D]
        rows = jnp.concatenate([rows_in[o][at, D:] for o in range(CLIPS)], axis=0).astype(F32)
        grad[:, k * ROWS : (k + 1) * ROWS] = rows.T[: GROUP * HD]
    proj[...] = dot(w_ref[...], all_ref[...], 1, 1).astype(BF16).astype(F32)

    def one_head(n, carry):
        def load(ref, base):
            at = pl.ds(pl.multiple_of(base + n * HD, 8), HD)
            return [ref[at, f * ROWS : (f + 1) * ROWS] for f in range(FRAMES)]

        q, k, v = (load(proj, p * GROUP * HD) for p in range(3))
        g = load(grad, 0)

        def total(a, b):
            return jnp.sum(a * b, axis=0, keepdims=True)

        span = range(FRAMES)
        ds, p_low = [], []
        for f in span:
            s = [total(q[f], k[j]) * SCALE for j in span]
            top = functools.reduce(jnp.maximum, s)
            e = [jnp.exp(x - top) for x in s]
            below = functools.reduce(jnp.add, e)
            prob = [x / below for x in e]
            dp = [total(g[f], v[j]) for j in span]
            mid = functools.reduce(jnp.add, [x * y for x, y in zip(prob, dp)])
            ds.append([(x * (y - mid)).astype(BF16).astype(F32) for x, y in zip(prob, dp)])
            p_low.append([x.astype(BF16).astype(F32) for x in prob])

        def put(base, f, value):
            at = pl.ds(pl.multiple_of(base + n * HD, 8), HD)
            dproj[at, f * ROWS : (f + 1) * ROWS] = value

        def mix(weights, values):
            return functools.reduce(jnp.add, [w * x for w, x in zip(weights, values)])

        for f in span:
            put(0, f, mix(ds[f], k) * SCALE)
            put(GROUP * HD, f, mix([ds[j][f] for j in span], q) * SCALE)
            put(2 * GROUP * HD, f, mix([p_low[j][f] for j in span], g))
        return carry

    lax.fori_loop(0, GROUP, one_head, 0)
    width = 3 * GROUP * HD
    gap = jnp.zeros((WIDE - width, CLIPS * ROWS), F32)
    low = jnp.concatenate([dproj[...], gap], axis=0).T.astype(BF16)
    dproj_ref[...] = low
    up = dot(low[:, :width], w_ref[...], 1, 0).astype(BF16)
    for k in range(FRAMES):
        for o in range(CLIPS):
            at = (k * CLIPS + o) * CHUNK
            up_ref[lax.rem(d + CLIPS - o, CLIPS), frame ^ k] = up[at : at + CHUNK]


def stream_kernel(up_ref, resid_ref, gain_ref, w_hbm, stream_ref, head_ref, w_ref, sem):
    copy = pltpu.make_async_copy(w_hbm, w_ref, sem)
    copy.start()
    parts = []
    for f in range(FRAMES):
        parts.append(functools.reduce(jnp.add, [up_ref[g, f].astype(F32) for g in range(CLIPS)]))
    up = jnp.concatenate(parts, axis=0)
    normed, inverse = norm_rows(resid_ref[...].astype(F32))
    scaled = up * gain_ref[...]
    mean_up = jnp.mean(scaled, axis=-1, keepdims=True)
    mean_cross = jnp.mean(scaled * normed, axis=-1, keepdims=True)
    stream = (inverse * (scaled - mean_up - normed * mean_cross)).astype(BF16)
    stream_ref[...] = stream
    copy.wait()
    spatial = dot(w_ref[...], stream, 1, 1)
    for h in range(HEADS):
        head_ref[h] = spatial[h * HD : (h + 1) * HD].astype(BF16)


def cols_kernel(stream_ref, *cols):
    wide = stream_ref[...].astype(F32)
    d = place("dp")
    for o in range(CLIPS):
        g = lax.rem(d + o, CLIPS)
        turned = pltpu.roll(wide, lax.rem(D - (D // CLIPS) * g, D), 1)
        cols[o][...] = turned[:, :GO_PAD].astype(BF16)


def split_core(total, keep_ref, away_ref):
    core = place("core")
    for xh in range(2):
        for ref, which in ((keep_ref, core), (away_ref, 1 - core)):
            at = pl.multiple_of((xh * 2 + which) * 288, 8)
            ref[xh] = total[pl.ds(at, 288), :].astype(BF16)


def qkv_grad_kernel(unit_ref, dproj_ref, keep_ref, away_ref, total):
    total[...] = dot(unit_ref[...].astype(F32).T.astype(BF16), dproj_ref[...], 1, 0)
    split_core(total, keep_ref, away_ref)


def proj_grad_kernel(*refs):
    outs, cols, (keep_ref, away_ref, total, rows, sems) = refs[:CLIPS], refs[CLIPS : 2 * CLIPS], refs[-5:]
    copies = [
        pltpu.make_async_copy(ref, rows.at[pl.ds(o * ROWS, ROWS)], sems.at[o])
        for o, ref in enumerate(outs)
    ]
    for copy in copies:
        copy.start()
    columns = jnp.concatenate([c[...] for c in cols], axis=0)
    for copy in copies:
        copy.wait()
    total[...] = dot(rows[...].astype(F32).T.astype(BF16), columns, 1, 0)
    split_core(total, keep_ref, away_ref)


def z_split_kernel(keep_ref, came_ref, near_ref, far_ref):
    half = place("z") // 4
    for xh in range(2):
        for xl in range(2):
            for ref, which in ((near_ref, half), (far_ref, 1 - half)):
                at = pl.ds(pl.multiple_of(xl * 144 + which * 72, 8), 72)
                both = keep_ref[xh, at, :].astype(F32) + came_ref[xh, at, :].astype(F32)
                ref[xh * 2 + xl] = both.astype(BF16)


def z_halve_kernel(keep_ref, came_ref, near_ref, far_ref):
    first = near_ref.shape[1] == 36
    high = lax.rem(place("z") // (1 if first else 2), 2) == 1
    for b in range(4):
        both = keep_ref[b].astype(F32) + came_ref[b].astype(F32)
        if first:
            upper = jnp.concatenate([both[18:36], both[54:]], axis=0)
            lower = jnp.concatenate([both[:18], both[36:54]], axis=0)
        else:
            upper, lower = both[18:], both[:18]
        near_ref[b] = jnp.where(high, upper, lower).astype(BF16)
        far_ref[b] = jnp.where(high, lower, upper).astype(BF16)


def xl_kernel(keep_ref, came_ref, near_ref, far_ref):
    xl = place("xl")
    for xh in range(2):
        for ref, which in ((near_ref, xl), (far_ref, 1 - xl)):
            at = xh * 2 + which
            ref[xh] = (keep_ref[at].astype(F32) + came_ref[at].astype(F32)).astype(BF16)


def pair_kernel(keep_ref, came_ref, near_ref, far_ref):
    xh = place("xh")
    for ref, which in ((near_ref, xh), (far_ref, 1 - xh)):
        ref[...] = (keep_ref[which].astype(F32) + came_ref[which].astype(F32)).astype(BF16)


def slot_kernel(keep_ref, came_ref, *outs):
    total = keep_ref[...].astype(F32) + came_ref[...].astype(F32)
    wide = jnp.concatenate([total, jnp.zeros((18, 128), F32)], axis=1)
    wide = jnp.concatenate([wide, jnp.zeros((6, WIDE + 128), F32)], axis=0)
    d = place("dp")
    for o in range(CLIPS):
        g = lax.rem(d + o, CLIPS)
        turned = pltpu.roll(wide, lax.rem(WIDE + 128 - 3 * HD * g, WIDE + 128), 1)
        outs[o][...] = turned[:, :256]


def order_kernel(*refs):
    slots, out_ref = refs[:CLIPS], refs[CLIPS]
    d = place("dp")
    for o in range(CLIPS):
        out_ref[lax.rem(d + CLIPS - o, CLIPS)] = slots[o][:18, : 3 * HD]


def pack_kernel(d_ref, near_ref, far_ref, out_ref, total):
    total[...] = near_ref[...].astype(F32) + far_ref[...].astype(F32)
    rest = jnp.zeros((RIDE - 54, 128), F32)
    for b in range(HEADS):
        at = slice(b * 18, (b + 1) * 18)
        parts = [total[at, i * 128 : (i + 1) * 128] for i in range(3)]
        block = [*parts, rest, d_ref[b].astype(F32)]
        out_ref[b] = jnp.concatenate(block, axis=0).astype(BF16)


def pad_rows(x, rows):
    return jnp.concatenate([x, jnp.zeros((rows - x.shape[0], x.shape[1]), x.dtype)], axis=0)


def probs_kernel(qkv_ref, p_ref, o_ref, k_ref, qt_ref, vt_ref, q_rows, kt, v_rows):
    @pl.when(pl.program_id(0) == 0)
    def _():
        for b in range(HEADS):
            at = slice(b * ROWS, (b + 1) * ROWS)
            block = qkv_ref[b].astype(F32)
            q, k, v = (pad_rows(block[p * HD : (p + 1) * HD], 128) for p in range(3))
            q_rows[at, :] = q.T.astype(BF16)
            k_ref[at, :] = k.T.astype(BF16)
            v_rows[at, :] = v.T.astype(BF16)
            kt[:, at] = k.astype(BF16)
            vt_ref[:, at] = v.astype(BF16)
            qt_ref[:, at] = q[:80].astype(BF16)

    factor = SCALE * math.log2(math.e)
    lane = lax.broadcasted_iota(jnp.int32, (PART, 128), 1)
    for i in range(BLOCK // PART):
        to = slice(i * PART, (i + 1) * PART)
        at = pl.multiple_of(pl.program_id(0) * BLOCK + i * PART, PART)
        scores = dot(q_rows[pl.ds(at, PART), :], kt[...], 1, 0)
        top = jnp.max(scores, axis=-1, keepdims=True)
        e = jnp.exp2((scores - top) * factor)
        low = e.astype(BF16)
        p_ref[to, :] = low
        part = 1.0 / jnp.sum(e, axis=-1, keepdims=True)
        mixed = dot(low, v_rows[...], 1, 0) * part
        o_ref[to, :] = jnp.where(lane == 127, part, mixed)


def prepare_kernel(do_ref, rows_ref):
    for b in range(HEADS):
        at = slice(b * ROWS, (b + 1) * ROWS)
        block = pad_rows(do_ref[b].astype(F32), 128)
        rows_ref[at, :] = block.T.astype(BF16)


def spatial_kernel(
    do_ref, p_ref, o_ref, k_ref, qt_ref, vt_ref, out_ref, dq, dk, dv
):
    step = pl.program_id(0)

    @pl.when(step == 0)
    def _():
        dk[...] = jnp.zeros_like(dk)
        dv[...] = jnp.zeros_like(dv)

    at = pl.ds(pl.multiple_of(step * STEP, STEP), STEP)
    mixed = o_ref[...]
    wide = do_ref[...].astype(F32) * mixed[:, 127:]
    do = wide.astype(BF16)
    probs = p_ref[...]
    dp = dot(do, vt_ref[...], 1, 0)
    mid = jnp.sum(wide * mixed, axis=-1, keepdims=True)
    ds = (probs.astype(F32) * (dp - mid)).astype(BF16)
    dq[:, at] = (dot(ds, k_ref[...], 1, 0) * SCALE).T[:HD]
    dk[...] += dot(qt_ref[...], ds, 1, 0)
    dv[...] += dot(wide.T[:80].astype(BF16), probs, 1, 0)

    @pl.when(step == pl.num_programs(0) - 1)
    def _():
        for b in range(HEADS):
            at = slice(b * ROWS, (b + 1) * ROWS)
            parts = [dq[:, at], dk[:HD, at] * SCALE, dv[:HD, at]]
            out_ref[b] = jnp.concatenate(parts, axis=0).astype(BF16)


def home_kernel(in_ref, out_ref, proj_ref, work, pack):
    for h in range(HEADS):
        block = in_ref[h].astype(F32)
        extra = block[:RIDE]
        pack[...] = extra if h == 0 else pack[...] + extra
        for p in range(3):
            at = (p * HEADS + h) * HD
            work[at : at + HD, :] = block[RIDE + p * HD : RIDE + (p + 1) * HD]
    for t in range(3 * D // 128):
        at = slice(t * 128, (t + 1) * 128)
        out_ref[:, at] = work[at, :].T.astype(BF16)
    for i, wide in enumerate((128, 128, 32)):
        proj_ref[:, i * 128 : i * 128 + wide] = pack[i * 18 : (i + 1) * 18, :wide]


def around(x, axis, size, step):
    return lax.ppermute(x, axis, [(i, (i + step) % size) for i in range(size)])


def across(x, axis, size, flip):
    return lax.ppermute(x, axis, [(i, i ^ flip) for i in range(size)])


def per_device(spatial_qkv, spatial_out, resid, norm_gain, qkv_weight, out_weight, grad_out):
    every = ("dp", "xh", "core")
    heads = ("xl", "z")
    frame = ("xh", "core")
    line = ("xh", "xl")
    shape = jax.ShapeDtypeStruct
    resid = resid.reshape(ROWS, D)
    grad_out = grad_out.reshape(ROWS, D)
    qkv_rows = spatial_qkv.reshape(ROWS, 3 * D)
    out_rows = spatial_out.reshape(ROWS, D)
    gain = norm_gain.reshape(1, D)
    rows = CLIPS * ROWS
    width = 3 * GROUP * HD

    hbm = pl.BlockSpec(memory_space=pltpu.HBM)
    vmem_spec = pl.BlockSpec(memory_space=pltpu.VMEM)
    bf16 = lambda *dims: shape(dims, BF16)
    f32 = lambda *dims: pltpu.VMEM(dims, F32)
    near_by = lambda blocks: [
        b if o == 0 else around(b, "dp", CLIPS, o) for o, b in enumerate(blocks)
    ]
    over_frame = lambda blocks: [
        b if k == 0 else across(b, frame, FRAMES, k) for k, b in enumerate(blocks)
    ]

    mine, t_unit = call(
        unit_kernel,
        [bf16(CHUNK, 2 * D)] * FRAMES,
        (resid, gain, grad_out),
        LOW,
        scratch=[f32(ROWS, 2 * D)],
    )
    ours = over_frame(mine)
    (qkv_out,), t_qkv = call(
        qkv_kernel,
        [bf16(HEADS, 3 * HD, ROWS)],
        (qkv_rows,),
        LOW,
        scratch=[f32(3 * D, ROWS)],
        after=[t_unit],
    )
    qkv_in = lax.all_to_all(qkv_out, heads, 0, 0, tiled=True)
    w_blocks, t_weight = call(
        weight_kernel,
        [bf16(3 * HD, HALF)] * CLIPS,
        (qkv_weight.T,),
        LOW,
        scratch=[f32(width, D)],
        after=[t_qkv],
    )
    w_in = near_by(w_blocks)
    groups, t_group = call(
        group_kernel,
        [bf16(ROWS, D + GO_PAD)] * CLIPS,
        tuple(ours),
        LOW,
        scratch=[f32(D, ROWS)],
        after=[t_weight],
    )
    rows_in = near_by(groups)
    (w_half,), t_join = call(
        join_kernel,
        [bf16(width, HALF)],
        tuple(w_in),
        LOW,
        scratch=[f32(width, HALF)],
        after=[t_group],
    )
    w_other = across(w_half, "core", 2, 1)
    (up_out, unit_all, d_proj), t_temporal = call(
        temporal_kernel,
        [bf16(CLIPS, FRAMES, CHUNK, D), bf16(rows, D), bf16(rows, WIDE)],
        (*rows_in, w_half, w_other),
        EARLY,
        scratch=[
            f32(width, rows),
            f32(GROUP * HD, rows),
            f32(width, rows),
            pltpu.VMEM((width, D), BF16),
        ],
    )
    up_out, qkv_in = lax.optimization_barrier((up_out, qkv_in))
    up_in = lax.all_to_all(
        up_out.reshape(16, CHUNK, D), every, 0, 0, tiled=True
    ).reshape(CLIPS, FRAMES, CHUNK, D)
    out_rows = lax.optimization_barrier((out_rows, *rows_in))[0]
    out_in = near_by([out_rows] * CLIPS)

    (keep, away), t_grad = call(
        qkv_grad_kernel,
        [bf16(2, 288, WIDE)] * 2,
        (unit_all, d_proj),
        LOW,
        scratch=[f32(D, WIDE)],
        after=[t_temporal],
    )
    came = across(away, "core", 2, 1)
    (near, far), t_split = call(
        z_split_kernel, [bf16(4, 72, WIDE)] * 2, (keep, came), LOW, after=[t_grad]
    )
    came = across(far, "z", 8, 4)

    whole = lambda *dims: pl.BlockSpec(dims, lambda i: (0,) * len(dims))
    by_row = lambda wide: pl.BlockSpec((BLOCK, wide), lambda i: (i, 0))
    (probs, mixed, keys, queries_t, values_t), t_probs = call(
        probs_kernel,
        [
            bf16(TOKENS, TOKENS),
            shape((TOKENS, 128), F32),
            bf16(TOKENS, 128),
            bf16(80, TOKENS),
            bf16(128, TOKENS),
        ],
        (qkv_in,),
        LOW,
        vmem=53,
        scratch=[
            pltpu.VMEM((TOKENS, 128), BF16),
            pltpu.VMEM((128, TOKENS), BF16),
            pltpu.VMEM((TOKENS, 128), BF16),
        ],
        grid=(TOKENS // BLOCK,),
        in_specs=[whole(HEADS, 3 * HD, ROWS)],
        out_specs=[
            by_row(TOKENS),
            by_row(128),
            whole(TOKENS, 128),
            whole(80, TOKENS),
            whole(128, TOKENS),
        ],
    )
    (stream, head_out), t_stream = call(
        stream_kernel,
        [bf16(ROWS, D), bf16(HEADS, HD, ROWS)],
        (up_in, resid, gain, out_weight),
        LOW,
        after=[t_probs],
        scratch=[pltpu.VMEM((D, D), BF16), pltpu.SemaphoreType.DMA],
        in_specs=[vmem_spec, vmem_spec, vmem_spec, hbm],
    )
    head_in = lax.all_to_all(head_out, heads, 0, 0, tiled=True)
    cols, t_cols = call(cols_kernel, [bf16(ROWS, GO_PAD)] * CLIPS, (stream,), LOW)
    cols = near_by(cols)
    (near, far), t_halve = call(
        z_halve_kernel, [bf16(4, 36, WIDE)] * 2, (near, came), LOW, after=[t_cols]
    )
    came = across(far, "z", 8, 1)
    (p_keep, p_away), t_proj = call(
        proj_grad_kernel,
        [bf16(2, 288, GO_PAD)] * 2,
        (*out_in, *cols),
        LOW,
        scratch=[
            f32(D, GO_PAD),
            pltpu.VMEM((rows, D), BF16),
            pltpu.SemaphoreType.DMA((CLIPS,)),
        ],
        after=[t_halve],
        in_specs=[hbm] * CLIPS + [vmem_spec] * CLIPS,
    )
    p_came = across(p_away, "core", 2, 1)

    (do_rows,), t_prepare = call(
        prepare_kernel,
        [bf16(TOKENS, 128)],
        (head_in,),
        LOW,
        after=[t_proj],
    )
    (p_near, p_far), t_pair = call(
        pair_kernel, [bf16(288, GO_PAD)] * 2, (p_keep, p_came), LOW, after=[t_prepare]
    )
    p_came = across(p_far, "xh", 2, 1)

    by_step = lambda wide: pl.BlockSpec((STEP, wide), lambda i: (i, 0))
    (d_out,), t_spatial = call(
        spatial_kernel,
        [bf16(HEADS, 3 * HD, ROWS)],
        (do_rows, probs, mixed, keys, queries_t, values_t),
        LOW,
        vmem=53,
        scratch=[
            f32(HD, TOKENS),
            f32(80, TOKENS),
            f32(80, TOKENS),
        ],
        grid=(TOKENS // STEP,),
        in_specs=[
            by_step(128),
            by_step(TOKENS),
            by_step(128),
            whole(TOKENS, 128),
            pl.BlockSpec((80, STEP), lambda i: (0, i)),
            whole(128, TOKENS),
        ],
        out_specs=[whole(HEADS, 3 * HD, ROWS)],
    )
    (near, far), t_halve = call(
        z_halve_kernel, [bf16(4, 18, WIDE)] * 2, (near, came), LOW, after=[t_spatial]
    )
    came = across(far, "z", 8, 2)

    (d_out,), t_pack = call(
        pack_kernel,
        [bf16(HEADS, RIDE + 3 * HD, ROWS)],
        (d_out, p_near, p_came),
        LOW,
        scratch=[f32(288, GO_PAD)],
        after=[t_halve],
    )
    d_in = lax.all_to_all(d_out, heads, 0, 0, tiled=True)

    (near, far), t_line = call(
        xl_kernel, [bf16(2, 18, WIDE)] * 2, (near, came), LOW, after=[t_pack]
    )
    came = across(far, "xl", 2, 1)
    (near, far), t_far = call(
        pair_kernel, [bf16(18, WIDE)] * 2, (near, came), LOW, after=[t_line]
    )
    came = across(far, "xh", 2, 1)
    slots, t_slot = call(slot_kernel, [shape((24, 256), F32)] * CLIPS, (near, came), TAIL)
    slots = near_by(slots)
    (ordered,), t_order = call(
        order_kernel, [shape((CLIPS, 18, 3 * HD), F32)], tuple(slots), LOW
    )
    grad_qkv = (
        ordered.reshape(CLIPS, 18, 3, HD).transpose(1, 2, 0, 3).reshape(18, 3 * D // CLIPS)
    )
    (d_qkv, grad_proj), _ = call(
        home_kernel,
        [bf16(ROWS, 3 * D), shape((18, D // CLIPS), F32)],
        (d_in,),
        LOW,
        scratch=[f32(3 * D, ROWS), f32(RIDE, 128)],
    )
    return (
        d_qkv.reshape(1, 1, ROWS, 3 * D),
        stream.reshape(1, 1, ROWS, D),
        grad_qkv,
        grad_proj,
    )


def solution(mesh):
    fine = Mesh(mesh.devices.reshape(4, 2, 2, 2, 8), ("dp", "xh", "core", "xl", "z"))
    frame = ("xh", "core")
    head = ("xl", "z")
    rows = P("dp", frame, head, None)
    return jax.shard_map(
        per_device,
        mesh=fine,
        in_specs=(rows, rows, rows, P(), P(None, "dp"), P(), rows),
        out_specs=(rows, rows, P(frame + head, "dp"), P(frame + head, "dp")),
        check_vma=False,
    )
```

```python
import functools
import math

import jax
import jax.numpy as jnp
from jax import lax
from jax.experimental import pallas as pl
from jax.experimental.pallas import tpu as pltpu
from jax.sharding import Mesh, PartitionSpec as P

D = 1152
HEADS = 16
HD = 72
ROWS = 128
CLIPS = 4
FRAMES = 4
CHUNK = 32
GROUP = 4
GO_PAD = 384
WIDE = 896
HALF = 640
TOKENS = 2048
BLOCK = 512
PART = 256
STEP = 512
EPS = 1e-06
LOW = 0.001
EARLY = 0.001
TAIL = 18
RIDE = 56
SCALE = HD ** (-0.5)
F32 = jnp.float32
BF16 = jnp.bfloat16
MIB = 1 << 20


def dot(left, right, left_dim, right_dim):
    return lax.dot_general(
        left, right, (((left_dim,), (right_dim,)), ((), ())), preferred_element_type=F32
    )


def call(kernel, out_shape, args, us, scratch=(), vmem=40, after=(), hold=(), in_specs=None, out_specs=None, **kw):
    held, extra, made = len(args), len(after) + len(hold), len(out_shape)
    vmem_spec, any_spec, hbm_spec = (
        pl.BlockSpec(memory_space=m) for m in (pltpu.VMEM, pl.ANY, pltpu.HBM)
    )
    token = jax.ShapeDtypeStruct((8, 128), F32)

    def body(*refs):
        ins, rest = refs[:held], refs[held + extra :]
        kernel(*ins, *rest[:made], *rest[made + 1 :])

    *outs, done = pl.pallas_call(
        body,
        out_shape=[*out_shape, token],
        in_specs=[*(in_specs or [vmem_spec] * held), *[any_spec] * len(after), *[hbm_spec] * len(hold)],
        out_specs=[*(out_specs or [vmem_spec] * made), any_spec],
        scratch_shapes=list(scratch),
        cost_estimate=pl.CostEstimate(
            flops=int(us * 1.1e9), bytes_accessed=int(us * 1e6), transcendentals=0
        ),
        compiler_params=pltpu.CompilerParams(vmem_limit_bytes=vmem * MIB),
        **kw,
    )(*args, *after, *hold)
    return outs, done


def norm_rows(rows):
    centred = rows - jnp.mean(rows, axis=-1, keepdims=True)
    spread = jnp.mean(centred * centred, axis=-1, keepdims=True)
    inverse = lax.rsqrt(spread + EPS)
    return centred * inverse, inverse


def place(name):
    return lax.axis_index(name)


def frame_index():
    return place("xh") * 2 + place("core")


def x_index():
    return place("xh") * 2 + place("xl")


def unit_kernel(resid_ref, gain_ref, grad_ref, *outs):
    normed, _ = norm_rows(resid_ref[...].astype(F32))
    work = outs[-1]
    work[:, :D] = normed * gain_ref[...]
    work[:, D:] = grad_ref[...].astype(F32)
    f = frame_index()
    for k in range(FRAMES):
        at = pl.multiple_of((f ^ k) * CHUNK, CHUNK)
        outs[k][...] = work[pl.ds(at, CHUNK), :].astype(BF16)


def group_kernel(*refs):
    ins, outs, work = refs[:FRAMES], refs[FRAMES : FRAMES + CLIPS], refs[-1]
    for k in range(FRAMES):
        at = slice(k * CHUNK, (k + 1) * CHUNK)
        for o in range(CLIPS):
            outs[o][at, :D] = ins[k][:, :D]
    grad = jnp.concatenate([ins[k][:, D:] for k in range(FRAMES)], axis=0).astype(F32)
    for t in range(D // 128):
        at = slice(t * 128, (t + 1) * 128)
        work[at, :] = grad[:, at].T
    d = place("dp")
    gap = jnp.zeros((GO_PAD - GROUP * HD, ROWS), F32)
    for o in range(CLIPS):
        g = lax.rem(d + o, CLIPS)
        heads = [
            work[pl.ds(pl.multiple_of((4 * i + g) * HD, 8), HD), :] for i in range(GROUP)
        ]
        outs[o][:, D:] = jnp.concatenate([*heads, gap], axis=0).T.astype(BF16)


def weight_kernel(w_ref, *refs):
    outs, work = refs[:CLIPS], refs[-1]
    work[...] = w_ref[...].astype(F32)
    d = place("dp")
    lanes = pl.ds(pl.multiple_of(place("core") * (D - HALF), 128), HALF)
    for o in range(CLIPS):
        g = lax.rem(d + o, CLIPS)
        heads = [work[pl.ds(pl.multiple_of((4 * j + g) * HD, 8), HD), lanes] for j in range(3)]
        outs[o][...] = jnp.concatenate(heads, axis=0).astype(BF16)


def join_kernel(*refs):
    ins, out_ref, work = refs[:CLIPS], refs[CLIPS], refs[-1]
    d = place("dp")
    for o in range(CLIPS):
        s = lax.rem(d + CLIPS - o, CLIPS)
        work[pl.ds(pl.multiple_of(s * 3 * HD, 8), 3 * HD), :] = ins[o][...].astype(F32)
    out_ref[...] = work[...].astype(BF16)


def qkv_kernel(qkv_ref, out_ref, work):
    for t in range(3 * D // 128):
        work[t * 128 : (t + 1) * 128, :] = qkv_ref[:, t * 128 : (t + 1) * 128].astype(F32).T
    for h in range(HEADS):
        parts = [work[(p * HEADS + h) * HD : (p * HEADS + h + 1) * HD, :] for p in range(3)]
        out_ref[h] = jnp.concatenate(parts, axis=0).astype(BF16)


def temporal_kernel(*refs):
    rows_in, halves = refs[:CLIPS], refs[CLIPS : CLIPS + 2]
    up_ref, all_ref, dproj_ref, proj, grad, dproj, w_ref = refs[CLIPS + 2 :]
    d, frame = place("dp"), frame_index()
    for core in range(2):

        @pl.when(place("core") == core)
        def _():
            w_ref[:, :HALF] = halves[core][...]
            w_ref[:, D - HALF :] = halves[1 - core][...]

    for k in range(FRAMES):
        at = slice(k * CHUNK, (k + 1) * CHUNK)
        for o in range(CLIPS):
            to = (k * CLIPS + o) * CHUNK
            all_ref[to : to + CHUNK, :] = rows_in[o][at, :D]
        rows = jnp.concatenate([rows_in[o][at, D:] for o in range(CLIPS)], axis=0).astype(F32)
        grad[:, k * ROWS : (k + 1) * ROWS] = rows.T[: GROUP * HD]
    proj[...] = dot(w_ref[...], all_ref[...], 1, 1).astype(BF16).astype(F32)

    def one_head(n, carry):
        def load(ref, base):
            at = pl.ds(pl.multiple_of(base + n * HD, 8), HD)
            return [ref[at, f * ROWS : (f + 1) * ROWS] for f in range(FRAMES)]

        q, k, v = (load(proj, p * GROUP * HD) for p in range(3))
        g = load(grad, 0)

        def total(a, b):
            return jnp.sum(a * b, axis=0, keepdims=True)

        span = range(FRAMES)
        ds, p_low = [], []
        for f in span:
            s = [total(q[f], k[j]) * SCALE for j in span]
            top = functools.reduce(jnp.maximum, s)
            e = [jnp.exp(x - top) for x in s]
            below = functools.reduce(jnp.add, e)
            prob = [x / below for x in e]
            dp = [total(g[f], v[j]) for j in span]
            mid = functools.reduce(jnp.add, [x * y for x, y in zip(prob, dp)])
            ds.append([(x * (y - mid)).astype(BF16).astype(F32) for x, y in zip(prob, dp)])
            p_low.append([x.astype(BF16).astype(F32) for x in prob])

        def put(base, f, value):
            at = pl.ds(pl.multiple_of(base + n * HD, 8), HD)
            dproj[at, f * ROWS : (f + 1) * ROWS] = value

        def mix(weights, values):
            return functools.reduce(jnp.add, [w * x for w, x in zip(weights, values)])

        for f in span:
            put(0, f, mix(ds[f], k) * SCALE)
            put(GROUP * HD, f, mix([ds[j][f] for j in span], q) * SCALE)
            put(2 * GROUP * HD, f, mix([p_low[j][f] for j in span], g))
        return carry

    lax.fori_loop(0, GROUP, one_head, 0)
    width = 3 * GROUP * HD
    gap = jnp.zeros((WIDE - width, CLIPS * ROWS), F32)
    low = jnp.concatenate([dproj[...], gap], axis=0).T.astype(BF16)
    dproj_ref[...] = low
    up = dot(low[:, :width], w_ref[...], 1, 0).astype(BF16)
    for k in range(FRAMES):
        for o in range(CLIPS):
            at = (k * CLIPS + o) * CHUNK
            up_ref[lax.rem(d + CLIPS - o, CLIPS), frame ^ k] = up[at : at + CHUNK]


def stream_kernel(up_ref, resid_ref, gain_ref, w_hbm, stream_ref, head_ref, w_ref, sem):
    copy = pltpu.make_async_copy(w_hbm, w_ref, sem)
    copy.start()
    parts = []
    for f in range(FRAMES):
        parts.append(functools.reduce(jnp.add, [up_ref[g, f].astype(F32) for g in range(CLIPS)]))
    up = jnp.concatenate(parts, axis=0)
    normed, inverse = norm_rows(resid_ref[...].astype(F32))
    scaled = up * gain_ref[...]
    mean_up = jnp.mean(scaled, axis=-1, keepdims=True)
    mean_cross = jnp.mean(scaled * normed, axis=-1, keepdims=True)
    stream = (inverse * (scaled - mean_up - normed * mean_cross)).astype(BF16)
    stream_ref[...] = stream
    copy.wait()
    spatial = dot(w_ref[...], stream, 1, 1)
    for h in range(HEADS):
        head_ref[h] = spatial[h * HD : (h + 1) * HD].astype(BF16)


def cols_kernel(stream_ref, *cols):
    wide = stream_ref[...].astype(F32)
    d = place("dp")
    for o in range(CLIPS):
        g = lax.rem(d + o, CLIPS)
        turned = pltpu.roll(wide, lax.rem(D - (D // CLIPS) * g, D), 1)
        cols[o][...] = turned[:, :GO_PAD].astype(BF16)


def split_core(total, keep_ref, away_ref):
    core = place("core")
    for xh in range(2):
        for ref, which in ((keep_ref, core), (away_ref, 1 - core)):
            at = pl.multiple_of((xh * 2 + which) * 288, 8)
            ref[xh] = total[pl.ds(at, 288), :].astype(BF16)


def qkv_grad_kernel(unit_ref, dproj_ref, keep_ref, away_ref, total):
    total[...] = dot(unit_ref[...].astype(F32).T.astype(BF16), dproj_ref[...], 1, 0)
    split_core(total, keep_ref, away_ref)


def proj_grad_kernel(*refs):
    outs, cols, (keep_ref, away_ref, total, rows, sems) = refs[:CLIPS], refs[CLIPS : 2 * CLIPS], refs[-5:]
    copies = [
        pltpu.make_async_copy(ref, rows.at[pl.ds(o * ROWS, ROWS)], sems.at[o])
        for o, ref in enumerate(outs)
    ]
    for copy in copies:
        copy.start()
    columns = jnp.concatenate([c[...] for c in cols], axis=0)
    for copy in copies:
        copy.wait()
    total[...] = dot(rows[...].astype(F32).T.astype(BF16), columns, 1, 0)
    split_core(total, keep_ref, away_ref)


def z_split_kernel(keep_ref, came_ref, near_ref, far_ref, total):
    half = place("z") // 4
    for xh in range(2):
        total[...] = keep_ref[xh].astype(F32) + came_ref[xh].astype(F32)
        for xl in range(2):
            for ref, which in ((near_ref, half), (far_ref, 1 - half)):
                at = pl.ds(pl.multiple_of(xl * 144 + which * 72, 8), 72)
                ref[xh * 2 + xl] = total[at, :].astype(BF16)


def z_halve_kernel(keep_ref, came_ref, near_ref, far_ref):
    first = near_ref.shape[1] == 36
    high = lax.rem(place("z") // (1 if first else 2), 2) == 1
    for b in range(4):
        both = keep_ref[b].astype(F32) + came_ref[b].astype(F32)
        if first:
            upper = jnp.concatenate([both[18:36], both[54:]], axis=0)
            lower = jnp.concatenate([both[:18], both[36:54]], axis=0)
        else:
            upper, lower = both[18:], both[:18]
        near_ref[b] = jnp.where(high, upper, lower).astype(BF16)
        far_ref[b] = jnp.where(high, lower, upper).astype(BF16)


def xl_kernel(keep_ref, came_ref, near_ref, far_ref):
    xl = place("xl")
    for xh in range(2):
        for ref, which in ((near_ref, xl), (far_ref, 1 - xl)):
            at = xh * 2 + which
            ref[xh] = (keep_ref[at].astype(F32) + came_ref[at].astype(F32)).astype(BF16)


def pair_kernel(keep_ref, came_ref, near_ref, far_ref):
    xh = place("xh")
    for ref, which in ((near_ref, xh), (far_ref, 1 - xh)):
        ref[...] = (keep_ref[which].astype(F32) + came_ref[which].astype(F32)).astype(BF16)


def slot_kernel(keep_ref, came_ref, *outs):
    total = keep_ref[...].astype(F32) + came_ref[...].astype(F32)
    wide = jnp.concatenate([total, jnp.zeros((18, 128), F32)], axis=1)
    wide = jnp.concatenate([wide, jnp.zeros((6, WIDE + 128), F32)], axis=0)
    d = place("dp")
    for o in range(CLIPS):
        g = lax.rem(d + o, CLIPS)
        turned = pltpu.roll(wide, lax.rem(WIDE + 128 - 3 * HD * g, WIDE + 128), 1)
        outs[o][...] = turned[:, :256]


def order_kernel(*refs):
    slots, out_ref = refs[:CLIPS], refs[CLIPS]
    d = place("dp")
    for o in range(CLIPS):
        out_ref[lax.rem(d + CLIPS - o, CLIPS)] = slots[o][:18, : 3 * HD]


def pack_kernel(d_ref, near_ref, far_ref, out_ref, total):
    total[...] = near_ref[...].astype(F32) + far_ref[...].astype(F32)
    rest = jnp.zeros((RIDE - 54, 128), F32)
    for b in range(HEADS):
        at = slice(b * 18, (b + 1) * 18)
        parts = [total[at, i * 128 : (i + 1) * 128] for i in range(3)]
        block = [*parts, rest, d_ref[b].astype(F32)]
        out_ref[b] = jnp.concatenate(block, axis=0).astype(BF16)


def pad_rows(x, rows):
    return jnp.concatenate([x, jnp.zeros((rows - x.shape[0], x.shape[1]), x.dtype)], axis=0)


def probs_kernel(qkv_ref, p_ref, o_ref, k_ref, qt_ref, vt_ref, q_rows, kt, v_rows):
    @pl.when(pl.program_id(0) == 0)
    def _():
        for b in range(HEADS):
            at = slice(b * ROWS, (b + 1) * ROWS)
            block = qkv_ref[b].astype(F32)
            q, k, v = (pad_rows(block[p * HD : (p + 1) * HD], 128) for p in range(3))
            q_rows[at, :] = q.T.astype(BF16)
            k_ref[at, :] = k.T.astype(BF16)
            v_rows[at, :] = v.T.astype(BF16)
            kt[:, at] = k.astype(BF16)
            vt_ref[:, at] = v.astype(BF16)
            qt_ref[:, at] = q[:80].astype(BF16)

    factor = SCALE * math.log2(math.e)
    lane = lax.broadcasted_iota(jnp.int32, (PART, 128), 1)
    for i in range(BLOCK // PART):
        to = slice(i * PART, (i + 1) * PART)
        at = pl.multiple_of(pl.program_id(0) * BLOCK + i * PART, PART)
        scores = dot(q_rows[pl.ds(at, PART), :], kt[...], 1, 0)
        top = jnp.max(scores, axis=-1, keepdims=True)
        e = jnp.exp2((scores - top) * factor)
        low = e.astype(BF16)
        p_ref[to, :] = low
        part = 1.0 / jnp.sum(e, axis=-1, keepdims=True)
        mixed = dot(low, v_rows[...], 1, 0) * part
        o_ref[to, :] = jnp.where(lane == 127, part, mixed)


def prepare_kernel(do_ref, rows_ref):
    for b in range(HEADS):
        at = slice(b * ROWS, (b + 1) * ROWS)
        block = pad_rows(do_ref[b].astype(F32), 128)
        rows_ref[at, :] = block.T.astype(BF16)


def spatial_kernel(
    do_ref, p_ref, o_ref, k_ref, qt_ref, vt_ref, out_ref, dq, dk, dv
):
    step = pl.program_id(0)

    @pl.when(step == 0)
    def _():
        dk[...] = jnp.zeros_like(dk)
        dv[...] = jnp.zeros_like(dv)

    at = pl.ds(pl.multiple_of(step * STEP, STEP), STEP)
    mixed = o_ref[...]
    wide = do_ref[...].astype(F32) * mixed[:, 127:]
    do = wide.astype(BF16)
    probs = p_ref[...]
    dp = dot(do, vt_ref[...], 1, 0)
    mid = jnp.sum(wide * mixed, axis=-1, keepdims=True)
    ds = (probs.astype(F32) * (dp - mid)).astype(BF16)
    dq[:, at] = (dot(ds, k_ref[...], 1, 0) * SCALE).T[:HD]
    dk[...] += dot(qt_ref[...], ds, 1, 0)
    dv[...] += dot(wide.T[:80].astype(BF16), probs, 1, 0)

    @pl.when(step == pl.num_programs(0) - 1)
    def _():
        for b in range(HEADS):
            at = slice(b * ROWS, (b + 1) * ROWS)
            parts = [dq[:, at], dk[:HD, at] * SCALE, dv[:HD, at]]
            out_ref[b] = jnp.concatenate(parts, axis=0).astype(BF16)


def home_kernel(in_ref, out_ref, proj_ref, work, pack):
    for h in range(HEADS):
        block = in_ref[h].astype(F32)
        extra = block[:RIDE]
        pack[...] = extra if h == 0 else pack[...] + extra
        for p in range(3):
            at = (p * HEADS + h) * HD
            work[at : at + HD, :] = block[RIDE + p * HD : RIDE + (p + 1) * HD]
    for t in range(3 * D // 128):
        at = slice(t * 128, (t + 1) * 128)
        out_ref[:, at] = work[at, :].T.astype(BF16)
    for i, wide in enumerate((128, 128, 32)):
        proj_ref[:, i * 128 : i * 128 + wide] = pack[i * 18 : (i + 1) * 18, :wide]


def around(x, axis, size, step):
    return lax.ppermute(x, axis, [(i, (i + step) % size) for i in range(size)])


def across(x, axis, size, flip):
    return lax.ppermute(x, axis, [(i, i ^ flip) for i in range(size)])


def per_device(spatial_qkv, spatial_out, resid, norm_gain, qkv_weight, out_weight, grad_out):
    every = ("dp", "xh", "core")
    heads = ("xl", "z")
    frame = ("xh", "core")
    line = ("xh", "xl")
    shape = jax.ShapeDtypeStruct
    resid = resid.reshape(ROWS, D)
    grad_out = grad_out.reshape(ROWS, D)
    qkv_rows = spatial_qkv.reshape(ROWS, 3 * D)
    out_rows = spatial_out.reshape(ROWS, D)
    gain = norm_gain.reshape(1, D)
    rows = CLIPS * ROWS
    width = 3 * GROUP * HD

    hbm = pl.BlockSpec(memory_space=pltpu.HBM)
    vmem_spec = pl.BlockSpec(memory_space=pltpu.VMEM)
    bf16 = lambda *dims: shape(dims, BF16)
    f32 = lambda *dims: pltpu.VMEM(dims, F32)
    near_by = lambda blocks: [
        b if o == 0 else around(b, "dp", CLIPS, o) for o, b in enumerate(blocks)
    ]
    over_frame = lambda blocks: [
        b if k == 0 else across(b, frame, FRAMES, k) for k, b in enumerate(blocks)
    ]

    mine, t_unit = call(
        unit_kernel,
        [bf16(CHUNK, 2 * D)] * FRAMES,
        (resid, gain, grad_out),
        LOW,
        scratch=[f32(ROWS, 2 * D)],
    )
    ours = over_frame(mine)
    (qkv_out,), t_qkv = call(
        qkv_kernel,
        [bf16(HEADS, 3 * HD, ROWS)],
        (qkv_rows,),
        LOW,
        scratch=[f32(3 * D, ROWS)],
        after=[t_unit],
    )
    qkv_in = lax.all_to_all(qkv_out, heads, 0, 0, tiled=True)
    w_blocks, t_weight = call(
        weight_kernel,
        [bf16(3 * HD, HALF)] * CLIPS,
        (qkv_weight.T,),
        LOW,
        scratch=[f32(width, D)],
        after=[t_qkv],
    )
    w_in = near_by(w_blocks)
    groups, t_group = call(
        group_kernel,
        [bf16(ROWS, D + GO_PAD)] * CLIPS,
        tuple(ours),
        LOW,
        scratch=[f32(D, ROWS)],
        after=[t_weight],
    )
    rows_in = near_by(groups)
    (w_half,), t_join = call(
        join_kernel,
        [bf16(width, HALF)],
        tuple(w_in),
        LOW,
        scratch=[f32(width, HALF)],
        after=[t_group],
    )
    w_other = across(w_half, "core", 2, 1)
    (up_out, unit_all, d_proj), t_temporal = call(
        temporal_kernel,
        [bf16(CLIPS, FRAMES, CHUNK, D), bf16(rows, D), bf16(rows, WIDE)],
        (*rows_in, w_half, w_other),
        EARLY,
        scratch=[
            f32(width, rows),
            f32(GROUP * HD, rows),
            f32(width, rows),
            pltpu.VMEM((width, D), BF16),
        ],
    )
    up_out, qkv_in = lax.optimization_barrier((up_out, qkv_in))
    up_in = lax.all_to_all(
        up_out.reshape(16, CHUNK, D), every, 0, 0, tiled=True
    ).reshape(CLIPS, FRAMES, CHUNK, D)
    out_rows = lax.optimization_barrier((out_rows, *rows_in))[0]
    out_in = near_by([out_rows] * CLIPS)

    (keep, away), t_grad = call(
        qkv_grad_kernel,
        [bf16(2, 288, WIDE)] * 2,
        (unit_all, d_proj),
        LOW,
        scratch=[f32(D, WIDE)],
        after=[t_temporal],
    )
    came = across(away, "core", 2, 1)
    (near, far), t_split = call(
        z_split_kernel,
        [bf16(4, 72, WIDE)] * 2,
        (keep, came),
        LOW,
        scratch=[f32(288, WIDE)],
        after=[t_grad],
    )
    came = across(far, "z", 8, 4)

    whole = lambda *dims: pl.BlockSpec(dims, lambda i: (0,) * len(dims))
    by_row = lambda wide: pl.BlockSpec((BLOCK, wide), lambda i: (i, 0))
    (probs, mixed, keys, queries_t, values_t), t_probs = call(
        probs_kernel,
        [
            bf16(TOKENS, TOKENS),
            shape((TOKENS, 128), F32),
            bf16(TOKENS, 128),
            bf16(80, TOKENS),
            bf16(128, TOKENS),
        ],
        (qkv_in,),
        LOW,
        vmem=53,
        scratch=[
            pltpu.VMEM((TOKENS, 128), BF16),
            pltpu.VMEM((128, TOKENS), BF16),
            pltpu.VMEM((TOKENS, 128), BF16),
        ],
        grid=(TOKENS // BLOCK,),
        in_specs=[whole(HEADS, 3 * HD, ROWS)],
        out_specs=[
            by_row(TOKENS),
            by_row(128),
            whole(TOKENS, 128),
            whole(80, TOKENS),
            whole(128, TOKENS),
        ],
    )
    (stream, head_out), t_stream = call(
        stream_kernel,
        [bf16(ROWS, D), bf16(HEADS, HD, ROWS)],
        (up_in, resid, gain, out_weight),
        LOW,
        after=[t_probs],
        scratch=[pltpu.VMEM((D, D), BF16), pltpu.SemaphoreType.DMA],
        in_specs=[vmem_spec, vmem_spec, vmem_spec, hbm],
    )
    head_in = lax.all_to_all(head_out, heads, 0, 0, tiled=True)
    cols, t_cols = call(cols_kernel, [bf16(ROWS, GO_PAD)] * CLIPS, (stream,), LOW)
    cols = near_by(cols)
    (near, far), t_halve = call(
        z_halve_kernel, [bf16(4, 36, WIDE)] * 2, (near, came), LOW, after=[t_cols]
    )
    came = across(far, "z", 8, 1)
    (p_keep, p_away), t_proj = call(
        proj_grad_kernel,
        [bf16(2, 288, GO_PAD)] * 2,
        (*out_in, *cols),
        LOW,
        scratch=[
            f32(D, GO_PAD),
            pltpu.VMEM((rows, D), BF16),
            pltpu.SemaphoreType.DMA((CLIPS,)),
        ],
        after=[t_halve],
        in_specs=[hbm] * CLIPS + [vmem_spec] * CLIPS,
    )
    p_came = across(p_away, "core", 2, 1)

    (do_rows,), t_prepare = call(
        prepare_kernel,
        [bf16(TOKENS, 128)],
        (head_in,),
        LOW,
        after=[t_proj],
    )
    (p_near, p_far), t_pair = call(
        pair_kernel, [bf16(288, GO_PAD)] * 2, (p_keep, p_came), LOW, after=[t_prepare]
    )
    p_came = across(p_far, "xh", 2, 1)

    by_step = lambda wide: pl.BlockSpec((STEP, wide), lambda i: (i, 0))
    (d_out,), t_spatial = call(
        spatial_kernel,
        [bf16(HEADS, 3 * HD, ROWS)],
        (do_rows, probs, mixed, keys, queries_t, values_t),
        LOW,
        vmem=53,
        scratch=[
            f32(HD, TOKENS),
            f32(80, TOKENS),
            f32(80, TOKENS),
        ],
        grid=(TOKENS // STEP,),
        in_specs=[
            by_step(128),
            by_step(TOKENS),
            by_step(128),
            whole(TOKENS, 128),
            pl.BlockSpec((80, STEP), lambda i: (0, i)),
            whole(128, TOKENS),
        ],
        out_specs=[whole(HEADS, 3 * HD, ROWS)],
    )
    (near, far), t_halve = call(
        z_halve_kernel, [bf16(4, 18, WIDE)] * 2, (near, came), LOW, after=[t_spatial]
    )
    came = across(far, "z", 8, 2)

    (d_out,), t_pack = call(
        pack_kernel,
        [bf16(HEADS, RIDE + 3 * HD, ROWS)],
        (d_out, p_near, p_came),
        LOW,
        scratch=[f32(288, GO_PAD)],
        after=[t_halve],
    )
    d_in = lax.all_to_all(d_out, heads, 0, 0, tiled=True)

    (near, far), t_line = call(
        xl_kernel, [bf16(2, 18, WIDE)] * 2, (near, came), LOW, after=[t_pack]
    )
    came = across(far, "xl", 2, 1)
    (near, far), t_far = call(
        pair_kernel, [bf16(18, WIDE)] * 2, (near, came), LOW, after=[t_line]
    )
    came = across(far, "xh", 2, 1)
    slots, t_slot = call(slot_kernel, [shape((24, 256), F32)] * CLIPS, (near, came), TAIL)
    slots = near_by(slots)
    (ordered,), t_order = call(
        order_kernel, [shape((CLIPS, 18, 3 * HD), F32)], tuple(slots), LOW
    )
    grad_qkv = (
        ordered.reshape(CLIPS, 18, 3, HD).transpose(1, 2, 0, 3).reshape(18, 3 * D // CLIPS)
    )
    (d_qkv, grad_proj), _ = call(
        home_kernel,
        [bf16(ROWS, 3 * D), shape((18, D // CLIPS), F32)],
        (d_in,),
        LOW,
        scratch=[f32(3 * D, ROWS), f32(RIDE, 128)],
    )
    return (
        d_qkv.reshape(1, 1, ROWS, 3 * D),
        stream.reshape(1, 1, ROWS, D),
        grad_qkv,
        grad_proj,
    )


def solution(mesh):
    fine = Mesh(mesh.devices.reshape(4, 2, 2, 2, 8), ("dp", "xh", "core", "xl", "z"))
    frame = ("xh", "core")
    head = ("xl", "z")
    rows = P("dp", frame, head, None)
    return jax.shard_map(
        per_device,
        mesh=fine,
        in_specs=(rows, rows, rows, P(), P(None, "dp"), P(), rows),
        out_specs=(rows, rows, P(frame + head, "dp"), P(frame + head, "dp")),
        check_vma=False,
    )
```
